32 devices in a mesh: grp: 4 (over z), req: 8 (over y, x, core).
Axes of the slice: x: 2, y: 2, z: 4, core: 2. Of those that a mesh axis runs over, the one named last changes fastest.
Arguments:
- tokens: bfloat16 [4, 2048, 1024], P('grp', 'req'), may hold values from -6 to 6
- attn_gain: float32 [1024], replicated, may hold values from 0.5 to 1.5
- w_query: bfloat16 [1024, 1024], replicated, may hold values from -0.75 to 0.75
- w_key: bfloat16 [1024, 512], replicated, may hold values from -0.75 to 0.75
- w_value: bfloat16 [1024, 512], replicated, may hold values from -0.1875 to 0.1875
- w_out: bfloat16 [1024, 1024], replicated, may hold values from -0.1875 to 0.1875
- prefix_keys: bfloat16 [4, 2048, 512], P('grp', 'req'), may hold values from -1600 to 1600
- prefix_values: bfloat16 [4, 2048, 512], P('grp', 'req'), may hold values from -6 to 6
- lengths: int32 [4, 8], P('grp'), may hold values from 1 to 256, 1536 in all within a row
- assignment: int32 [4, 8], P('grp'), may hold values from 0 to 7, each once within a row
- moe_gain: float32 [1024], replicated, may hold values from 0.5 to 1.5
- expert_ids: int32 [4, 2048, 8], P('grp', 'req'), may hold values from 0 to 31, all different within a row; in each aligned block of 256 rows (0 to 255, 256 to 511, ..., all dimensions but the last counted through in order) at most 96 rows name the same one
- route_weights: float32 [4, 2048, 8], P('grp', 'req'), may hold values from 0.1 to 0.4
- w_gate: bfloat16 [32, 1024, 512], P('req'), may hold values from -0.1875 to 0.1875
- w_up: bfloat16 [32, 1024, 512], P('req'), may hold values from -0.1875 to 0.1875
- w_down: bfloat16 [32, 512, 1024], P('req'), may hold values from -0.25 to 0.25
Outputs:
- context: bfloat16 [4, 2048, 1024], P('grp', 'req')
- hidden: bfloat16 [4, 2048, 1024], P('grp', 'req')
- expert_mix: bfloat16 [4, 2048, 1024], P('grp', 'req')
The draws below stay inside these ranges and needn't reach their ends.
Inputs may be any that keep to these rules, and one draw needn't show every extreme that they name: `lengths`: each row sums to 1536, and some request of each row has exactly 256. `assignment`: each row names every request once. `expert_ids`: each token slot names 8 different experts; within the rows of one req index no expert is named more than 96 times, a bound that some block reaches.
All inputs are finite; a program needn't handle non-finite values.
Results may differ from the reference program's by a relative error of at most 0.014.
The reference program's roundings to bfloat16 on the way count: a program that leaves them out, or rounds other values in their place, can miss the bound.
Values may be sent and summed in bfloat16 or wider, within the bound.
No kernel may reach another device: no remote copies, remote signals or barrier semaphores. Data moves between devices by JAX's collectives and lax.ppermute only.
A program may use at most 256 MiB of HBM per device.

```python
import math
import jax
import jax.numpy as jnp
import numpy as np
from jax import lax

D = 1024
H = 16
KV = 8
HD = 64
FF = 512
EXPERTS = 32
TOP = 8
TOK_DEV = 256
GROUPS = 4
REQS = 8
TOKENS_G = 2048
SUFFIX = 1536
PREFIX = 2048
CAP = 96


def draw_prefix_keys(key, part):
    base_keys = jnp.clip(jax.random.normal(key, (GROUPS, PREFIX, KV * HD), jnp.float32) * 4.0, -24.0, 24.0)
    return base_keys.astype(jnp.bfloat16)


def steps_of(key, extent, shards, smallest, largest):
    loudness, own = 1.0, jax.random.fold_in(key, 6)
    for dim, parts in shards:
        heights = jnp.exp(jax.random.uniform(jax.random.fold_in(own, dim), (parts,), jnp.float32, smallest / len(shards), largest / len(shards)))
        loudness = loudness * jnp.repeat(heights, extent[dim] // parts).reshape([-1 if axis == dim else 1 for axis in range(len(extent))])
    return loudness


def split_up(number_of, total, limit, lean):
    weights = [(1 << 20) // math.isqrt(grade ** lean) + 1 for grade in range(2, number_of + 1)]
    surplus, holding = total - limit - (number_of - 1), [1] * (number_of - 1)
    while surplus > 0:
        free = [i for i in range(number_of - 1) if holding[i] < limit]
        whole, left = sum([weights[i] for i in free]), surplus
        for i in free:
            more = min(limit - holding[i], max(1, left * weights[i] // whole), surplus)
            holding[i] = holding[i] + more
            surplus = surplus - more
    return np.array([limit] + holding)


def ragged_sizes(rng, count, total, limit, skew):
    if count == 2:
        one = jax.random.randint(rng, (), max(1, total - limit), min(limit, total - 1) + 1)
        return jnp.stack([one, total - one])
    sizes = jnp.asarray(split_up(count, total, limit, skew), jnp.int32)
    couples = (count - 1) // 2
    giver, taker = sizes[1:1 + 2 * couples:2], sizes[2:2 + 2 * couples:2]
    margin = jnp.minimum(giver - 1, limit - taker)
    moved = jax.random.randint(jax.random.fold_in(rng, 1), (couples,), 0, 1 << 20) % (margin + 1)
    sizes = sizes.at[1:1 + 2 * couples:2].set(giver - moved).at[2:2 + 2 * couples:2].set(taker + moved)
    return sizes[jax.random.permutation(jax.random.fold_in(rng, 2), count)]


def assign_block(rng, own, number, rows, amount, top, reach, skew):
    sequence = jax.random.permutation(rng, amount)
    packed, usual = shares(amount, rows * top, reach, skew, True), shares(amount, rows * top, reach, skew, False)
    places = jnp.arange(amount)

    def named(tallies, offset_by):
        used = int((tallies > 0).sum())
        fixed = max(1, used // 4)
        passed = fixed + (places - fixed + offset_by * (used - fixed)) % max(1, amount - fixed)
        return jnp.zeros((amount,), jnp.int32).at[sequence[jnp.where(places < fixed, places, passed)]].set(jnp.asarray(tallies, jnp.int32))

    tallies = jnp.where(number % 4 == 0, named(packed, number // 4), named(usual, number - number // 4 - 1))
    mixed = jax.random.permutation(jax.random.fold_in(own, 3), amount)
    donor, receiver = mixed[0:amount // 2 * 2:2], mixed[1:amount // 2 * 2:2]
    room = jnp.minimum(tallies[donor] - 1, reach - tallies[receiver]) // 2
    room = jnp.where((donor == sequence[0]) | (receiver == sequence[0]) | (tallies[receiver] == 0), 0, jnp.maximum(room, 0))
    passed = jax.random.randint(jax.random.fold_in(own, 4), (amount // 2,), 0, 1 << 20) % (room + 1)
    tallies = tallies.at[donor].add(-passed).at[receiver].add(passed)
    labels = jnp.searchsorted(jnp.cumsum(tallies), jnp.arange(rows * top), side="right").astype(jnp.int32)
    listing = labels.reshape(top, rows).T
    listing = listing[jax.random.permutation(jax.random.fold_in(own, 1), rows)]
    offset_by = jax.random.randint(jax.random.fold_in(own, 2), (rows, 1), 0, top)
    return jnp.take_along_axis(listing, (jnp.arange(top)[None, :] + offset_by) % top, axis=1)


def shares(number_of, total, most, skew, full):
    portions = [(1 << 20) // math.isqrt(rank ** skew) + 1 for rank in range(1, number_of + 1)]
    largest = most if full else min(most, max(-(-total // number_of), total * portions[0] // sum(portions)))
    least = 1 if total - largest >= number_of - 1 else 0
    given, rest = [largest] + [least] * (number_of - 1), total - largest - least * (number_of - 1)
    while rest > 0:
        free = [i for i in range(1, number_of) if given[i] < largest] or [i for i in range(1, number_of) if given[i] < most]
        mass, remaining = sum([portions[i] for i in free]), rest
        for i in free:
            extra = min(most - given[i], max(1, remaining * portions[i] // mass), rest)
            given[i] = given[i] + extra
            rest = rest - extra
    return np.array(given)


def bell_draw(own_key, dims, deviation, limit, cuts=(), kind=jnp.bfloat16):
    level = steps_of(own_key, dims, cuts, -0.22, 0.18) if cuts else 1.0
    values = jax.random.normal(own_key, dims, jnp.float32) * deviation * level
    return jnp.minimum(jnp.maximum(values, -limit), limit).astype(kind)


def setup_inputs(seed: int = 0) -> dict:
    arg_keys = jax.random.split(jax.random.key(seed), 17)
    tokens = bell_draw(arg_keys[0], (GROUPS, TOKENS_G, D), 1.0, 6.0, ((0, 4), (1, 8)))
    attn_gain = jnp.clip(1.0 + 0.1 * jax.random.normal(arg_keys[1], (D,), jnp.float32), 0.5, 1.5)
    w_query = bell_draw(arg_keys[2], (D, H * HD), (D // 16) ** -0.5, 0.75)
    w_key = bell_draw(arg_keys[3], (D, KV * HD), (D // 16) ** -0.5, 0.75)
    w_value = bell_draw(arg_keys[4], (D, KV * HD), D ** -0.5, 0.1875)
    w_out = bell_draw(arg_keys[5], (H * HD, D), (H * HD) ** -0.5, 0.1875)
    prefix_keys = draw_prefix_keys(jax.random.fold_in(arg_keys[16], 71), 0)
    prefix_values = bell_draw(arg_keys[7], (GROUPS, PREFIX, KV * HD), 1.0, 6.0, ((0, 4), (1, 8)))
    lengths = jax.vmap(lambda own: ragged_sizes(own, REQS, SUFFIX, TOK_DEV, 2))(jax.random.split(arg_keys[8], GROUPS)).reshape((GROUPS, REQS)).astype(jnp.int32)
    assignment = jax.vmap(lambda own: jax.random.permutation(own, REQS))(jax.random.split(arg_keys[9], GROUPS)).reshape((GROUPS, REQS)).astype(jnp.int32)
    moe_gain = jnp.clip(1.0 + 0.1 * jax.random.normal(arg_keys[10], (D,), jnp.float32), 0.5, 1.5)
    expert_ids_keys = jax.random.split(jax.random.fold_in(arg_keys[11], 1), GROUPS * TOKENS_G // TOK_DEV)
    expert_ids_turns = jax.random.permutation(jax.random.fold_in(arg_keys[11], 3), GROUPS * TOKENS_G // TOK_DEV)
    expert_ids = jax.vmap(lambda own, number: assign_block(jax.random.fold_in(arg_keys[11], 2), own, number, TOK_DEV, EXPERTS, TOP, CAP, 2))(expert_ids_keys, expert_ids_turns).reshape((GROUPS, TOKENS_G, TOP))
    route_weights = jnp.clip(0.1 + 0.3 * jax.random.uniform(arg_keys[12], (GROUPS, TOKENS_G, TOP), jnp.float32) ** steps_of(arg_keys[12], (GROUPS, TOKENS_G, TOP), ((0, 4), (1, 8)), -0.2, 0.2), 0.1, 0.4)
    w_gate = bell_draw(arg_keys[13], (EXPERTS, D, FF), D ** -0.5, 0.1875, ((0, 8),))
    w_up = bell_draw(arg_keys[14], (EXPERTS, D, FF), D ** -0.5, 0.1875, ((0, 8),))
    w_down = bell_draw(arg_keys[15], (EXPERTS, FF, D), FF ** -0.5, 0.25, ((0, 8),))
    return dict(tokens=tokens, attn_gain=attn_gain, w_query=w_query, w_key=w_key, w_value=w_value, w_out=w_out, prefix_keys=prefix_keys, prefix_values=prefix_values, lengths=lengths, assignment=assignment, moe_gain=moe_gain, expert_ids=expert_ids, route_weights=route_weights, w_gate=w_gate, w_up=w_up, w_down=w_down)


NORM_EPS = 1e-06
ATTN_SCALE = 0.015625
RESIDUAL_SCALE = 0.22
ROPE_BASE = 10000.0

def normalize(head_rows, gain):
    widened = head_rows.astype(jnp.float32)
    mean_square = lax.optimization_barrier(jnp.mean(widened * widened, axis=-1, keepdims=True))
    return (widened * lax.rsqrt(mean_square + NORM_EPS) * gain).astype(jnp.bfloat16)

def rotate(head_rows, positions):
    half_dim = head_rows.shape[-1] // 2
    frequency = ROPE_BASE ** (-(jnp.arange(half_dim, dtype=jnp.float32) * 2.0 / head_rows.shape[-1]))
    angles = positions[:, None] * frequency[None, :]
    cosine = jnp.cos(angles)[:, None, :]
    sine_part = jnp.sin(angles)[:, None, :]
    first_half = head_rows[..., :half_dim]
    second_half = head_rows[..., half_dim:]
    return jnp.concatenate([first_half * cosine - second_half * sine_part, second_half * cosine + first_half * sine_part], axis=-1)

def attend_block(normed, keys_pre, values_pre, suffix_len, w_query, w_key, w_value):
    tok_count = normed.shape[0]
    positions = (PREFIX + jnp.arange(tok_count, dtype=jnp.int32)).astype(jnp.float32)
    queries = jnp.dot(normed, w_query, preferred_element_type=jnp.float32).reshape(tok_count, H, HD)
    suffix_keys = jnp.dot(normed, w_key, preferred_element_type=jnp.float32).reshape(tok_count, KV, HD)
    suffix_values = jnp.dot(normed, w_value, preferred_element_type=jnp.float32).astype(jnp.bfloat16).reshape(tok_count, KV, HD)
    queries = rotate(queries, positions).astype(jnp.bfloat16)
    suffix_keys = rotate(suffix_keys, positions).astype(jnp.bfloat16)
    keys_all = jnp.concatenate([keys_pre.reshape(PREFIX, KV, HD), suffix_keys], axis=0).astype(jnp.float32)
    values_all = jnp.concatenate([values_pre.reshape(PREFIX, KV, HD), suffix_values], axis=0).astype(jnp.float32)
    grouped = queries.astype(jnp.float32).reshape(tok_count, KV, H // KV, HD)
    scores = jnp.einsum('tkgd,skd->kgts', grouped, keys_all) * ATTN_SCALE
    column = jnp.arange(PREFIX + tok_count, dtype=jnp.int32)
    row_index = jnp.arange(tok_count, dtype=jnp.int32)
    suffix_col = column - PREFIX
    visible = (column[None, :] < PREFIX) | (suffix_col[None, :] <= row_index[:, None]) & (suffix_col[None, :] < suffix_len)
    scores = jnp.where(visible[None, None], scores, -jnp.inf)
    row_max = lax.optimization_barrier(jnp.max(scores, axis=-1, keepdims=True))
    weights = jnp.exp(scores - row_max)
    row_total = lax.optimization_barrier(jnp.sum(weights, axis=-1))
    rounded = lax.optimization_barrier(weights.astype(jnp.bfloat16)).astype(jnp.float32)
    mixed_out = jnp.einsum('kgts,skd->tkgd', rounded, values_all) / jnp.transpose(row_total, (2, 0, 1))[..., None]
    return mixed_out.reshape(tok_count, H * HD).astype(jnp.bfloat16)

def slot_numbers(ids):
    chosen = ids.reshape(-1)
    hit_table = (chosen[:, None] == jnp.arange(EXPERTS, dtype=jnp.int32)[None, :]).astype(jnp.int32)
    before = jnp.cumsum(hit_table, axis=0) - hit_table
    ranked = lax.optimization_barrier(jnp.sum(before * hit_table, axis=1))
    return (chosen, ranked)

def experts_of(moe_in, ids, gains, w_gate, w_up, w_down):
    chosen, ranked = jax.vmap(slot_numbers)(ids.reshape(REQS, TOK_DEV, TOP))
    source = jnp.arange(REQS, dtype=jnp.int32)[:, None]
    column = source * CAP + ranked
    token_rows = jnp.repeat(moe_in.reshape(REQS, TOK_DEV, D), TOP, axis=1)
    buffer_rows = jnp.zeros((EXPERTS, REQS * CAP, D), jnp.bfloat16).at[chosen, column].set(token_rows)

    def one_expert(item_set):
        expert_rows, gate_weight, up_weight, down_weight = item_set
        gate_act = jnp.dot(expert_rows, gate_weight, preferred_element_type=jnp.float32)
        up_act = jnp.dot(expert_rows, up_weight, preferred_element_type=jnp.float32)
        product = (jax.nn.silu(gate_act) * up_act).astype(jnp.bfloat16)
        return jnp.dot(product, down_weight, preferred_element_type=jnp.float32).astype(jnp.bfloat16)
    produced = lax.map(one_expert, (buffer_rows, w_gate, w_up, w_down))
    picked = produced[chosen, column].astype(jnp.float32).reshape(REQS, TOK_DEV, TOP, D)
    weighted = lax.optimization_barrier(jnp.sum(picked * gains.reshape(REQS, TOK_DEV, TOP)[..., None], axis=2))
    return weighted.reshape(TOKENS_G, D).astype(jnp.bfloat16)

def reference(tokens, attn_gain, w_query, w_key, w_value, w_out, prefix_keys, prefix_values, lengths, assignment, moe_gain, expert_ids, route_weights, w_gate, w_up, w_down):

    def one_group(item_set):
        own_rows, keys_pre, values_pre, length_row, order_row, ids, gains = item_set
        normed = normalize(own_rows, attn_gain).reshape(REQS, TOK_DEV, D)
        request_ids = jnp.arange(REQS, dtype=jnp.int32)
        own_lengths = lax.optimization_barrier(jnp.sum(jnp.where(order_row[:, None] == request_ids[None, :], length_row[None, :], 0), axis=1)).astype(jnp.int32)

        def per_index(pair_set):
            block_rows, suffix_len = pair_set
            return attend_block(block_rows, keys_pre, values_pre, suffix_len, w_query, w_key, w_value)
        context = lax.map(per_index, (normed, own_lengths)).reshape(TOKENS_G, H * HD)
        projected = jnp.dot(context, w_out, preferred_element_type=jnp.float32)
        hidden = (own_rows.astype(jnp.float32) + RESIDUAL_SCALE * projected).astype(jnp.bfloat16)
        mixed_out = experts_of(normalize(hidden, moe_gain), ids, gains, w_gate, w_up, w_down)
        return (context, hidden, mixed_out)
    context, hidden, expert_mix = lax.map(one_group, (tokens, prefix_keys, prefix_values, lengths, assignment, expert_ids, route_weights))
    return (context, hidden, expert_mix)
```

```python
import functools
import math

import jax
import jax.numpy as jnp
import numpy as np
from jax import lax
from jax.experimental import pallas as pl
from jax.experimental.pallas import tpu as pltpu
from jax.sharding import PartitionSpec as P

H = 16
KV = 8
HD = 64
EXPERTS = 32
TOP = 8
CAP = 96


NORM_EPS = 1e-06
ATTN_SCALE = 0.015625
RESIDUAL_SCALE = 0.22
ROPE_BASE = 10000.0


def normalize(head_rows, gain):
    widened = head_rows.astype(jnp.float32)
    mean_square = jnp.mean(widened * widened, axis=-1, keepdims=True)
    return (widened * lax.rsqrt(mean_square + NORM_EPS) * gain).astype(jnp.bfloat16)


def rotate(head_rows, positions):
    half_dim = head_rows.shape[-1] // 2
    frequency = ROPE_BASE ** (
        -(jnp.arange(half_dim, dtype=jnp.float32) * 2.0 / head_rows.shape[-1])
    )
    angles = positions[:, None] * frequency[None, :]
    cosine = jnp.cos(angles)[:, None, :]
    sine_part = jnp.sin(angles)[:, None, :]
    first_half = head_rows[..., :half_dim]
    second_half = head_rows[..., half_dim:]
    return jnp.concatenate(
        [
            first_half * cosine - second_half * sine_part,
            second_half * cosine + first_half * sine_part,
        ],
        axis=-1,
    )


def fresh_state(tok_count):
    return (
        jnp.full((KV, H // KV, tok_count), -jnp.inf, jnp.float32),
        jnp.zeros((KV, H // KV, tok_count), jnp.float32),
        jnp.zeros((KV, H // KV, tok_count, HD), jnp.float32),
    )


def absorb(run_state, grouped, key_rows, value_rows, visible):
    run_max, run_sum, run_acc = run_state
    scores = (
        jnp.einsum("tkgd,skd->kgts", grouped, key_rows, preferred_element_type=jnp.float32)
        * ATTN_SCALE
    )
    scores = jnp.where(visible, scores, -jnp.inf)
    new_max = jnp.maximum(run_max, jnp.max(scores, axis=-1))
    factor = jnp.exp(run_max - new_max)
    weights = jnp.exp(scores - new_max[..., None])
    run_sum = run_sum * factor + jnp.sum(weights, axis=-1)
    gathered_values = jnp.einsum(
        "kgts,skd->kgtd",
        weights.astype(jnp.bfloat16),
        value_rows,
        preferred_element_type=jnp.float32,
    )
    run_acc = run_acc * factor[..., None] + gathered_values
    return (new_max, run_sum, run_acc)


def slot_numbers(ids):
    chosen = ids.reshape(-1)
    hit_table = (chosen[:, None] == jnp.arange(EXPERTS, dtype=jnp.int32)[None, :]).astype(jnp.int32)
    before = jnp.cumsum(hit_table, axis=0) - hit_table
    ranked = jnp.sum(before * hit_table, axis=1)
    return (chosen, ranked)


def local_general(
    tokens,
    attn_gain,
    w_query,
    w_key,
    w_value,
    w_out,
    prefix_keys,
    prefix_values,
    lengths,
    assignment,
    moe_gain,
    expert_ids,
    route_weights,
    w_gate,
    w_up,
    w_down,
):
    tok_count = tokens.shape[1]
    model_width = tokens.shape[2]
    peer_count = lax.axis_size("req")
    prefix_len = prefix_keys.shape[1] * peer_count
    own_rows = tokens[0]
    normed = normalize(own_rows, attn_gain)
    my_index = lax.axis_index("req")
    request_ids = jnp.arange(lengths.shape[1], dtype=jnp.int32)
    request = jnp.sum(jnp.where(request_ids == my_index, assignment[0], 0))
    suffix_len = jnp.sum(jnp.where(request_ids == request, lengths[0], 0))
    positions = (prefix_len + jnp.arange(tok_count, dtype=jnp.int32)).astype(jnp.float32)
    queries = jnp.dot(normed, w_query, preferred_element_type=jnp.float32).reshape(tok_count, H, HD)
    queries = rotate(queries, positions).astype(jnp.bfloat16)
    suffix_keys = jnp.dot(normed, w_key, preferred_element_type=jnp.float32).reshape(
        tok_count, KV, HD
    )
    suffix_keys = rotate(suffix_keys, positions).astype(jnp.bfloat16)
    suffix_values = (
        jnp.dot(normed, w_value, preferred_element_type=jnp.float32)
        .astype(jnp.bfloat16)
        .reshape(tok_count, KV, HD)
    )
    grouped = queries.reshape(tok_count, KV, H // KV, HD)
    slot_row = jnp.arange(tok_count, dtype=jnp.int32)
    suffix_visible = (slot_row[None, :] <= slot_row[:, None]) & (slot_row[None, :] < suffix_len)
    suffix_state = absorb(
        fresh_state(tok_count), grouped, suffix_keys, suffix_values, suffix_visible[None, None]
    )
    run_state = suffix_state
    key_piece = lax.all_gather(prefix_keys, "req", axis=1, tiled=True)
    value_piece = lax.all_gather(prefix_values, "req", axis=1, tiled=True)
    piece_len = key_piece.shape[1]
    key_block = math.gcd(piece_len, 512)
    key_blocks = key_piece[0].reshape(piece_len // key_block, key_block, KV, HD)
    value_blocks = value_piece[0].reshape(piece_len // key_block, key_block, KV, HD)

    def absorb_step(carry, pair_set):
        return (absorb(carry, grouped, pair_set[0], pair_set[1], True), None)

    run_state, unused = lax.scan(absorb_step, run_state, (key_blocks, value_blocks))
    run_max, run_sum, run_acc = run_state
    context = (
        (run_acc / run_sum[..., None])
        .transpose(2, 0, 1, 3)
        .reshape(tok_count, H * HD)
        .astype(jnp.bfloat16)
    )
    projected = jnp.dot(context, w_out, preferred_element_type=jnp.float32)
    hidden = (own_rows.astype(jnp.float32) + RESIDUAL_SCALE * projected).astype(jnp.bfloat16)
    moe_in = normalize(hidden, moe_gain)
    chosen, ranked = slot_numbers(expert_ids[0])
    slot_index = chosen * CAP + ranked
    sources = jnp.repeat(moe_in, TOP, axis=0)
    outgoing = jnp.zeros((EXPERTS * CAP, model_width), jnp.bfloat16).at[slot_index].set(sources)
    outgoing = outgoing.reshape(peer_count, EXPERTS // peer_count, CAP, model_width)
    arrived = lax.all_to_all(outgoing, "req", split_axis=0, concat_axis=0, tiled=True)
    slot_span = arrived.shape[2]
    results = []
    for expert_local in range(arrived.shape[1]):
        expert_rows = arrived[:, expert_local].reshape(-1, model_width)
        gate_act = jnp.dot(expert_rows, w_gate[expert_local], preferred_element_type=jnp.float32)
        up_act = jnp.dot(expert_rows, w_up[expert_local], preferred_element_type=jnp.float32)
        product = (jax.nn.silu(gate_act) * up_act).astype(jnp.bfloat16)
        expert_out = jnp.dot(
            product, w_down[expert_local], preferred_element_type=jnp.float32
        ).astype(jnp.bfloat16)
        results.append(expert_out.reshape(arrived.shape[0], slot_span, model_width))
    produced = jnp.stack(results, axis=1)
    returned = lax.all_to_all(produced, "req", split_axis=0, concat_axis=0, tiled=True).reshape(
        EXPERTS * CAP, model_width
    )
    picked = returned[slot_index].astype(jnp.float32).reshape(tok_count, TOP, model_width)
    expert_mix = jnp.sum(picked * route_weights[0][..., None], axis=1).astype(jnp.bfloat16)
    return (context[None], hidden[None], expert_mix[None])


F32 = jnp.float32
BF16 = jnp.bfloat16
MIB = 1 << 20
LANES = 128


def dot(lhs, rhs):
    return jnp.dot(lhs, rhs, preferred_element_type=F32)


def dot_nt(lhs, rhs):
    return lax.dot_general(lhs, rhs, (((1,), (1,)), ((), ())), preferred_element_type=F32)


def dot_tn(lhs, rhs):
    return lax.dot_general(lhs, rhs, (((0,), (0,)), ((), ())), preferred_element_type=F32)


def lane_index(shape):
    return lax.broadcasted_iota(jnp.int32, shape, len(shape) - 1)


def rope_tables(prefix_len, tok_count):
    frequency = ROPE_BASE ** (-(np.arange(HD // 2, dtype=np.float64) * 2.0 / HD))
    angles = (prefix_len + np.arange(tok_count, dtype=np.float64))[:, None] * frequency[None, :]
    cosine, sine = np.cos(angles), np.sin(angles)
    cosine = np.concatenate([cosine, cosine, cosine, cosine], axis=1)
    sine = np.concatenate([-sine, sine, -sine, sine], axis=1)
    return jnp.asarray(cosine, F32), jnp.asarray(sine, F32)


def rotate_tile(tile, cosine, sine):
    first = lane_index(tile.shape) % HD < HD // 2
    other = jnp.where(
        first, pltpu.roll(tile, LANES - HD // 2, 1), pltpu.roll(tile, HD // 2, 1)
    )
    return tile * cosine + other * sine


def project_kernel(tok_ref, gain_ref, wq_ref, wk_ref, wv_ref, cos_ref, sin_ref, q_ref, k_ref, v_ref, normed_ref):
    @pl.when(pl.program_id(0) == 0)
    def _():
        rows = tok_ref[...].astype(F32)
        mean_square = jnp.mean(rows * rows, axis=-1, keepdims=True)
        normed_ref[...] = (rows * lax.rsqrt(mean_square + NORM_EPS) * gain_ref[...]).astype(BF16)

    normed = normed_ref[...]
    tok_count = normed.shape[0]
    cosine, sine = cos_ref[...], sin_ref[...]
    queries = dot(normed, wq_ref[...])
    low = lane_index((tok_count, LANES)) < HD
    for half in range(2):
        tile = rotate_tile(queries[:, half * LANES : (half + 1) * LANES], cosine, sine) * ATTN_SCALE
        turned = pltpu.roll(tile, HD, 1)
        if half == 0:
            first, second = jnp.where(low, tile, 0.0), jnp.where(low, turned, 0.0)
        else:
            first, second = jnp.where(low, 0.0, turned), jnp.where(low, 0.0, tile)
        q_ref[half, :tok_count, :] = first.astype(BF16)
        q_ref[half, tok_count:, :] = second.astype(BF16)
    k_ref[...] = rotate_tile(dot(normed, wk_ref[...]), cosine, sine).astype(BF16)
    v_ref[...] = dot(normed, wv_ref[...]).astype(BF16)


def project(own_rows, attn_gain, w_query, w_key, w_value, prefix_len):
    tok_count, width = own_rows.shape
    cosine, sine = rope_tables(prefix_len, tok_count)
    steps = KV // 2
    whole = lambda i: (0, 0)
    column = lambda i: (0, i)
    return pl.pallas_call(
        project_kernel,
        grid=(steps,),
        in_specs=[
            pl.BlockSpec((tok_count, width), whole),
            pl.BlockSpec((1, width), whole),
            pl.BlockSpec((width, 2 * LANES), column),
            pl.BlockSpec((width, LANES), column),
            pl.BlockSpec((width, LANES), column),
            pl.BlockSpec((tok_count, LANES), whole),
            pl.BlockSpec((tok_count, LANES), whole),
        ],
        out_specs=[
            pl.BlockSpec((2, 2 * tok_count, LANES), lambda i: (i, 0, 0)),
            pl.BlockSpec((tok_count, LANES), column),
            pl.BlockSpec((tok_count, LANES), column),
        ],
        out_shape=[
            jax.ShapeDtypeStruct((KV, 2 * tok_count, LANES), BF16),
            jax.ShapeDtypeStruct((tok_count, KV * HD), BF16),
            jax.ShapeDtypeStruct((tok_count, KV * HD), BF16),
        ],
        scratch_shapes=[pltpu.VMEM((tok_count, width), BF16)],
        compiler_params=pltpu.CompilerParams(vmem_limit_bytes=32 * MIB),
        cost_estimate=pl.CostEstimate(flops=2 * tok_count * width * 2048, bytes_accessed=6 * MIB, transcendentals=0),
        name="project",
    )(own_rows, attn_gain.reshape(1, width), w_query, w_key, w_value, cosine, sine)


def attend_head(half, queries, key_tiles, value_tiles, suffix_mask, state):
    scores = [dot_nt(queries, tile) for tile in key_tiles]
    if suffix_mask is not None:
        scores[0] = jnp.where(suffix_mask, scores[0], -1e30)
    top = functools.reduce(jnp.maximum, scores)
    new_max = jnp.max(top, axis=1, keepdims=True)
    if state is not None:
        new_max = jnp.maximum(new_max, state[0])
    total = None
    for score, tile in zip(scores, value_tiles):
        weights = jnp.exp(score - new_max).astype(BF16)
        low = lane_index(tile.shape) < HD
        one = jnp.ones_like(tile)
        values = jnp.where(low, tile, one) if half == 0 else jnp.where(low, one, tile)
        part = dot(weights, values)
        total = part if total is None else total + part
    if state is not None:
        total = total + state[1] * jnp.exp(state[0] - new_max)
    return new_max, total


def attend_kernel(blocks, first, last, *refs):
    refs = list(refs)
    take = lambda n: [refs.pop(0) for _ in range(n)]
    (q_ref,) = take(1)
    key_refs, value_refs = take(blocks), take(blocks)
    if first:
        (len_ref,) = take(1)
    else:
        max_in, acc_in = take(2)
    if last:
        tok_ref, w_out_ref, gain_ref = take(3)
        ctx_ref, hidden_ref, moe_ref, projected_ref = take(4)
    else:
        max_out, acc_out = take(2)
    step = pl.program_id(0)
    tok_count = q_ref.shape[1] // 2
    suffix_mask = None
    if first:
        shape = (2 * tok_count, tok_count)
        slot = lane_index(shape)
        row = lax.broadcasted_iota(jnp.int32, shape, 0) % tok_count
        suffix_mask = (slot <= row) & (slot < len_ref[0])
    key_tiles = [ref[...] for ref in key_refs]
    value_tiles = [ref[...] for ref in value_refs]
    outs = []
    for half in range(2):
        state = None if first else (max_in[half], acc_in[half])
        new_max, total = attend_head(half, q_ref[half], key_tiles, value_tiles, suffix_mask, state)
        if not last:
            max_out[half] = new_max
            acc_out[half] = total
            continue
        mixed = total / pltpu.roll(total, HD, 1)
        low = lane_index((tok_count, LANES)) < HD
        one, two = mixed[:tok_count], mixed[tok_count:]
        if half == 0:
            outs.append(jnp.where(low, one, pltpu.roll(two, HD, 1)))
        else:
            outs.append(jnp.where(low, pltpu.roll(one, HD, 1), two))
    if last:
        context = jnp.concatenate(outs, axis=1).astype(BF16)
        ctx_ref[...] = context
        part = dot(context, w_out_ref[...])

        @pl.when(step == 0)
        def _():
            projected_ref[...] = part

        @pl.when(step > 0)
        def _():
            projected_ref[...] += part

        @pl.when(step == pl.num_programs(0) - 1)
        def _():
            hidden = (tok_ref[...].astype(F32) + RESIDUAL_SCALE * projected_ref[...]).astype(BF16)
            hidden_ref[...] = hidden
            wide = hidden.astype(F32)
            mean_square = jnp.mean(wide * wide, axis=-1, keepdims=True)
            moe_ref[...] = (wide * lax.rsqrt(mean_square + NORM_EPS) * gain_ref[...]).astype(BF16)


def attend(queries, keys, values, suffix_len=None, state=None, final=None):
    first, last = state is None, final is not None
    blocks = len(keys)
    rows = queries.shape[1]
    tok_count = rows // 2
    tile = pl.BlockSpec((keys[0].shape[0], LANES), lambda i: (0, i))
    pair = lambda lanes: pl.BlockSpec((2, rows, lanes), lambda i: (i, 0, 0))
    args, in_specs = [queries, *keys, *values], [pair(LANES)] + [tile] * (2 * blocks)
    if first:
        args.append(suffix_len)
        in_specs.append(pl.BlockSpec(memory_space=pltpu.SMEM))
    else:
        args.extend(state)
        in_specs.extend([pair(1), pair(LANES)])
    scratch = []
    if last:
        own_rows, w_out, moe_gain = final
        width = own_rows.shape[1]
        args.extend([own_rows, w_out, moe_gain.reshape(1, width)])
        whole = pl.BlockSpec((tok_count, width), lambda i: (0, 0))
        in_specs.extend([whole, pl.BlockSpec((2 * LANES, width), lambda i: (i, 0)), pl.BlockSpec((1, width), lambda i: (0, 0))])
        out_specs = [pl.BlockSpec((tok_count, 2 * LANES), lambda i: (0, i)), whole, whole]
        out_shape = [jax.ShapeDtypeStruct((tok_count, width), BF16)] * 3
        scratch = [pltpu.VMEM((tok_count, width), F32)]
    else:
        out_specs = [pair(1), pair(LANES)]
        out_shape = [jax.ShapeDtypeStruct((KV, rows, 1), F32), jax.ShapeDtypeStruct((KV, rows, LANES), F32)]
    return pl.pallas_call(
        functools.partial(attend_kernel, blocks, first, last),
        grid=(KV // 2,),
        in_specs=in_specs,
        out_specs=out_specs,
        out_shape=out_shape,
        scratch_shapes=scratch,
        compiler_params=pltpu.CompilerParams(vmem_limit_bytes=48 * MIB),
        cost_estimate=pl.CostEstimate(flops=blocks * 1200 * MIB, bytes_accessed=4 * MIB, transcendentals=0),
        name="attend",
    )(*args)


def experts_kernel(sources, *refs):
    refs = list(refs)
    take = lambda n: [refs.pop(0) for _ in range(n)]
    row_refs, route_refs = take(sources), take(sources)
    gate_own, gate_mate, up_own, up_mate, down_own, down_mate = take(6)
    own_ref, *away_refs = take(sources)
    picked_ref, made_ref, combine_ref = refs
    step = pl.program_id(0)
    n_experts = pl.num_programs(0)
    chip_experts = route_refs[0].shape[0]
    tok_count = row_refs[0].shape[0]
    slots = chip_experts * CAP

    @pl.when(step == 0)
    def _():
        before = lax.broadcasted_iota(jnp.int32, (tok_count, tok_count), 0)
        after = lax.broadcasted_iota(jnp.int32, (tok_count, tok_count), 1)
        earlier = jnp.where(before < after, 1.0, 0.0).astype(BF16)
        slot = lax.broadcasted_iota(jnp.int32, (slots, chip_experts), 0)
        expert = lane_index((slots, chip_experts))
        spread = jnp.where(slot // CAP == expert, 1.0, 0.0).astype(BF16)
        within = (lax.broadcasted_iota(jnp.int32, (slots, tok_count), 0) % CAP).astype(F32)
        for source in range(sources):
            route = route_refs[source][...]
            hit = route > 0.0
            ranked = dot(jnp.where(hit, 1.0, 0.0).astype(BF16), earlier)
            ranked = jnp.where(hit, ranked, -1.0).astype(BF16)
            match = dot(spread, ranked) == within
            pick = jnp.where(match, 1.0, 0.0).astype(BF16)
            combine_ref[source] = jnp.where(match, dot(spread, route.astype(BF16)), 0.0).astype(BF16)
            picked = dot(pick, row_refs[source][...]).astype(BF16)
            for e in range(chip_experts):
                picked_ref[e, source] = picked[e * CAP : (e + 1) * CAP]

    def one_expert(gate_ref, up_ref, down_ref):
        width = picked_ref.shape[-1]
        rows = picked_ref[step].reshape(sources * CAP, width)
        gate = dot(rows, gate_ref[0])
        up = dot(rows, up_ref[0])
        act = (jax.nn.silu(gate) * up).astype(BF16)
        made = dot(act, down_ref[0]).astype(BF16)
        for source in range(sources):
            made_ref[source, pl.ds(pl.multiple_of(step * CAP, CAP), CAP), :] = made[source * CAP : (source + 1) * CAP]

    @pl.when(step < n_experts // 2)
    def _():
        one_expert(gate_own, up_own, down_own)

    @pl.when(step >= n_experts // 2)
    def _():
        one_expert(gate_mate, up_mate, down_mate)

    @pl.when(step == n_experts - 1)
    def _():
        for source, ref in enumerate([own_ref, *away_refs]):
            ref[...] = dot_tn(combine_ref[source], made_ref[source]).astype(ref.dtype)


def run_experts(rows, routes, gate, up, down):
    sources = len(rows)
    tok_count, width = rows[0].shape
    local_experts, _, hidden = gate[0].shape
    chip_experts = 2 * local_experts
    whole = lambda shape: pl.BlockSpec(shape, lambda e: (0,) * len(shape))
    own = lambda e: (jnp.minimum(e, local_experts - 1), 0, 0)
    mate = lambda e: (jnp.maximum(e - local_experts, 0), 0, 0)
    wide = [pl.BlockSpec((1, width, hidden), own), pl.BlockSpec((1, width, hidden), mate)]
    tall = [pl.BlockSpec((1, hidden, width), own), pl.BlockSpec((1, hidden, width), mate)]
    return pl.pallas_call(
        functools.partial(experts_kernel, sources),
        grid=(chip_experts,),
        in_specs=[whole((tok_count, width))] * sources
        + [whole((chip_experts, tok_count))] * sources
        + wide + wide + tall,
        out_specs=[whole((tok_count, width))] * sources,
        out_shape=[jax.ShapeDtypeStruct((tok_count, width), F32 if s == 0 else BF16) for s in range(sources)],
        scratch_shapes=[
            pltpu.VMEM((chip_experts, sources, CAP, width), BF16),
            pltpu.VMEM((sources, chip_experts * CAP, width), BF16),
            pltpu.VMEM((sources, chip_experts * CAP, tok_count), BF16),
        ],
        compiler_params=pltpu.CompilerParams(vmem_limit_bytes=56 * MIB),
        cost_estimate=pl.CostEstimate(flops=12000 * MIB, bytes_accessed=30 * MIB, transcendentals=0),
        name="experts",
    )(*rows, *routes, *gate, *up, *down)


CORE, ACROSS_X, ACROSS_Y = 1, 2, 4


def swap(array, mask):
    return lax.ppermute(array, "req", [(i, i ^ mask) for i in range(lax.axis_size("req"))])


def gather_pair(one, two):
    one_x, two_y = swap(one, ACROSS_X), swap(two, ACROSS_Y)
    two_x, one_y = swap(two, ACROSS_X), swap(one, ACROSS_Y)
    one_xy, two_xy = swap(one_x, ACROSS_Y), swap(two_y, ACROSS_X)
    return (one_x, two_x), (one_y, two_y), (one_xy, two_xy)


def routes_of(expert_ids, route_weights, peer_count):
    ids, gains = expert_ids.T, route_weights.T
    named = ids[None, :, :] == jnp.arange(EXPERTS, dtype=jnp.int32)[:, None, None]
    dense = jnp.sum(jnp.where(named, gains[None], 0.0), axis=1)
    tok_count = ids.shape[1]
    dense = dense.reshape(peer_count // 2, 2, EXPERTS // peer_count, tok_count)
    core = lax.axis_index("req") % 2
    dense = jnp.where(core == 0, dense, dense[:, ::-1])
    return dense.reshape(peer_count // 2, 2 * EXPERTS // peer_count, tok_count)


def local_chips(
    tokens,
    attn_gain,
    w_query,
    w_key,
    w_value,
    w_out,
    prefix_keys,
    prefix_values,
    lengths,
    assignment,
    moe_gain,
    expert_ids,
    route_weights,
    w_gate,
    w_up,
    w_down,
):
    peer_count = lax.axis_size("req")
    own_rows = tokens[0]
    tok_count = own_rows.shape[0]
    prefix_len = prefix_keys.shape[1] * peer_count
    my_index = lax.axis_index("req")
    request_ids = jnp.arange(lengths.shape[1], dtype=jnp.int32)
    request = jnp.sum(jnp.where(request_ids == my_index, assignment[0], 0))
    suffix_len = jnp.sum(jnp.where(request_ids == request, lengths[0], 0)).reshape(1)

    keys, values = prefix_keys[0], prefix_values[0]
    far = gather_pair(keys, values)
    pairs = [(keys, values), *far]
    mates = [(swap(k, CORE), swap(v, CORE)) for k, v in pairs]

    routes = routes_of(expert_ids[0], route_weights[0], peer_count)
    chip = my_index // 2
    routes = [
        routes[chip],
        swap(routes[chip ^ 1], ACROSS_X),
        swap(routes[chip ^ 2], ACROSS_Y),
        swap(routes[chip ^ 3], ACROSS_X | ACROSS_Y),
    ]
    gate, up, down = [(w, swap(w, CORE)) for w in (w_gate, w_up, w_down)]

    queries, suffix_keys, suffix_values = project(own_rows, attn_gain, w_query, w_key, w_value, prefix_len)
    near = [(suffix_keys, suffix_values), pairs[0], mates[0]]
    state = attend(queries, [k for k, _ in near], [v for _, v in near], suffix_len=suffix_len)
    rest = pairs[1:] + mates[1:]
    context, hidden, moe_in = attend(
        queries, [k for k, _ in rest], [v for _, v in rest], state=state, final=(own_rows, w_out, moe_gain)
    )

    half = tok_count // 2
    parts = gather_pair(moe_in[:half], moe_in[half:])
    rows = [moe_in] + [jnp.concatenate(part, axis=0) for part in parts]
    own, to_x, to_y, to_xy = run_experts(rows, routes, gate, up, down)

    via_x, via_y = swap(to_xy[:half], ACROSS_X), swap(to_xy[half:], ACROSS_Y)
    low_y = (to_y[:half].astype(F32) + via_x.astype(F32)).astype(BF16)
    high_x = (to_x[half:].astype(F32) + via_y.astype(F32)).astype(BF16)
    low = own[:half] + swap(to_x[:half], ACROSS_X).astype(F32) + swap(low_y, ACROSS_Y).astype(F32)
    high = own[half:] + swap(to_y[half:], ACROSS_Y).astype(F32) + swap(high_x, ACROSS_X).astype(F32)
    expert_mix = jnp.concatenate([low, high], axis=0).astype(BF16)
    return (context[None], hidden[None], expert_mix[None])


def solution(mesh):
    placed = (
        P("grp", "req", None),
        P(),
        P(),
        P(),
        P(),
        P(),
        P("grp", "req", None),
        P("grp", "req", None),
        P("grp", None),
        P("grp", None),
        P(),
        P("grp", "req", None),
        P("grp", "req", None),
        P("req", None, None),
        P("req", None, None),
        P("req", None, None),
    )
    return jax.shard_map(
        local_chips if mesh.shape["req"] == 8 else local_general,
        mesh=mesh,
        in_specs=placed,
        out_specs=(P("grp", "req", None), P("grp", "req", None), P("grp", "req", None)),
        check_vma=False,
    )
```

```python
import functools
import math

import jax
import jax.numpy as jnp
import numpy as np
from jax import lax
from jax.experimental import pallas as pl
from jax.experimental.pallas import tpu as pltpu
from jax.sharding import PartitionSpec as P

H = 16
KV = 8
HD = 64
EXPERTS = 32
TOP = 8
CAP = 96


NORM_EPS = 1e-06
ATTN_SCALE = 0.015625
RESIDUAL_SCALE = 0.22
ROPE_BASE = 10000.0


def normalize(head_rows, gain):
    widened = head_rows.astype(jnp.float32)
    mean_square = jnp.mean(widened * widened, axis=-1, keepdims=True)
    return (widened * lax.rsqrt(mean_square + NORM_EPS) * gain).astype(jnp.bfloat16)


def rotate(head_rows, positions):
    half_dim = head_rows.shape[-1] // 2
    frequency = ROPE_BASE ** (
        -(jnp.arange(half_dim, dtype=jnp.float32) * 2.0 / head_rows.shape[-1])
    )
    angles = positions[:, None] * frequency[None, :]
    cosine = jnp.cos(angles)[:, None, :]
    sine_part = jnp.sin(angles)[:, None, :]
    first_half = head_rows[..., :half_dim]
    second_half = head_rows[..., half_dim:]
    return jnp.concatenate(
        [
            first_half * cosine - second_half * sine_part,
            second_half * cosine + first_half * sine_part,
        ],
        axis=-1,
    )


def fresh_state(tok_count):
    return (
        jnp.full((KV, H // KV, tok_count), -jnp.inf, jnp.float32),
        jnp.zeros((KV, H // KV, tok_count), jnp.float32),
        jnp.zeros((KV, H // KV, tok_count, HD), jnp.float32),
    )


def absorb(run_state, grouped, key_rows, value_rows, visible):
    run_max, run_sum, run_acc = run_state
    scores = (
        jnp.einsum("tkgd,skd->kgts", grouped, key_rows, preferred_element_type=jnp.float32)
        * ATTN_SCALE
    )
    scores = jnp.where(visible, scores, -jnp.inf)
    new_max = jnp.maximum(run_max, jnp.max(scores, axis=-1))
    factor = jnp.exp(run_max - new_max)
    weights = jnp.exp(scores - new_max[..., None])
    run_sum = run_sum * factor + jnp.sum(weights, axis=-1)
    gathered_values = jnp.einsum(
        "kgts,skd->kgtd",
        weights.astype(jnp.bfloat16),
        value_rows,
        preferred_element_type=jnp.float32,
    )
    run_acc = run_acc * factor[..., None] + gathered_values
    return (new_max, run_sum, run_acc)


def slot_numbers(ids):
    chosen = ids.reshape(-1)
    hit_table = (chosen[:, None] == jnp.arange(EXPERTS, dtype=jnp.int32)[None, :]).astype(jnp.int32)
    before = jnp.cumsum(hit_table, axis=0) - hit_table
    ranked = jnp.sum(before * hit_table, axis=1)
    return (chosen, ranked)


def local_general(
    tokens,
    attn_gain,
    w_query,
    w_key,
    w_value,
    w_out,
    prefix_keys,
    prefix_values,
    lengths,
    assignment,
    moe_gain,
    expert_ids,
    route_weights,
    w_gate,
    w_up,
    w_down,
):
    tok_count = tokens.shape[1]
    model_width = tokens.shape[2]
    peer_count = lax.axis_size("req")
    prefix_len = prefix_keys.shape[1] * peer_count
    own_rows = tokens[0]
    normed = normalize(own_rows, attn_gain)
    my_index = lax.axis_index("req")
    request_ids = jnp.arange(lengths.shape[1], dtype=jnp.int32)
    request = jnp.sum(jnp.where(request_ids == my_index, assignment[0], 0))
    suffix_len = jnp.sum(jnp.where(request_ids == request, lengths[0], 0))
    positions = (prefix_len + jnp.arange(tok_count, dtype=jnp.int32)).astype(jnp.float32)
    queries = jnp.dot(normed, w_query, preferred_element_type=jnp.float32).reshape(tok_count, H, HD)
    queries = rotate(queries, positions).astype(jnp.bfloat16)
    suffix_keys = jnp.dot(normed, w_key, preferred_element_type=jnp.float32).reshape(
        tok_count, KV, HD
    )
    suffix_keys = rotate(suffix_keys, positions).astype(jnp.bfloat16)
    suffix_values = (
        jnp.dot(normed, w_value, preferred_element_type=jnp.float32)
        .astype(jnp.bfloat16)
        .reshape(tok_count, KV, HD)
    )
    grouped = queries.reshape(tok_count, KV, H // KV, HD)
    slot_row = jnp.arange(tok_count, dtype=jnp.int32)
    suffix_visible = (slot_row[None, :] <= slot_row[:, None]) & (slot_row[None, :] < suffix_len)
    suffix_state = absorb(
        fresh_state(tok_count), grouped, suffix_keys, suffix_values, suffix_visible[None, None]
    )
    run_state = suffix_state
    key_piece = lax.all_gather(prefix_keys, "req", axis=1, tiled=True)
    value_piece = lax.all_gather(prefix_values, "req", axis=1, tiled=True)
    piece_len = key_piece.shape[1]
    key_block = math.gcd(piece_len, 512)
    key_blocks = key_piece[0].reshape(piece_len // key_block, key_block, KV, HD)
    value_blocks = value_piece[0].reshape(piece_len // key_block, key_block, KV, HD)

    def absorb_step(carry, pair_set):
        return (absorb(carry, grouped, pair_set[0], pair_set[1], True), None)

    run_state, unused = lax.scan(absorb_step, run_state, (key_blocks, value_blocks))
    run_max, run_sum, run_acc = run_state
    context = (
        (run_acc / run_sum[..., None])
        .transpose(2, 0, 1, 3)
        .reshape(tok_count, H * HD)
        .astype(jnp.bfloat16)
    )
    projected = jnp.dot(context, w_out, preferred_element_type=jnp.float32)
    hidden = (own_rows.astype(jnp.float32) + RESIDUAL_SCALE * projected).astype(jnp.bfloat16)
    moe_in = normalize(hidden, moe_gain)
    chosen, ranked = slot_numbers(expert_ids[0])
    slot_index = chosen * CAP + ranked
    sources = jnp.repeat(moe_in, TOP, axis=0)
    outgoing = jnp.zeros((EXPERTS * CAP, model_width), jnp.bfloat16).at[slot_index].set(sources)
    outgoing = outgoing.reshape(peer_count, EXPERTS // peer_count, CAP, model_width)
    arrived = lax.all_to_all(outgoing, "req", split_axis=0, concat_axis=0, tiled=True)
    slot_span = arrived.shape[2]
    results = []
    for expert_local in range(arrived.shape[1]):
        expert_rows = arrived[:, expert_local].reshape(-1, model_width)
        gate_act = jnp.dot(expert_rows, w_gate[expert_local], preferred_element_type=jnp.float32)
        up_act = jnp.dot(expert_rows, w_up[expert_local], preferred_element_type=jnp.float32)
        product = (jax.nn.silu(gate_act) * up_act).astype(jnp.bfloat16)
        expert_out = jnp.dot(
            product, w_down[expert_local], preferred_element_type=jnp.float32
        ).astype(jnp.bfloat16)
        results.append(expert_out.reshape(arrived.shape[0], slot_span, model_width))
    produced = jnp.stack(results, axis=1)
    returned = lax.all_to_all(produced, "req", split_axis=0, concat_axis=0, tiled=True).reshape(
        EXPERTS * CAP, model_width
    )
    picked = returned[slot_index].astype(jnp.float32).reshape(tok_count, TOP, model_width)
    expert_mix = jnp.sum(picked * route_weights[0][..., None], axis=1).astype(jnp.bfloat16)
    return (context[None], hidden[None], expert_mix[None])


F32 = jnp.float32
BF16 = jnp.bfloat16
MIB = 1 << 20
LANES = 128
VMEM_ATTEND = 48
VMEM_EXPERTS = 60


def dot(lhs, rhs):
    return jnp.dot(lhs, rhs, preferred_element_type=F32)


def dot_nt(lhs, rhs):
    return lax.dot_general(lhs, rhs, (((1,), (1,)), ((), ())), preferred_element_type=F32)


def dot_tn(lhs, rhs):
    return lax.dot_general(lhs, rhs, (((0,), (0,)), ((), ())), preferred_element_type=F32)


def held_in_hbm(arrays):
    return [pltpu.with_memory_space_constraint(array, pltpu.HBM) for array in arrays]


def lane_index(shape):
    return lax.broadcasted_iota(jnp.int32, shape, len(shape) - 1)


def rope_tables(prefix_len, tok_count):
    frequency = ROPE_BASE ** (-(np.arange(HD // 2, dtype=np.float64) * 2.0 / HD))
    angles = (prefix_len + np.arange(tok_count, dtype=np.float64))[:, None] * frequency[None, :]
    cosine, sine = np.cos(angles), np.sin(angles)
    cosine = np.concatenate([cosine, cosine, cosine, cosine], axis=1)
    sine = np.concatenate([-sine, sine, -sine, sine], axis=1)
    return jnp.asarray(cosine, F32), jnp.asarray(sine, F32)


def rotate_tile(tile, cosine, sine):
    first = lane_index(tile.shape) % HD < HD // 2
    other = jnp.where(
        first, pltpu.roll(tile, LANES - HD // 2, 1), pltpu.roll(tile, HD // 2, 1)
    )
    return tile * cosine + other * sine


SUM_ROWS = 16


def attend_pair(queries, key_tiles, value_tiles, suffix_len, states):
    tok_count = queries[0].shape[0] // 2
    turned = [tile.astype(F32).T.astype(BF16) for tile in value_tiles]
    ones = jnp.ones((SUM_ROWS, turned[0].shape[1]), BF16)
    scores = []
    for half in range(2):
        scores.append([dot_nt(tile, queries[half]) for tile in key_tiles])
        if suffix_len is not None:
            shape = scores[half][0].shape
            slot = lax.broadcasted_iota(jnp.int32, shape, 0)
            row = lane_index(shape) % tok_count
            visible = (slot <= row) & (slot < suffix_len)
            scores[half][0] = jnp.where(visible, scores[half][0], -1e30)
    results = []
    for half in range(2):
        new_max = jnp.max(functools.reduce(jnp.maximum, scores[half]), axis=0, keepdims=True)
        total = None
        if states is not None:
            old_max, old_total = states[half]
            new_max = jnp.maximum(new_max, old_max)
            total = old_total * jnp.exp(old_max - new_max)
        for score, tile in zip(scores[half], turned):
            weights = jnp.exp(score - new_max).astype(BF16)
            part = dot(jnp.concatenate([tile[half * HD : (half + 1) * HD], ones], axis=0), weights)
            total = part if total is None else total + part
        results.append((new_max, total))
    return results


def near_kernel(blocks, *refs):
    tok_ref, gain_ref, wq_ref, wk_ref, wv_ref, cos_ref, sin_ref, len_ref = refs[:8]
    key_refs, value_refs = refs[8 : 8 + blocks], refs[8 + blocks : 8 + 2 * blocks]
    q_ref, max_ref, acc_ref, normed_ref = refs[8 + 2 * blocks :]

    @pl.when(pl.program_id(0) == 0)
    def _():
        rows = tok_ref[...].astype(F32)
        mean_square = jnp.mean(rows * rows, axis=-1, keepdims=True)
        normed_ref[...] = (rows * lax.rsqrt(mean_square + NORM_EPS) * gain_ref[...]).astype(BF16)

    normed = normed_ref[...]
    tok_count = normed.shape[0]
    cosine, sine = cos_ref[...], sin_ref[...]
    low = lane_index((tok_count, LANES)) < HD
    projected = dot(normed, wq_ref[...])
    suffix_keys = rotate_tile(dot(normed, wk_ref[...]), cosine, sine).astype(BF16)
    suffix_values = dot(normed, wv_ref[...]).astype(BF16)
    queries = []
    for half in range(2):
        tile = rotate_tile(projected[:, half * LANES : (half + 1) * LANES], cosine, sine) * ATTN_SCALE
        turned = pltpu.roll(tile, HD, 1)
        if half == 0:
            first, second = jnp.where(low, tile, 0.0), jnp.where(low, turned, 0.0)
        else:
            first, second = jnp.where(low, 0.0, turned), jnp.where(low, 0.0, tile)
        queries.append(jnp.concatenate([first, second], axis=0).astype(BF16))
        q_ref[half] = queries[half]
    key_tiles = [suffix_keys] + [ref[...] for ref in key_refs]
    value_tiles = [suffix_values] + [ref[...] for ref in value_refs]
    results = attend_pair(queries, key_tiles, value_tiles, len_ref[0], None)
    for half, (new_max, total) in enumerate(results):
        max_ref[half] = new_max
        acc_ref[half] = total


def pair_spec(*shape):
    return pl.BlockSpec((2, *shape), lambda i: (i, 0, 0))


def whole_spec(*shape):
    return pl.BlockSpec(shape, lambda i: (0,) * len(shape))


def cached_specs(cached):
    specs = []
    for kind in range(2):
        for array in cached:
            stacked = not isinstance(array, tuple)
            length = array.shape[0] // 2 if stacked else array[kind].shape[0]
            place = kind if stacked else 0
            specs.append(pl.BlockSpec((length, LANES), lambda i, place=place: (place, i)))
    return specs


def cached_args(cached):
    return [array[kind] if isinstance(array, tuple) else array for kind in range(2) for array in cached]


def attend_near(own_rows, attn_gain, w_query, w_key, w_value, prefix_len, suffix_len, cached):
    tok_count, width = own_rows.shape
    rows, blocks = 2 * tok_count, len(cached)
    cosine, sine = rope_tables(prefix_len, tok_count)
    column = lambda i: (0, i)
    queries, *state = pl.pallas_call(
        functools.partial(near_kernel, blocks),
        grid=(KV // 2,),
        in_specs=[
            whole_spec(tok_count, width),
            whole_spec(1, width),
            pl.BlockSpec((width, 2 * LANES), column),
            pl.BlockSpec((width, LANES), column),
            pl.BlockSpec((width, LANES), column),
            whole_spec(tok_count, LANES),
            whole_spec(tok_count, LANES),
            pl.BlockSpec(memory_space=pltpu.SMEM),
        ]
        + cached_specs(cached),
        out_specs=[pair_spec(rows, LANES), pair_spec(1, rows), pair_spec(HD + SUM_ROWS, rows)],
        out_shape=[
            pltpu.HBM((KV, rows, LANES), BF16),
            pltpu.HBM((KV, 1, rows), F32),
            pltpu.HBM((KV, HD + SUM_ROWS, rows), F32),
        ],
        scratch_shapes=[pltpu.VMEM((tok_count, width), BF16)],
        compiler_params=pltpu.CompilerParams(vmem_limit_bytes=VMEM_ATTEND * MIB),
        cost_estimate=pl.CostEstimate(flops=4000 * MIB, bytes_accessed=6 * MIB, transcendentals=0),
        name="attend_near",
    )(
        *held_in_hbm([own_rows, attn_gain.reshape(1, width), w_query, w_key, w_value, cosine, sine]),
        suffix_len,
        *held_in_hbm(cached_args(cached)),
    )
    return queries, state


def far_kernel(blocks, last, *refs):
    q_ref, max_in, acc_in = refs[:3]
    key_refs, value_refs = refs[3 : 3 + blocks], refs[3 + blocks : 3 + 2 * blocks]
    refs = refs[3 + 2 * blocks :]
    states = [(max_in[half], acc_in[half]) for half in range(2)]
    key_tiles = [ref[...] for ref in key_refs]
    value_tiles = [ref[...] for ref in value_refs]
    results = attend_pair([q_ref[0], q_ref[1]], key_tiles, value_tiles, None, states)
    if not last:
        max_ref, acc_ref = refs
        for half, (new_max, total) in enumerate(results):
            max_ref[half] = new_max
            acc_ref[half] = total
        return
    tok_ref, w_out_ref, gain_ref, ctx_ref, hidden_ref, moe_ref, projected_ref = refs
    tok_count = tok_ref.shape[0]
    step = pl.program_id(0)
    tiles = []
    for _, total in results:
        mixed = total[:HD] / total[HD : HD + 1]
        tiles.append(jnp.concatenate([mixed[:, :tok_count], mixed[:, tok_count:]], axis=0).T)
    context = jnp.concatenate(tiles, axis=1).astype(BF16)
    ctx_ref[...] = context
    part = dot(context, w_out_ref[...])

    @pl.when(step == 0)
    def _():
        projected_ref[...] = part

    @pl.when(step > 0)
    def _():
        projected_ref[...] += part

    @pl.when(step == pl.num_programs(0) - 1)
    def _():
        hidden = (tok_ref[...].astype(F32) + RESIDUAL_SCALE * projected_ref[...]).astype(BF16)
        hidden_ref[...] = hidden
        wide = hidden.astype(F32)
        mean_square = jnp.mean(wide * wide, axis=-1, keepdims=True)
        moe_ref[...] = (wide * lax.rsqrt(mean_square + NORM_EPS) * gain_ref[...]).astype(BF16)


def attend_far(queries, state, cached, final=None):
    last, blocks, rows = final is not None, len(cached), queries.shape[1]
    tok_count = rows // 2
    args = [queries, *state, *cached_args(cached)]
    in_specs = [pair_spec(rows, LANES), pair_spec(1, rows), pair_spec(HD + SUM_ROWS, rows)]
    in_specs += cached_specs(cached)
    if last:
        own_rows, w_out, moe_gain = final
        width = own_rows.shape[1]
        args += [own_rows, w_out, moe_gain.reshape(1, width)]
        whole = whole_spec(tok_count, width)
        in_specs += [whole, pl.BlockSpec((2 * LANES, width), lambda i: (i, 0)), whole_spec(1, width)]
        out_specs = [pl.BlockSpec((tok_count, 2 * LANES), lambda i: (0, i)), whole, whole]
        out_shape = [pltpu.HBM((tok_count, width), BF16)] * 3
        scratch = [pltpu.VMEM((tok_count, width), F32)]
    else:
        out_specs = in_specs[1:3]
        out_shape = [pltpu.HBM(array.shape, F32) for array in state]
        scratch = []
    return pl.pallas_call(
        functools.partial(far_kernel, blocks, last),
        grid=(KV // 2,),
        in_specs=in_specs,
        out_specs=out_specs,
        out_shape=out_shape,
        scratch_shapes=scratch,
        compiler_params=pltpu.CompilerParams(vmem_limit_bytes=VMEM_ATTEND * MIB),
        cost_estimate=pl.CostEstimate(flops=blocks * 1200 * MIB, bytes_accessed=4 * MIB, transcendentals=0),
        name="attend_far",
    )(*held_in_hbm(args))


def experts_kernel(sources, pieces, *refs):
    refs = list(refs)
    take = lambda n: [refs.pop(0) for _ in range(n)]
    row_refs, route_refs = [take(pieces) for _ in range(sources)], take(sources)
    weight_refs = [take(2) for _ in range(3)]
    out_refs = take(sources)
    picked_ref, made_ref, combine_ref, *held, sem = refs
    local_experts = weight_refs[0][0].shape[0]
    chip_experts = route_refs[0].shape[0]
    tok_count, width = out_refs[0].shape
    slots = chip_experts * CAP

    def copy(kind, owner, e, expert):
        return pltpu.make_async_copy(
            weight_refs[kind][owner].at[e], held[kind].at[expert], sem.at[kind, expert]
        )

    for expert in range(chip_experts):
        for kind in range(3):
            copy(kind, expert // local_experts, expert % local_experts, expert).start()

    before = lax.broadcasted_iota(jnp.int32, (tok_count, tok_count), 0)
    after = lane_index((tok_count, tok_count))
    earlier = jnp.where(before < after, 1.0, 0.0).astype(BF16)
    slot = lax.broadcasted_iota(jnp.int32, (slots, chip_experts), 0)
    spread = jnp.where(slot // CAP == lane_index((slots, chip_experts)), 1.0, 0.0).astype(BF16)
    within = (lax.broadcasted_iota(jnp.int32, (slots, tok_count), 0) % CAP).astype(F32)
    for source in range(sources):
        route = route_refs[source][...]
        hit = route > 0.0
        ranked = dot(jnp.where(hit, 1.0, 0.0).astype(BF16), earlier)
        ranked = jnp.where(hit, ranked, -1.0).astype(BF16)
        match = dot(spread, ranked) == within
        pick = jnp.where(match, 1.0, 0.0).astype(BF16)
        combine_ref[source] = jnp.where(match, dot(spread, route.astype(BF16)), 0.0).astype(BF16)
        rows = jnp.concatenate([ref[...] for ref in row_refs[source]], axis=0)
        picked = dot(pick, rows).astype(BF16)
        for e in range(chip_experts):
            picked_ref[e, source] = picked[e * CAP : (e + 1) * CAP]

    def one_expert(expert, carry):
        for kind in range(3):
            copy(kind, 0, 0, expert).wait()
        rows = picked_ref[expert].reshape(sources * CAP, width)
        gate = dot(rows, held[0][expert])
        up = dot(rows, held[1][expert])
        act = (jax.nn.silu(gate) * up).astype(BF16)
        made = dot(act, held[2][expert]).astype(BF16)
        for source in range(sources):
            made_ref[source, pl.ds(pl.multiple_of(expert * CAP, CAP), CAP), :] = made[
                source * CAP : (source + 1) * CAP
            ]
        return carry

    lax.fori_loop(0, chip_experts, one_expert, 0)
    for source, ref in enumerate(out_refs):
        ref[...] = dot_tn(combine_ref[source], made_ref[source]).astype(ref.dtype)


def run_experts(rows, routes, weights, out_type=BF16):
    sources, pieces = len(rows), len(rows[0])
    tok_count, width = routes[0].shape[1], rows[0][0].shape[1]
    chip_experts = routes[0].shape[0]
    hidden = weights[0][0].shape[2]
    vmem = pl.BlockSpec(memory_space=pltpu.VMEM)
    return pl.pallas_call(
        functools.partial(experts_kernel, sources, pieces),
        in_specs=[vmem] * ((pieces + 1) * sources) + [pl.BlockSpec(memory_space=pl.ANY)] * 6,
        out_specs=[vmem] * sources,
        out_shape=[pltpu.HBM((tok_count, width), out_type)] * sources,
        scratch_shapes=[
            pltpu.VMEM((chip_experts, sources, CAP, width), BF16),
            pltpu.VMEM((sources, chip_experts * CAP, width), BF16),
            pltpu.VMEM((sources, chip_experts * CAP, tok_count), BF16),
            pltpu.VMEM((chip_experts, width, hidden), BF16),
            pltpu.VMEM((chip_experts, width, hidden), BF16),
            pltpu.VMEM((chip_experts, hidden, width), BF16),
            pltpu.SemaphoreType.DMA((3, chip_experts)),
        ],
        compiler_params=pltpu.CompilerParams(vmem_limit_bytes=VMEM_EXPERTS * MIB),
        cost_estimate=pl.CostEstimate(flops=12000 * MIB, bytes_accessed=30 * MIB, transcendentals=0),
        name="experts",
    )(*held_in_hbm([*[piece for source in rows for piece in source], *routes, *[array for pair in weights for array in pair]]))


CORE, ACROSS_X, ACROSS_Y = 1, 2, 4


def swap(array, mask):
    return lax.ppermute(array, "req", [(i, i ^ mask) for i in range(lax.axis_size("req"))])


def ordered(*arrays):
    return lax.optimization_barrier(arrays)


def routes_of(expert_ids, route_weights, peer_count):
    ids, gains = expert_ids.T, route_weights.T
    named = ids[None, :, :] == jnp.arange(EXPERTS, dtype=jnp.int32)[:, None, None]
    dense = jnp.sum(jnp.where(named, gains[None], 0.0), axis=1)
    tok_count = ids.shape[1]
    dense = dense.reshape(peer_count // 2, 2, EXPERTS // peer_count, tok_count)
    core = lax.axis_index("req") % 2
    dense = jnp.where(core == 0, dense, dense[:, ::-1])
    return dense.reshape(peer_count // 2, 2 * EXPERTS // peer_count, tok_count)


def local_chips(
    tokens,
    attn_gain,
    w_query,
    w_key,
    w_value,
    w_out,
    prefix_keys,
    prefix_values,
    lengths,
    assignment,
    moe_gain,
    expert_ids,
    route_weights,
    w_gate,
    w_up,
    w_down,
):
    peer_count = lax.axis_size("req")
    own_rows = tokens[0]
    tok_count = own_rows.shape[0]
    prefix_len = prefix_keys.shape[1] * peer_count
    my_index = lax.axis_index("req")
    request_ids = jnp.arange(lengths.shape[1], dtype=jnp.int32)
    request = jnp.sum(jnp.where(request_ids == my_index, assignment[0], 0))
    suffix_len = jnp.sum(jnp.where(request_ids == request, lengths[0], 0)).reshape(1)

    keys, values = prefix_keys[0], prefix_values[0]
    block = keys.shape[0]
    cached = jnp.concatenate([keys, values], axis=0)
    cached_x, cached_y = swap(cached, ACROSS_X), swap(cached, ACROSS_Y)
    cached_mate = swap(cached, CORE)
    gate, up = (w_gate, swap(w_gate, CORE)), (w_up, swap(w_up, CORE))
    routes = routes_of(expert_ids[0], route_weights[0], peer_count)
    chip = my_index // 2
    own_route = routes[chip]

    queries, state = attend_near(
        own_rows, attn_gain, w_query, w_key, w_value, prefix_len, suffix_len, [(keys, values), cached_mate]
    )
    cached_x, cached_y, w_down, routes, *state = ordered(cached_x, cached_y, w_down, routes, *state)
    far = [swap(cached_x[:block], ACROSS_Y), swap(cached_y[block:], ACROSS_X)]
    mates = [swap(cached_x, CORE), swap(cached_y, CORE)]
    routes = [
        own_route,
        swap(routes[chip ^ 1], ACROSS_X),
        swap(routes[chip ^ 2], ACROSS_Y),
        swap(routes[chip ^ 3], ACROSS_X | ACROSS_Y),
    ]
    cached_x, cached_y, w_down, *mates = ordered(cached_x, cached_y, w_down, *mates)
    down = (w_down, swap(w_down, CORE))
    state = attend_far(queries, state, [cached_x, cached_y, *mates])
    *far, routes_x, routes_y, routes_xy, s0, s1 = ordered(*far, *routes[1:], *state)
    context, hidden, moe_in = attend_far(
        queries,
        [s0, s1],
        [tuple(far), tuple(swap(array, CORE) for array in far)],
        final=(own_rows, w_out, moe_gain),
    )

    weights = (gate, up, down)
    half = tok_count // 2
    rows_x, rows_y = swap(moe_in, ACROSS_X), swap(moe_in, ACROSS_Y)
    (own,) = run_experts([[moe_in]], [own_route], weights, F32)
    rows_x, rows_y, own = ordered(rows_x, rows_y, own)
    low_xy, high_xy = swap(rows_x[:half], ACROSS_Y), swap(rows_y[half:], ACROSS_X)
    to_x, to_y = run_experts([[rows_x], [rows_y]], [routes_x, routes_y], weights)
    low_xy, high_xy, to_x, to_y = ordered(low_xy, high_xy, to_x, to_y)
    from_x, from_y = swap(to_x, ACROSS_X), swap(to_y, ACROSS_Y)
    (to_xy,) = run_experts([[low_xy, high_xy]], [routes_xy], weights)
    from_xy = swap(to_xy, ACROSS_X | ACROSS_Y)
    partial, from_xy = ordered(own + from_x.astype(F32) + from_y.astype(F32), from_xy)
    expert_mix = (partial + from_xy.astype(F32)).astype(BF16)
    return (context[None], hidden[None], expert_mix[None])


def solution(mesh):
    placed = (
        P("grp", "req", None),
        P(),
        P(),
        P(),
        P(),
        P(),
        P("grp", "req", None),
        P("grp", "req", None),
        P("grp", None),
        P("grp", None),
        P(),
        P("grp", "req", None),
        P("grp", "req", None),
        P("req", None, None),
        P("req", None, None),
        P("req", None, None),
    )
    return jax.shard_map(
        local_chips if mesh.shape["req"] == 8 else local_general,
        mesh=mesh,
        in_specs=placed,
        out_specs=(P("grp", "req", None), P("grp", "req", None), P("grp", "req", None)),
        check_vma=False,
    )
```

```python
import functools
import math

import jax
import jax.numpy as jnp
import numpy as np
from jax import lax
from jax.experimental import pallas as pl
from jax.experimental.pallas import tpu as pltpu
from jax.sharding import PartitionSpec as P

H = 16
KV = 8
HD = 64
EXPERTS = 32
TOP = 8
CAP = 96


NORM_EPS = 1e-06
ATTN_SCALE = 0.015625
RESIDUAL_SCALE = 0.22
ROPE_BASE = 10000.0


def normalize(head_rows, gain):
    widened = head_rows.astype(jnp.float32)
    mean_square = jnp.mean(widened * widened, axis=-1, keepdims=True)
    return (widened * lax.rsqrt(mean_square + NORM_EPS) * gain).astype(jnp.bfloat16)


def rotate(head_rows, positions):
    half_dim = head_rows.shape[-1] // 2
    frequency = ROPE_BASE ** (
        -(jnp.arange(half_dim, dtype=jnp.float32) * 2.0 / head_rows.shape[-1])
    )
    angles = positions[:, None] * frequency[None, :]
    cosine = jnp.cos(angles)[:, None, :]
    sine_part = jnp.sin(angles)[:, None, :]
    first_half = head_rows[..., :half_dim]
    second_half = head_rows[..., half_dim:]
    return jnp.concatenate(
        [
            first_half * cosine - second_half * sine_part,
            second_half * cosine + first_half * sine_part,
        ],
        axis=-1,
    )


def fresh_state(tok_count):
    return (
        jnp.full((KV, H // KV, tok_count), -jnp.inf, jnp.float32),
        jnp.zeros((KV, H // KV, tok_count), jnp.float32),
        jnp.zeros((KV, H // KV, tok_count, HD), jnp.float32),
    )


def absorb(run_state, grouped, key_rows, value_rows, visible):
    run_max, run_sum, run_acc = run_state
    scores = (
        jnp.einsum("tkgd,skd->kgts", grouped, key_rows, preferred_element_type=jnp.float32)
        * ATTN_SCALE
    )
    scores = jnp.where(visible, scores, -jnp.inf)
    new_max = jnp.maximum(run_max, jnp.max(scores, axis=-1))
    factor = jnp.exp(run_max - new_max)
    weights = jnp.exp(scores - new_max[..., None])
    run_sum = run_sum * factor + jnp.sum(weights, axis=-1)
    gathered_values = jnp.einsum(
        "kgts,skd->kgtd",
        weights.astype(jnp.bfloat16),
        value_rows,
        preferred_element_type=jnp.float32,
    )
    run_acc = run_acc * factor[..., None] + gathered_values
    return (new_max, run_sum, run_acc)


def slot_numbers(ids):
    chosen = ids.reshape(-1)
    hit_table = (chosen[:, None] == jnp.arange(EXPERTS, dtype=jnp.int32)[None, :]).astype(jnp.int32)
    before = jnp.cumsum(hit_table, axis=0) - hit_table
    ranked = jnp.sum(before * hit_table, axis=1)
    return (chosen, ranked)


def local_general(
    tokens,
    attn_gain,
    w_query,
    w_key,
    w_value,
    w_out,
    prefix_keys,
    prefix_values,
    lengths,
    assignment,
    moe_gain,
    expert_ids,
    route_weights,
    w_gate,
    w_up,
    w_down,
):
    tok_count = tokens.shape[1]
    model_width = tokens.shape[2]
    peer_count = lax.axis_size("req")
    prefix_len = prefix_keys.shape[1] * peer_count
    own_rows = tokens[0]
    normed = normalize(own_rows, attn_gain)
    my_index = lax.axis_index("req")
    request_ids = jnp.arange(lengths.shape[1], dtype=jnp.int32)
    request = jnp.sum(jnp.where(request_ids == my_index, assignment[0], 0))
    suffix_len = jnp.sum(jnp.where(request_ids == request, lengths[0], 0))
    positions = (prefix_len + jnp.arange(tok_count, dtype=jnp.int32)).astype(jnp.float32)
    queries = jnp.dot(normed, w_query, preferred_element_type=jnp.float32).reshape(tok_count, H, HD)
    queries = rotate(queries, positions).astype(jnp.bfloat16)
    suffix_keys = jnp.dot(normed, w_key, preferred_element_type=jnp.float32).reshape(
        tok_count, KV, HD
    )
    suffix_keys = rotate(suffix_keys, positions).astype(jnp.bfloat16)
    suffix_values = (
        jnp.dot(normed, w_value, preferred_element_type=jnp.float32)
        .astype(jnp.bfloat16)
        .reshape(tok_count, KV, HD)
    )
    grouped = queries.reshape(tok_count, KV, H // KV, HD)
    slot_row = jnp.arange(tok_count, dtype=jnp.int32)
    suffix_visible = (slot_row[None, :] <= slot_row[:, None]) & (slot_row[None, :] < suffix_len)
    suffix_state = absorb(
        fresh_state(tok_count), grouped, suffix_keys, suffix_values, suffix_visible[None, None]
    )
    run_state = suffix_state
    key_piece = lax.all_gather(prefix_keys, "req", axis=1, tiled=True)
    value_piece = lax.all_gather(prefix_values, "req", axis=1, tiled=True)
    piece_len = key_piece.shape[1]
    key_block = math.gcd(piece_len, 512)
    key_blocks = key_piece[0].reshape(piece_len // key_block, key_block, KV, HD)
    value_blocks = value_piece[0].reshape(piece_len // key_block, key_block, KV, HD)

    def absorb_step(carry, pair_set):
        return (absorb(carry, grouped, pair_set[0], pair_set[1], True), None)

    run_state, unused = lax.scan(absorb_step, run_state, (key_blocks, value_blocks))
    run_max, run_sum, run_acc = run_state
    context = (
        (run_acc / run_sum[..., None])
        .transpose(2, 0, 1, 3)
        .reshape(tok_count, H * HD)
        .astype(jnp.bfloat16)
    )
    projected = jnp.dot(context, w_out, preferred_element_type=jnp.float32)
    hidden = (own_rows.astype(jnp.float32) + RESIDUAL_SCALE * projected).astype(jnp.bfloat16)
    moe_in = normalize(hidden, moe_gain)
    chosen, ranked = slot_numbers(expert_ids[0])
    slot_index = chosen * CAP + ranked
    sources = jnp.repeat(moe_in, TOP, axis=0)
    outgoing = jnp.zeros((EXPERTS * CAP, model_width), jnp.bfloat16).at[slot_index].set(sources)
    outgoing = outgoing.reshape(peer_count, EXPERTS // peer_count, CAP, model_width)
    arrived = lax.all_to_all(outgoing, "req", split_axis=0, concat_axis=0, tiled=True)
    slot_span = arrived.shape[2]
    results = []
    for expert_local in range(arrived.shape[1]):
        expert_rows = arrived[:, expert_local].reshape(-1, model_width)
        gate_act = jnp.dot(expert_rows, w_gate[expert_local], preferred_element_type=jnp.float32)
        up_act = jnp.dot(expert_rows, w_up[expert_local], preferred_element_type=jnp.float32)
        product = (jax.nn.silu(gate_act) * up_act).astype(jnp.bfloat16)
        expert_out = jnp.dot(
            product, w_down[expert_local], preferred_element_type=jnp.float32
        ).astype(jnp.bfloat16)
        results.append(expert_out.reshape(arrived.shape[0], slot_span, model_width))
    produced = jnp.stack(results, axis=1)
    returned = lax.all_to_all(produced, "req", split_axis=0, concat_axis=0, tiled=True).reshape(
        EXPERTS * CAP, model_width
    )
    picked = returned[slot_index].astype(jnp.float32).reshape(tok_count, TOP, model_width)
    expert_mix = jnp.sum(picked * route_weights[0][..., None], axis=1).astype(jnp.bfloat16)
    return (context[None], hidden[None], expert_mix[None])


F32 = jnp.float32
BF16 = jnp.bfloat16
MIB = 1 << 20
LANES = 128
VMEM_ATTEND = 48
NOTE_ROWS = 16
VMEM_EXPERTS = 50


def dot(lhs, rhs):
    return jnp.dot(lhs, rhs, preferred_element_type=F32)


def dot_nt(lhs, rhs):
    return lax.dot_general(lhs, rhs, (((1,), (1,)), ((), ())), preferred_element_type=F32)


def dot_tn(lhs, rhs):
    return lax.dot_general(lhs, rhs, (((0,), (0,)), ((), ())), preferred_element_type=F32)


def held_in_hbm(arrays):
    return [pltpu.with_memory_space_constraint(array, pltpu.HBM) for array in arrays]


def held_in_vmem(arrays):
    return [pltpu.with_memory_space_constraint(array, pltpu.VMEM) for array in arrays]


def lane_index(shape):
    return lax.broadcasted_iota(jnp.int32, shape, len(shape) - 1)


def rope_tables(prefix_len, tok_count):
    frequency = ROPE_BASE ** (-(np.arange(HD // 2, dtype=np.float64) * 2.0 / HD))
    angles = (prefix_len + np.arange(tok_count, dtype=np.float64))[:, None] * frequency[None, :]
    cosine, sine = np.cos(angles), np.sin(angles)
    cosine = np.concatenate([cosine, cosine, cosine, cosine], axis=1)
    sine = np.concatenate([-sine, sine, -sine, sine], axis=1)
    return jnp.asarray(cosine, F32), jnp.asarray(sine, F32)


def rotate_tile(tile, cosine, sine):
    first = lane_index(tile.shape) % HD < HD // 2
    other = jnp.where(
        first, pltpu.roll(tile, LANES - HD // 2, 1), pltpu.roll(tile, HD // 2, 1)
    )
    return tile * cosine + other * sine


SUM_ROWS = 16


def attend_pair(queries, key_tiles, value_tiles, suffix_len, states):
    tok_count = queries[0].shape[0] // 2
    turned = [tile.astype(F32).T.astype(BF16) for tile in value_tiles]
    ones = jnp.ones((SUM_ROWS, turned[0].shape[1]), BF16)
    scores = []
    for half in range(2):
        scores.append([dot_nt(tile, queries[half]) for tile in key_tiles])
        if suffix_len is not None:
            shape = scores[half][0].shape
            slot = lax.broadcasted_iota(jnp.int32, shape, 0)
            row = lane_index(shape) % tok_count
            visible = (slot <= row) & (slot < suffix_len)
            scores[half][0] = jnp.where(visible, scores[half][0], -1e30)
    results = []
    for half in range(2):
        new_max = jnp.max(functools.reduce(jnp.maximum, scores[half]), axis=0, keepdims=True)
        total = None
        if states is not None:
            old_max, old_total = states[half]
            new_max = jnp.maximum(new_max, old_max)
            total = old_total * jnp.exp(old_max - new_max)
        for score, tile in zip(scores[half], turned):
            weights = jnp.exp(score - new_max).astype(BF16)
            part = dot(jnp.concatenate([tile[half * HD : (half + 1) * HD], ones], axis=0), weights)
            total = part if total is None else total + part
        results.append((new_max, total))
    return results


def near_kernel(blocks, *refs):
    tok_ref, gain_ref, wq_ref, wk_ref, wv_ref, cos_ref, sin_ref, lengths_ref, order_ref = refs[:9]
    key_refs, value_refs = refs[9 : 9 + blocks], refs[9 + blocks : 9 + 2 * blocks]
    q_ref, max_ref, acc_ref, normed_ref = refs[9 + 2 * blocks :]
    suffix_len = lengths_ref[0, order_ref[0, lax.axis_index("req")]]

    @pl.when(pl.program_id(0) == 0)
    def _():
        rows = tok_ref[...].astype(F32)
        mean_square = jnp.mean(rows * rows, axis=-1, keepdims=True)
        normed_ref[...] = (rows * lax.rsqrt(mean_square + NORM_EPS) * gain_ref[...]).astype(BF16)

    normed = normed_ref[...]
    tok_count = normed.shape[0]
    cosine, sine = cos_ref[...], sin_ref[...]
    low = lane_index((tok_count, LANES)) < HD
    projected = dot(normed, wq_ref[...])
    suffix_keys = rotate_tile(dot(normed, wk_ref[...]), cosine, sine).astype(BF16)
    suffix_values = dot(normed, wv_ref[...]).astype(BF16)
    queries = []
    for half in range(2):
        tile = rotate_tile(projected[:, half * LANES : (half + 1) * LANES], cosine, sine) * ATTN_SCALE
        turned = pltpu.roll(tile, HD, 1)
        if half == 0:
            first, second = jnp.where(low, tile, 0.0), jnp.where(low, turned, 0.0)
        else:
            first, second = jnp.where(low, 0.0, turned), jnp.where(low, 0.0, tile)
        queries.append(jnp.concatenate([first, second], axis=0).astype(BF16))
        q_ref[half] = queries[half]
    key_tiles = [suffix_keys] + [ref[...] for ref in key_refs]
    value_tiles = [suffix_values] + [ref[...] for ref in value_refs]
    results = attend_pair(queries, key_tiles, value_tiles, suffix_len, None)
    for half, (new_max, total) in enumerate(results):
        max_ref[half] = new_max
        acc_ref[half] = total


def pair_spec(*shape):
    return pl.BlockSpec((2, *shape), lambda i: (i, 0, 0))


def whole_spec(*shape):
    return pl.BlockSpec(shape, lambda i: (0,) * len(shape))


def cached_specs(cached):
    specs = []
    for kind in range(2):
        for array in cached:
            stacked = not isinstance(array, tuple)
            length = array.shape[0] // 2 if stacked else array[0].shape[0]
            place = kind if stacked else 0
            specs.append(pl.BlockSpec((length, LANES), lambda i, place=place: (place, i)))
    return specs


def cached_args(cached):
    return [array[kind] if isinstance(array, tuple) else array for kind in range(2) for array in cached]


def attend_near(own_rows, attn_gain, w_query, w_key, w_value, prefix_len, lengths, assignment, keys, values, mate):
    tok_count, width = own_rows.shape
    cached = [(keys, values), mate]
    rows, blocks = 2 * tok_count, len(cached)
    cosine, sine = rope_tables(prefix_len, tok_count)
    column = lambda i: (0, i)
    queries, *state = pl.pallas_call(
        functools.partial(near_kernel, blocks),
        grid=(KV // 2,),
        in_specs=[
            whole_spec(tok_count, width),
            whole_spec(1, width),
            pl.BlockSpec((width, 2 * LANES), column),
            pl.BlockSpec((width, LANES), column),
            pl.BlockSpec((width, LANES), column),
            whole_spec(tok_count, LANES),
            whole_spec(tok_count, LANES),
            pl.BlockSpec(memory_space=pltpu.SMEM),
            pl.BlockSpec(memory_space=pltpu.SMEM),
        ]
        + cached_specs(cached),
        out_specs=[pair_spec(rows, LANES), pair_spec(1, rows), pair_spec(HD + SUM_ROWS, rows)],
        out_shape=[
            pltpu.VMEM((KV, rows, LANES), BF16),
            pltpu.VMEM((KV, 1, rows), F32),
            pltpu.VMEM((KV, HD + SUM_ROWS, rows), F32),
        ],
        scratch_shapes=[pltpu.VMEM((tok_count, width), BF16)],
        compiler_params=pltpu.CompilerParams(vmem_limit_bytes=VMEM_ATTEND * MIB),
        cost_estimate=pl.CostEstimate(flops=4000 * MIB, bytes_accessed=6 * MIB, transcendentals=0),
        name="attend_near",
    )(
        *held_in_hbm([own_rows, attn_gain.reshape(1, width), w_query, w_key, w_value, cosine, sine]),
        *held_in_hbm([lengths, assignment, keys]),
        held_in_vmem([mate])[0],
        *held_in_hbm([values]),
        held_in_vmem([mate])[0],
    )
    return queries, state


def far_kernel(blocks, last, *refs):
    q_ref, max_in, acc_in = refs[:3]
    key_refs, value_refs = refs[3 : 3 + blocks], refs[3 + blocks : 3 + 2 * blocks]
    refs = refs[3 + 2 * blocks :]
    states = [(max_in[half], acc_in[half]) for half in range(2)]
    key_tiles = [ref[...] for ref in key_refs]
    value_tiles = [ref[...] for ref in value_refs]
    results = attend_pair([q_ref[0], q_ref[1]], key_tiles, value_tiles, None, states)
    if not last:
        max_ref, acc_ref = refs
        for half, (new_max, total) in enumerate(results):
            max_ref[half] = new_max
            acc_ref[half] = total
        return
    tok_ref, w_out_ref, gain_ref, ids_ref, route_ref, ctx_ref, hidden_ref, moe_ref, projected_ref = refs
    tok_count = tok_ref.shape[0]
    step = pl.program_id(0)
    tiles = []
    for _, total in results:
        mixed = total[:HD] / total[HD : HD + 1]
        tiles.append(jnp.concatenate([mixed[:, :tok_count], mixed[:, tok_count:]], axis=0).T)
    context = jnp.concatenate(tiles, axis=1).astype(BF16)
    ctx_ref[...] = context
    part = dot(context, w_out_ref[...])

    @pl.when(step == 0)
    def _():
        projected_ref[...] = part

    @pl.when(step > 0)
    def _():
        projected_ref[...] += part

    @pl.when(step == pl.num_programs(0) - 1)
    def _():
        hidden = (tok_ref[...].astype(F32) + RESIDUAL_SCALE * projected_ref[...]).astype(BF16)
        hidden_ref[...] = hidden
        wide = hidden.astype(F32)
        mean_square = jnp.mean(wide * wide, axis=-1, keepdims=True)
        moe_ref[:tok_count] = (wide * lax.rsqrt(mean_square + NORM_EPS) * gain_ref[...]).astype(BF16)
        moe_ref[tok_count:] = jnp.zeros((NOTE_ROWS, wide.shape[1]), BF16)
        moe_ref[tok_count : tok_count + TOP, :tok_count] = ids_ref[...].astype(F32).astype(BF16)
        moe_ref[tok_count : tok_count + TOP, tok_count : 2 * tok_count] = route_ref[...].astype(BF16)


def attend_far(queries, state, cached, final=None):
    last, blocks, rows = final is not None, len(cached), queries.shape[1]
    tok_count = rows // 2
    args, tiles = [queries, *state], held_in_vmem(cached_args(cached))
    in_specs = [pair_spec(rows, LANES), pair_spec(1, rows), pair_spec(HD + SUM_ROWS, rows)]
    in_specs += cached_specs(cached)
    if last:
        own_rows, w_out, moe_gain, expert_ids, route_weights = final
        width = own_rows.shape[1]
        own_args = [own_rows, w_out, moe_gain.reshape(1, width), expert_ids.T, route_weights.T]
        whole = whole_spec(tok_count, width)
        in_specs += [whole, pl.BlockSpec((2 * LANES, width), lambda i: (i, 0)), whole_spec(1, width)]
        in_specs += [whole_spec(TOP, tok_count)] * 2
        out_specs = [pl.BlockSpec((tok_count, 2 * LANES), lambda i: (0, i)), whole, whole_spec(tok_count + NOTE_ROWS, width)]
        out_shape = [pltpu.HBM((tok_count, width), BF16)] * 2 + [pltpu.VMEM((tok_count + NOTE_ROWS, width), BF16)]
        scratch = [pltpu.VMEM((tok_count, width), F32)]
    else:
        own_args = []
        out_specs = in_specs[1:3]
        out_shape = [pltpu.VMEM(array.shape, F32) for array in state]
        scratch = []
    return pl.pallas_call(
        functools.partial(far_kernel, blocks, last),
        grid=(KV // 2,),
        in_specs=in_specs,
        out_specs=out_specs,
        out_shape=out_shape,
        scratch_shapes=scratch,
        compiler_params=pltpu.CompilerParams(vmem_limit_bytes=VMEM_ATTEND * MIB),
        cost_estimate=pl.CostEstimate(flops=blocks * 1200 * MIB, bytes_accessed=4 * MIB, transcendentals=0),
        name="attend_far",
    )(*held_in_vmem(args), *tiles, *held_in_hbm(own_args))


def experts_kernel(sources, pieces, *refs):
    refs = list(refs)
    take = lambda n: [refs.pop(0) for _ in range(n)]
    row_refs = [take(pieces) for _ in range(sources)]
    weight_refs = [take(2) for _ in range(3)]
    out_refs = take(sources)
    picked_ref, made_ref, combine_ref, *held, sem = refs
    local_experts = weight_refs[0][0].shape[0]
    chip_experts = 2 * local_experts
    tok_count, width = out_refs[0].shape
    slots = chip_experts * CAP
    me = lax.axis_index("req")
    first_own, first_mate = me * local_experts, (me + 1 - 2 * lax.rem(me, 2)) * local_experts

    def copy(kind, owner, e, expert):
        return pltpu.make_async_copy(
            weight_refs[kind][owner].at[e], held[kind].at[expert], sem.at[kind, expert]
        )

    for expert in range(chip_experts):
        for kind in range(3):
            copy(kind, expert // local_experts, expert % local_experts, expert).start()

    before = lax.broadcasted_iota(jnp.int32, (tok_count, tok_count), 0)
    after = lane_index((tok_count, tok_count))
    earlier = jnp.where(before < after, 1.0, 0.0).astype(BF16)
    slot = lax.broadcasted_iota(jnp.int32, (slots, EXPERTS), 0) // CAP
    held_here = jnp.where(slot < local_experts, slot + first_own, slot + (first_mate - local_experts))
    spread = jnp.where(held_here == lane_index((slots, EXPERTS)), 1.0, 0.0).astype(BF16)
    within = (lax.broadcasted_iota(jnp.int32, (slots, tok_count), 0) % CAP).astype(F32)
    expert_row = lax.broadcasted_iota(jnp.int32, (EXPERTS, tok_count), 0).astype(F32)
    for source in range(sources):
        message = jnp.concatenate([ref[...] for ref in row_refs[source]], axis=0)
        rows, note = message[:tok_count], message[tok_count:].astype(F32)
        route = jnp.zeros((EXPERTS, tok_count), F32)
        for k in range(TOP):
            chosen, gain = note[k : k + 1, :tok_count], note[k : k + 1, tok_count : 2 * tok_count]
            route = jnp.where(chosen == expert_row, gain, route)
        hit = route > 0.0
        ranked = dot(jnp.where(hit, 1.0, 0.0).astype(BF16), earlier)
        ranked = jnp.where(hit, ranked, -1.0).astype(BF16)
        match = dot(spread, ranked) == within
        pick = jnp.where(match, 1.0, 0.0).astype(BF16)
        combine_ref[source] = jnp.where(match, dot(spread, route.astype(BF16)), 0.0).astype(BF16)
        picked = dot(pick, rows).astype(BF16)
        for e in range(chip_experts):
            picked_ref[e, source] = picked[e * CAP : (e + 1) * CAP]

    def one_expert(expert, carry):
        for kind in range(3):
            copy(kind, 0, 0, expert).wait()
        rows = picked_ref[expert].reshape(sources * CAP, width)
        gate = dot(rows, held[0][expert])
        up = dot(rows, held[1][expert])
        act = (jax.nn.silu(gate) * up).astype(BF16)
        made = dot(act, held[2][expert]).astype(BF16)
        for source in range(sources):
            made_ref[source, pl.ds(pl.multiple_of(expert * CAP, CAP), CAP), :] = made[
                source * CAP : (source + 1) * CAP
            ]
        return carry

    lax.fori_loop(0, chip_experts, one_expert, 0)
    for source, ref in enumerate(out_refs):
        ref[...] = dot_tn(combine_ref[source], made_ref[source]).astype(ref.dtype)


def run_experts(rows, weights, out_type=BF16):
    sources, pieces = len(rows), len(rows[0])
    tok_count, width = sum(piece.shape[0] for piece in rows[0]) - NOTE_ROWS, rows[0][0].shape[1]
    chip_experts = 2 * weights[0][0].shape[0]
    hidden = weights[0][0].shape[2]
    vmem = pl.BlockSpec(memory_space=pltpu.VMEM)
    return pl.pallas_call(
        functools.partial(experts_kernel, sources, pieces),
        in_specs=[vmem] * (pieces * sources) + [pl.BlockSpec(memory_space=pl.ANY)] * 6,
        out_specs=[vmem] * sources,
        out_shape=[pltpu.VMEM((tok_count, width), out_type)] * sources,
        scratch_shapes=[
            pltpu.VMEM((chip_experts, sources, CAP, width), BF16),
            pltpu.VMEM((sources, chip_experts * CAP, width), BF16),
            pltpu.VMEM((sources, chip_experts * CAP, tok_count), BF16),
            pltpu.VMEM((chip_experts, width, hidden), BF16),
            pltpu.VMEM((chip_experts, width, hidden), BF16),
            pltpu.VMEM((chip_experts, hidden, width), BF16),
            pltpu.SemaphoreType.DMA((3, chip_experts)),
        ],
        compiler_params=pltpu.CompilerParams(vmem_limit_bytes=VMEM_EXPERTS * MIB),
        cost_estimate=pl.CostEstimate(flops=12000 * MIB, bytes_accessed=30 * MIB, transcendentals=0),
        name="experts",
    )(
        *held_in_vmem([piece for source in rows for piece in source]),
        *[array for pair in weights for array in pair],
    )


CORE, ACROSS_X, ACROSS_Y = 1, 2, 4


def swap(array, mask):
    return lax.ppermute(array, "req", [(i, i ^ mask) for i in range(lax.axis_size("req"))])


def ordered(*arrays):
    return lax.optimization_barrier(arrays)


def local_chips(
    tokens,
    attn_gain,
    w_query,
    w_key,
    w_value,
    w_out,
    prefix_keys,
    prefix_values,
    lengths,
    assignment,
    moe_gain,
    expert_ids,
    route_weights,
    w_gate,
    w_up,
    w_down,
):
    peer_count = lax.axis_size("req")
    own_rows = tokens[0]
    tok_count = own_rows.shape[0]
    prefix_len = prefix_keys.shape[1] * peer_count
    keys, values = prefix_keys[0], prefix_values[0]
    block = keys.shape[0]
    cached = jnp.concatenate([keys, values], axis=0)
    cached_x, cached_y = swap(cached, ACROSS_X), swap(cached, ACROSS_Y)
    cached_mate = swap(cached, CORE)

    queries, state = attend_near(
        own_rows, attn_gain, w_query, w_key, w_value, prefix_len, lengths, assignment, keys, values, cached_mate
    )
    cached_x, cached_y, *state = ordered(cached_x, cached_y, *state)
    far = [swap(cached_x[:block], ACROSS_Y), swap(cached_y[block:], ACROSS_X)]
    mates = [swap(cached_x, CORE), swap(cached_y, CORE)]
    *mates, w_gate = ordered(*mates, w_gate)
    gate = (w_gate, swap(w_gate, CORE))
    state = attend_far(queries, state, [cached_x, cached_y, *mates])
    *far, gate, s0, s1 = ordered(*far, gate, *state)
    far_mate = [swap(array, CORE) for array in far]
    *far_mate, w_up, w_down = ordered(*far_mate, w_up, w_down)
    up, down = (w_up, swap(w_up, CORE)), (w_down, swap(w_down, CORE))
    context, hidden, moe_in = attend_far(
        queries,
        [s0, s1],
        [tuple(far), tuple(far_mate)],
        final=(own_rows, w_out, moe_gain, expert_ids[0], route_weights[0]),
    )

    weights = (gate, up, down)
    half = tok_count // 2
    rows_x, rows_y = swap(moe_in, ACROSS_X), swap(moe_in, ACROSS_Y)
    (own,) = run_experts([[moe_in]], weights, F32)
    rows_x, rows_y, own = ordered(rows_x, rows_y, own)
    low_xy, high_xy = swap(rows_x[:half], ACROSS_Y), swap(rows_y[half:], ACROSS_X)
    to_x, to_y = run_experts([[rows_x], [rows_y]], weights)
    low_xy, high_xy, to_x, to_y = ordered(low_xy, high_xy, to_x, to_y)
    from_x, from_y = swap(to_x, ACROSS_X), swap(to_y, ACROSS_Y)
    (to_xy,) = run_experts([[low_xy, high_xy]], weights)
    from_xy = swap(to_xy, ACROSS_X | ACROSS_Y)
    partial, from_xy = ordered(own + from_x.astype(F32) + from_y.astype(F32), from_xy)
    expert_mix = (partial + from_xy.astype(F32)).astype(BF16)
    return (context[None], hidden[None], expert_mix[None])


def solution(mesh):
    placed = (
        P("grp", "req", None),
        P(),
        P(),
        P(),
        P(),
        P(),
        P("grp", "req", None),
        P("grp", "req", None),
        P("grp", None),
        P("grp", None),
        P(),
        P("grp", "req", None),
        P("grp", "req", None),
        P("req", None, None),
        P("req", None, None),
        P("req", None, None),
    )
    return jax.shard_map(
        local_chips if mesh.shape["req"] == 8 else local_general,
        mesh=mesh,
        in_specs=placed,
        out_specs=(P("grp", "req", None), P("grp", "req", None), P("grp", "req", None)),
        check_vma=False,
    )
```

```python
import functools
import math

import jax
import jax.numpy as jnp
import numpy as np
from jax import lax
from jax.experimental import pallas as pl
from jax.experimental.pallas import tpu as pltpu
from jax.sharding import PartitionSpec as P

H = 16
KV = 8
HD = 64
EXPERTS = 32
TOP = 8
CAP = 96


NORM_EPS = 1e-06
ATTN_SCALE = 0.015625
RESIDUAL_SCALE = 0.22
ROPE_BASE = 10000.0


def normalize(head_rows, gain):
    widened = head_rows.astype(jnp.float32)
    mean_square = jnp.mean(widened * widened, axis=-1, keepdims=True)
    return (widened * lax.rsqrt(mean_square + NORM_EPS) * gain).astype(jnp.bfloat16)


def rotate(head_rows, positions):
    half_dim = head_rows.shape[-1] // 2
    frequency = ROPE_BASE ** (
        -(jnp.arange(half_dim, dtype=jnp.float32) * 2.0 / head_rows.shape[-1])
    )
    angles = positions[:, None] * frequency[None, :]
    cosine = jnp.cos(angles)[:, None, :]
    sine_part = jnp.sin(angles)[:, None, :]
    first_half = head_rows[..., :half_dim]
    second_half = head_rows[..., half_dim:]
    return jnp.concatenate(
        [
            first_half * cosine - second_half * sine_part,
            second_half * cosine + first_half * sine_part,
        ],
        axis=-1,
    )


def fresh_state(tok_count):
    return (
        jnp.full((KV, H // KV, tok_count), -jnp.inf, jnp.float32),
        jnp.zeros((KV, H // KV, tok_count), jnp.float32),
        jnp.zeros((KV, H // KV, tok_count, HD), jnp.float32),
    )


def absorb(run_state, grouped, key_rows, value_rows, visible):
    run_max, run_sum, run_acc = run_state
    scores = (
        jnp.einsum("tkgd,skd->kgts", grouped, key_rows, preferred_element_type=jnp.float32)
        * ATTN_SCALE
    )
    scores = jnp.where(visible, scores, -jnp.inf)
    new_max = jnp.maximum(run_max, jnp.max(scores, axis=-1))
    factor = jnp.exp(run_max - new_max)
    weights = jnp.exp(scores - new_max[..., None])
    run_sum = run_sum * factor + jnp.sum(weights, axis=-1)
    gathered_values = jnp.einsum(
        "kgts,skd->kgtd",
        weights.astype(jnp.bfloat16),
        value_rows,
        preferred_element_type=jnp.float32,
    )
    run_acc = run_acc * factor[..., None] + gathered_values
    return (new_max, run_sum, run_acc)


def slot_numbers(ids):
    chosen = ids.reshape(-1)
    hit_table = (chosen[:, None] == jnp.arange(EXPERTS, dtype=jnp.int32)[None, :]).astype(jnp.int32)
    before = jnp.cumsum(hit_table, axis=0) - hit_table
    ranked = jnp.sum(before * hit_table, axis=1)
    return (chosen, ranked)


def local_general(
    tokens,
    attn_gain,
    w_query,
    w_key,
    w_value,
    w_out,
    prefix_keys,
    prefix_values,
    lengths,
    assignment,
    moe_gain,
    expert_ids,
    route_weights,
    w_gate,
    w_up,
    w_down,
):
    tok_count = tokens.shape[1]
    model_width = tokens.shape[2]
    peer_count = lax.axis_size("req")
    prefix_len = prefix_keys.shape[1] * peer_count
    own_rows = tokens[0]
    normed = normalize(own_rows, attn_gain)
    my_index = lax.axis_index("req")
    request_ids = jnp.arange(lengths.shape[1], dtype=jnp.int32)
    request = jnp.sum(jnp.where(request_ids == my_index, assignment[0], 0))
    suffix_len = jnp.sum(jnp.where(request_ids == request, lengths[0], 0))
    positions = (prefix_len + jnp.arange(tok_count, dtype=jnp.int32)).astype(jnp.float32)
    queries = jnp.dot(normed, w_query, preferred_element_type=jnp.float32).reshape(tok_count, H, HD)
    queries = rotate(queries, positions).astype(jnp.bfloat16)
    suffix_keys = jnp.dot(normed, w_key, preferred_element_type=jnp.float32).reshape(
        tok_count, KV, HD
    )
    suffix_keys = rotate(suffix_keys, positions).astype(jnp.bfloat16)
    suffix_values = (
        jnp.dot(normed, w_value, preferred_element_type=jnp.float32)
        .astype(jnp.bfloat16)
        .reshape(tok_count, KV, HD)
    )
    grouped = queries.reshape(tok_count, KV, H // KV, HD)
    slot_row = jnp.arange(tok_count, dtype=jnp.int32)
    suffix_visible = (slot_row[None, :] <= slot_row[:, None]) & (slot_row[None, :] < suffix_len)
    suffix_state = absorb(
        fresh_state(tok_count), grouped, suffix_keys, suffix_values, suffix_visible[None, None]
    )
    run_state = suffix_state
    key_piece = lax.all_gather(prefix_keys, "req", axis=1, tiled=True)
    value_piece = lax.all_gather(prefix_values, "req", axis=1, tiled=True)
    piece_len = key_piece.shape[1]
    key_block = math.gcd(piece_len, 512)
    key_blocks = key_piece[0].reshape(piece_len // key_block, key_block, KV, HD)
    value_blocks = value_piece[0].reshape(piece_len // key_block, key_block, KV, HD)

    def absorb_step(carry, pair_set):
        return (absorb(carry, grouped, pair_set[0], pair_set[1], True), None)

    run_state, unused = lax.scan(absorb_step, run_state, (key_blocks, value_blocks))
    run_max, run_sum, run_acc = run_state
    context = (
        (run_acc / run_sum[..., None])
        .transpose(2, 0, 1, 3)
        .reshape(tok_count, H * HD)
        .astype(jnp.bfloat16)
    )
    projected = jnp.dot(context, w_out, preferred_element_type=jnp.float32)
    hidden = (own_rows.astype(jnp.float32) + RESIDUAL_SCALE * projected).astype(jnp.bfloat16)
    moe_in = normalize(hidden, moe_gain)
    chosen, ranked = slot_numbers(expert_ids[0])
    slot_index = chosen * CAP + ranked
    sources = jnp.repeat(moe_in, TOP, axis=0)
    outgoing = jnp.zeros((EXPERTS * CAP, model_width), jnp.bfloat16).at[slot_index].set(sources)
    outgoing = outgoing.reshape(peer_count, EXPERTS // peer_count, CAP, model_width)
    arrived = lax.all_to_all(outgoing, "req", split_axis=0, concat_axis=0, tiled=True)
    slot_span = arrived.shape[2]
    results = []
    for expert_local in range(arrived.shape[1]):
        expert_rows = arrived[:, expert_local].reshape(-1, model_width)
        gate_act = jnp.dot(expert_rows, w_gate[expert_local], preferred_element_type=jnp.float32)
        up_act = jnp.dot(expert_rows, w_up[expert_local], preferred_element_type=jnp.float32)
        product = (jax.nn.silu(gate_act) * up_act).astype(jnp.bfloat16)
        expert_out = jnp.dot(
            product, w_down[expert_local], preferred_element_type=jnp.float32
        ).astype(jnp.bfloat16)
        results.append(expert_out.reshape(arrived.shape[0], slot_span, model_width))
    produced = jnp.stack(results, axis=1)
    returned = lax.all_to_all(produced, "req", split_axis=0, concat_axis=0, tiled=True).reshape(
        EXPERTS * CAP, model_width
    )
    picked = returned[slot_index].astype(jnp.float32).reshape(tok_count, TOP, model_width)
    expert_mix = jnp.sum(picked * route_weights[0][..., None], axis=1).astype(jnp.bfloat16)
    return (context[None], hidden[None], expert_mix[None])


F32 = jnp.float32
BF16 = jnp.bfloat16
MIB = 1 << 20
LANES = 128
VMEM_ATTEND = 48
NOTE_ROWS = 16
VMEM_EXPERTS = 30


def dot(lhs, rhs):
    return jnp.dot(lhs, rhs, preferred_element_type=F32)


def dot_nt(lhs, rhs):
    return lax.dot_general(lhs, rhs, (((1,), (1,)), ((), ())), preferred_element_type=F32)


def dot_tn(lhs, rhs):
    return lax.dot_general(lhs, rhs, (((0,), (0,)), ((), ())), preferred_element_type=F32)


def held_in_hbm(arrays):
    return [pltpu.with_memory_space_constraint(array, pltpu.HBM) for array in arrays]


def held_in_vmem(arrays):
    return [pltpu.with_memory_space_constraint(array, pltpu.VMEM) for array in arrays]


def lane_index(shape):
    return lax.broadcasted_iota(jnp.int32, shape, len(shape) - 1)


def rope_tables(prefix_len, tok_count):
    frequency = ROPE_BASE ** (-(np.arange(HD // 2, dtype=np.float64) * 2.0 / HD))
    angles = (prefix_len + np.arange(tok_count, dtype=np.float64))[:, None] * frequency[None, :]
    cosine, sine = np.cos(angles), np.sin(angles)
    cosine = np.concatenate([cosine, cosine, cosine, cosine], axis=1)
    sine = np.concatenate([-sine, sine, -sine, sine], axis=1)
    return jnp.asarray(cosine, F32), jnp.asarray(sine, F32)


def rotate_tile(tile, cosine, sine):
    first = lane_index(tile.shape) % HD < HD // 2
    other = jnp.where(
        first, pltpu.roll(tile, LANES - HD // 2, 1), pltpu.roll(tile, HD // 2, 1)
    )
    return tile * cosine + other * sine


SUM_ROWS = 16


def attend_heads(queries, key_tiles, value_tiles, suffix_len, states):
    heads = len(queries)
    tok_count = queries[0].shape[0] // 2
    turned = [[tile.astype(F32).T.astype(BF16) for tile in tiles] for tiles in value_tiles]
    ones = jnp.ones((SUM_ROWS, turned[0][0].shape[1]), BF16)

    def scores_of(head):
        scores = [dot_nt(tile, queries[head]) for tile in key_tiles[head // 2]]
        if suffix_len is not None:
            shape = scores[0].shape
            slot = lax.broadcasted_iota(jnp.int32, shape, 0)
            row = lane_index(shape) % tok_count
            visible = (slot <= row) & (slot < suffix_len)
            scores[0] = jnp.where(visible, scores[0], -1e30)
        return scores

    results = []
    ahead = scores_of(0)
    for head in range(heads):
        scores, ahead = ahead, scores_of(head + 1) if head + 1 < heads else None
        new_max = jnp.max(functools.reduce(jnp.maximum, scores), axis=0, keepdims=True)
        total = None
        if states is not None:
            old_max, old_total = states[head]
            new_max = jnp.maximum(new_max, old_max)
            total = old_total * jnp.exp(old_max - new_max)
        first_row = head % 2 * HD
        for score, tile in zip(scores, turned[head // 2]):
            weights = jnp.exp(score - new_max).astype(BF16)
            part = dot(jnp.concatenate([tile[first_row : first_row + HD], ones], axis=0), weights)
            total = part if total is None else total + part
        results.append((new_max, total))
    return results


def pair_tiles(refs):
    pairs = refs[0].shape[1] // LANES
    return [[ref[:, pair * LANES : (pair + 1) * LANES] for ref in refs] for pair in range(pairs)]


def near_kernel(*refs):
    tok_ref, gain_ref, *held = refs[:5]
    cos_ref, sin_ref, lengths_ref, order_ref, keys_ref, values_ref, mate_keys_ref, mate_values_ref = refs[5:13]
    q_ref, max_ref, acc_ref = refs[13:]
    suffix_len = lengths_ref[0, order_ref[0, lax.axis_index("req")]]
    rows = tok_ref[...].astype(F32)
    mean_square = jnp.mean(rows * rows, axis=-1, keepdims=True)
    normed = (rows * lax.rsqrt(mean_square + NORM_EPS) * gain_ref[...]).astype(BF16)
    cosine, sine = cos_ref[...], sin_ref[...]
    low = lane_index(cosine.shape) < HD
    queries, key_tiles, value_tiles = [], [], []
    for pair in range(KV // 2):
        lanes = slice(pair * LANES, (pair + 1) * LANES)
        suffix_keys = rotate_tile(dot(normed, held[1][:, lanes]), cosine, sine).astype(BF16)
        suffix_values = dot(normed, held[2][:, lanes]).astype(BF16)
        key_tiles.append([suffix_keys, keys_ref[:, lanes], mate_keys_ref[:, lanes]])
        value_tiles.append([suffix_values, values_ref[:, lanes], mate_values_ref[:, lanes]])
        projected = dot(normed, held[0][:, 2 * pair * LANES : 2 * (pair + 1) * LANES])
        for half in range(2):
            tile = rotate_tile(projected[:, half * LANES : (half + 1) * LANES], cosine, sine) * ATTN_SCALE
            turned = pltpu.roll(tile, HD, 1)
            if half == 0:
                first, second = jnp.where(low, tile, 0.0), jnp.where(low, turned, 0.0)
            else:
                first, second = jnp.where(low, 0.0, turned), jnp.where(low, 0.0, tile)
            queries.append(jnp.concatenate([first, second], axis=0).astype(BF16))
            q_ref[2 * pair + half] = queries[-1]
    results = attend_heads(queries, key_tiles, value_tiles, suffix_len, None)
    for head, (new_max, total) in enumerate(results):
        max_ref[head] = new_max
        acc_ref[head] = total


def whole_spec(*shape):
    return pl.BlockSpec(shape, lambda i: (0,) * len(shape))


def cached_specs(cached):
    specs = []
    for kind in range(2):
        for array in cached:
            stacked = not isinstance(array, tuple)
            length = array.shape[0] // 2 if stacked else array[0].shape[0]
            place = kind if stacked else 0
            specs.append(pl.BlockSpec((length, KV * HD), lambda i, place=place: (place, 0)))
    return specs


def cached_args(cached):
    return [array[kind] if isinstance(array, tuple) else array for kind in range(2) for array in cached]


def attend_near(own_rows, attn_gain, w_query, w_key, w_value, prefix_len, lengths, assignment, keys, values, mate):
    tok_count, width = own_rows.shape
    rows, block = 2 * tok_count, keys.shape[0]
    cosine, sine = rope_tables(prefix_len, tok_count)
    smem = pl.BlockSpec(memory_space=pltpu.SMEM)
    mate_specs = [pl.BlockSpec((block, KV * HD), lambda i, kind=kind: (kind, 0)) for kind in range(2)]
    queries, *state = pl.pallas_call(
        near_kernel,
        grid=(1,),
        in_specs=[whole_spec(tok_count, width), whole_spec(1, width)]
        + [whole_spec(*array.shape) for array in (w_query, w_key, w_value)]
        + [whole_spec(tok_count, LANES)] * 2
        + [smem, smem]
        + [whole_spec(block, KV * HD)] * 2
        + mate_specs,
        out_specs=[whole_spec(KV, rows, LANES), whole_spec(KV, 1, rows), whole_spec(KV, HD + SUM_ROWS, rows)],
        out_shape=[
            pltpu.VMEM((KV, rows, LANES), BF16),
            pltpu.VMEM((KV, 1, rows), F32),
            pltpu.VMEM((KV, HD + SUM_ROWS, rows), F32),
        ],
        compiler_params=pltpu.CompilerParams(vmem_limit_bytes=VMEM_ATTEND * MIB),
        cost_estimate=pl.CostEstimate(flops=4000 * MIB, bytes_accessed=6 * MIB, transcendentals=0),
        name="attend_near",
    )(
        *held_in_hbm([own_rows, attn_gain.reshape(1, width), w_query, w_key, w_value, cosine, sine]),
        *held_in_hbm([lengths, assignment, keys, values]),
        *held_in_vmem([mate, mate]),
    )
    return queries, state


def far_kernel(blocks, last, *refs):
    q_ref, max_in, acc_in = refs[:3]
    key_refs, value_refs = refs[3 : 3 + blocks], refs[3 + blocks : 3 + 2 * blocks]
    refs = refs[3 + 2 * blocks :]
    heads = q_ref.shape[0]
    states = [(max_in[head], acc_in[head]) for head in range(heads)]
    queries = [q_ref[head] for head in range(heads)]
    results = attend_heads(queries, pair_tiles(key_refs), pair_tiles(value_refs), None, states)
    if not last:
        max_ref, acc_ref = refs
        for half, (new_max, total) in enumerate(results):
            max_ref[half] = new_max
            acc_ref[half] = total
        return
    tok_ref, w_out_ref, gain_ref, ids_ref, route_ref, ctx_ref, hidden_ref, moe_ref = refs
    tok_count = tok_ref.shape[0]
    tiles = []
    for _, total in results:
        mixed = total[:HD] / total[HD : HD + 1]
        tiles.append(jnp.concatenate([mixed[:, :tok_count], mixed[:, tok_count:]], axis=0).T)
    context = jnp.concatenate(tiles, axis=1).astype(BF16)
    ctx_ref[...] = context
    projected = dot(context, w_out_ref[...])
    hidden = (tok_ref[...].astype(F32) + RESIDUAL_SCALE * projected).astype(BF16)
    hidden_ref[...] = hidden
    wide = hidden.astype(F32)
    mean_square = jnp.mean(wide * wide, axis=-1, keepdims=True)
    moe_ref[:tok_count] = (wide * lax.rsqrt(mean_square + NORM_EPS) * gain_ref[...]).astype(BF16)
    moe_ref[tok_count:] = jnp.zeros((NOTE_ROWS, wide.shape[1]), BF16)
    moe_ref[tok_count : tok_count + TOP, :tok_count] = ids_ref[...].astype(F32).astype(BF16)
    moe_ref[tok_count : tok_count + TOP, tok_count : 2 * tok_count] = route_ref[...].astype(BF16)


def attend_far(queries, state, cached, final=None):
    last, blocks, rows = final is not None, len(cached), queries.shape[1]
    tok_count = rows // 2
    args, tiles = [queries, *state], held_in_vmem(cached_args(cached))
    in_specs = [whole_spec(KV, rows, LANES), whole_spec(KV, 1, rows), whole_spec(KV, HD + SUM_ROWS, rows)]
    in_specs += cached_specs(cached)
    if last:
        own_rows, w_out, moe_gain, expert_ids, route_weights = final
        width = own_rows.shape[1]
        own_args = [own_rows, w_out, moe_gain.reshape(1, width), expert_ids.T, route_weights.T]
        whole = whole_spec(tok_count, width)
        in_specs += [whole, whole_spec(*w_out.shape), whole_spec(1, width)]
        in_specs += [whole_spec(TOP, tok_count)] * 2
        out_specs = [whole, whole, whole_spec(tok_count + NOTE_ROWS, width)]
        out_shape = [pltpu.HBM((tok_count, width), BF16)] * 2 + [pltpu.VMEM((tok_count + NOTE_ROWS, width), BF16)]
    else:
        own_args = []
        out_specs = in_specs[1:3]
        out_shape = [pltpu.VMEM(array.shape, F32) for array in state]
    return pl.pallas_call(
        functools.partial(far_kernel, blocks, last),
        grid=(1,),
        in_specs=in_specs,
        out_specs=out_specs,
        out_shape=out_shape,
        compiler_params=pltpu.CompilerParams(vmem_limit_bytes=VMEM_ATTEND * MIB),
        cost_estimate=pl.CostEstimate(flops=blocks * 1200 * MIB, bytes_accessed=4 * MIB, transcendentals=0),
        name="attend_far",
    )(*held_in_vmem(args), *tiles, *held_in_hbm(own_args))


def experts_kernel(sources, pieces, load, *refs):
    refs = list(refs)
    take = lambda n: [refs.pop(0) for _ in range(n)]
    row_refs = [take(pieces) for _ in range(sources)]
    weight_refs = [take(2) for _ in range(3)] if load else None
    held = None if load else take(3)
    out_refs = take(sources)
    held = take(3) if load else held
    picked_ref, made_ref, combine_ref, *sems = refs
    chip_experts = held[0].shape[0]
    local_experts = chip_experts // 2
    tok_count, width = out_refs[0].shape
    slots = chip_experts * CAP
    me = lax.axis_index("req")
    first_own, first_mate = me * local_experts, (me + 1 - 2 * lax.rem(me, 2)) * local_experts

    def copy(kind, owner, e, expert):
        return pltpu.make_async_copy(
            weight_refs[kind][owner].at[e], held[kind].at[expert], sems[0].at[kind, expert]
        )

    for expert in range(chip_experts if load else 0):
        for kind in range(3):
            copy(kind, expert // local_experts, expert % local_experts, expert).start()

    before = lax.broadcasted_iota(jnp.int32, (tok_count, tok_count), 0)
    after = lane_index((tok_count, tok_count))
    earlier = jnp.where(before < after, 1.0, 0.0).astype(BF16)
    slot = lax.broadcasted_iota(jnp.int32, (slots, EXPERTS), 0) // CAP
    held_here = jnp.where(slot < local_experts, slot + first_own, slot + (first_mate - local_experts))
    spread = jnp.where(held_here == lane_index((slots, EXPERTS)), 1.0, 0.0).astype(BF16)
    within = (lax.broadcasted_iota(jnp.int32, (slots, tok_count), 0) % CAP).astype(F32)
    expert_row = lax.broadcasted_iota(jnp.int32, (EXPERTS, tok_count), 0).astype(F32)
    for source in range(sources):
        message = jnp.concatenate([ref[...] for ref in row_refs[source]], axis=0)
        rows, note = message[:tok_count], message[tok_count:].astype(F32)
        route = jnp.zeros((EXPERTS, tok_count), F32)
        for k in range(TOP):
            chosen, gain = note[k : k + 1, :tok_count], note[k : k + 1, tok_count : 2 * tok_count]
            route = jnp.where(chosen == expert_row, gain, route)
        hit = route > 0.0
        ranked = dot(jnp.where(hit, 1.0, 0.0).astype(BF16), earlier)
        ranked = jnp.where(hit, ranked, -1.0).astype(BF16)
        match = dot(spread, ranked) == within
        pick = jnp.where(match, 1.0, 0.0).astype(BF16)
        combine_ref[source] = jnp.where(match, dot(spread, route.astype(BF16)), 0.0).astype(BF16)
        picked = dot(pick, rows).astype(BF16)
        for e in range(chip_experts):
            picked_ref[e, source] = picked[e * CAP : (e + 1) * CAP]

    def one_expert(expert, carry):
        for kind in range(3 if load else 0):
            copy(kind, 0, 0, expert).wait()
        rows = picked_ref[expert].reshape(sources * CAP, width)
        gate = dot(rows, held[0][expert])
        up = dot(rows, held[1][expert])
        act = (jax.nn.silu(gate) * up).astype(BF16)
        made = dot(act, held[2][expert]).astype(BF16)
        for source in range(sources):
            made_ref[source, pl.ds(pl.multiple_of(expert * CAP, CAP), CAP), :] = made[
                source * CAP : (source + 1) * CAP
            ]
        return carry

    lax.fori_loop(0, chip_experts, one_expert, 0)
    for source, ref in enumerate(out_refs):
        ref[...] = dot_tn(combine_ref[source], made_ref[source]).astype(ref.dtype)


def run_experts(rows, weights, load=False, out_type=BF16):
    sources, pieces = len(rows), len(rows[0])
    tok_count, width = sum(piece.shape[0] for piece in rows[0]) - NOTE_ROWS, rows[0][0].shape[1]
    vmem = pl.BlockSpec(memory_space=pltpu.VMEM)
    out_shape = [pltpu.VMEM((tok_count, width), out_type)] * sources
    if load:
        chip_experts = 2 * weights[0][0].shape[0]
        out_shape = out_shape + [pltpu.VMEM((chip_experts, *own.shape[1:]), BF16) for own, _ in weights]
        weight_args = [array for pair in weights for array in pair]
        weight_specs = [pl.BlockSpec(memory_space=pl.ANY)] * 6
        semaphores = [pltpu.SemaphoreType.DMA((3, chip_experts))]
    else:
        chip_experts = weights[0].shape[0]
        weight_args, weight_specs, semaphores = held_in_vmem(weights), [vmem] * 3, []
    return pl.pallas_call(
        functools.partial(experts_kernel, sources, pieces, load),
        in_specs=[vmem] * (pieces * sources) + weight_specs,
        out_specs=[vmem] * len(out_shape),
        out_shape=out_shape,
        scratch_shapes=[
            pltpu.VMEM((chip_experts, sources, CAP, width), BF16),
            pltpu.VMEM((sources, chip_experts * CAP, width), BF16),
            pltpu.VMEM((sources, chip_experts * CAP, tok_count), BF16),
            *semaphores,
        ],
        compiler_params=pltpu.CompilerParams(vmem_limit_bytes=VMEM_EXPERTS * MIB),
        cost_estimate=pl.CostEstimate(flops=12000 * MIB, bytes_accessed=30 * MIB, transcendentals=0),
        name="experts",
    )(*held_in_vmem([piece for source in rows for piece in source]), *weight_args)


CORE, ACROSS_X, ACROSS_Y = 1, 2, 4


def swap(array, mask):
    return lax.ppermute(array, "req", [(i, i ^ mask) for i in range(lax.axis_size("req"))])


def ordered(*arrays):
    return lax.optimization_barrier(arrays)


def local_chips(
    tokens,
    attn_gain,
    w_query,
    w_key,
    w_value,
    w_out,
    prefix_keys,
    prefix_values,
    lengths,
    assignment,
    moe_gain,
    expert_ids,
    route_weights,
    w_gate,
    w_up,
    w_down,
):
    peer_count = lax.axis_size("req")
    own_rows = tokens[0]
    tok_count = own_rows.shape[0]
    prefix_len = prefix_keys.shape[1] * peer_count
    keys, values = prefix_keys[0], prefix_values[0]
    block = keys.shape[0]
    cached = jnp.concatenate([keys, values], axis=0)
    cached_x, cached_y = swap(cached, ACROSS_X), swap(cached, ACROSS_Y)
    cached_mate = swap(cached, CORE)

    queries, state = attend_near(
        own_rows, attn_gain, w_query, w_key, w_value, prefix_len, lengths, assignment, keys, values, cached_mate
    )
    cached_x, cached_y, *state = ordered(cached_x, cached_y, *state)
    far = [swap(cached_x[:block], ACROSS_Y), swap(cached_y[block:], ACROSS_X)]
    mates = [swap(cached_x, CORE), swap(cached_y, CORE)]
    *mates, w_gate = ordered(*mates, w_gate)
    gate = (w_gate, swap(w_gate, CORE))
    state = attend_far(queries, state, [cached_x, cached_y, *mates])
    *far, gate, s0, s1 = ordered(*far, gate, *state)
    far_mate = [swap(array, CORE) for array in far]
    *far_mate, w_up, w_down = ordered(*far_mate, w_up, w_down)
    up, down = (w_up, swap(w_up, CORE)), (w_down, swap(w_down, CORE))
    context, hidden, moe_in = attend_far(
        queries,
        [s0, s1],
        [tuple(far), tuple(far_mate)],
        final=(own_rows, w_out, moe_gain, expert_ids[0], route_weights[0]),
    )

    weights = (gate, up, down)
    half = tok_count // 2
    rows_x, rows_y = swap(moe_in, ACROSS_X), swap(moe_in, ACROSS_Y)
    own, *weights = run_experts([[moe_in]], weights, load=True, out_type=F32)
    rows_x, rows_y, own = ordered(rows_x, rows_y, own)
    low_xy, high_xy = swap(rows_x[:half], ACROSS_Y), swap(rows_y[half:], ACROSS_X)
    to_x, to_y = run_experts([[rows_x], [rows_y]], weights)
    low_xy, high_xy, to_x, to_y = ordered(low_xy, high_xy, to_x, to_y)
    from_x, from_y = swap(to_x, ACROSS_X), swap(to_y, ACROSS_Y)
    (to_xy,) = run_experts([[low_xy, high_xy]], weights)
    from_xy = swap(to_xy, ACROSS_X | ACROSS_Y)
    partial, from_xy = ordered(own + from_x.astype(F32) + from_y.astype(F32), from_xy)
    expert_mix = (partial + from_xy.astype(F32)).astype(BF16)
    return (context[None], hidden[None], expert_mix[None])


def solution(mesh):
    placed = (
        P("grp", "req", None),
        P(),
        P(),
        P(),
        P(),
        P(),
        P("grp", "req", None),
        P("grp", "req", None),
        P("grp", None),
        P("grp", None),
        P(),
        P("grp", "req", None),
        P("grp", "req", None),
        P("req", None, None),
        P("req", None, None),
        P("req", None, None),
    )
    return jax.shard_map(
        local_chips if mesh.shape["req"] == 8 else local_general,
        mesh=mesh,
        in_specs=placed,
        out_specs=(P("grp", "req", None), P("grp", "req", None), P("grp", "req", None)),
        check_vma=False,
    )
```

```python
import functools
import math

import jax
import jax.numpy as jnp
import numpy as np
from jax import lax
from jax.experimental import pallas as pl
from jax.experimental.pallas import tpu as pltpu
from jax.sharding import PartitionSpec as P

H = 16
KV = 8
HD = 64
EXPERTS = 32
TOP = 8
CAP = 96


NORM_EPS = 1e-06
ATTN_SCALE = 0.015625
RESIDUAL_SCALE = 0.22
ROPE_BASE = 10000.0


def normalize(head_rows, gain):
    widened = head_rows.astype(jnp.float32)
    mean_square = jnp.mean(widened * widened, axis=-1, keepdims=True)
    return (widened * lax.rsqrt(mean_square + NORM_EPS) * gain).astype(jnp.bfloat16)


def rotate(head_rows, positions):
    half_dim = head_rows.shape[-1] // 2
    frequency = ROPE_BASE ** (
        -(jnp.arange(half_dim, dtype=jnp.float32) * 2.0 / head_rows.shape[-1])
    )
    angles = positions[:, None] * frequency[None, :]
    cosine = jnp.cos(angles)[:, None, :]
    sine_part = jnp.sin(angles)[:, None, :]
    first_half = head_rows[..., :half_dim]
    second_half = head_rows[..., half_dim:]
    return jnp.concatenate(
        [
            first_half * cosine - second_half * sine_part,
            second_half * cosine + first_half * sine_part,
        ],
        axis=-1,
    )


def fresh_state(tok_count):
    return (
        jnp.full((KV, H // KV, tok_count), -jnp.inf, jnp.float32),
        jnp.zeros((KV, H // KV, tok_count), jnp.float32),
        jnp.zeros((KV, H // KV, tok_count, HD), jnp.float32),
    )


def absorb(run_state, grouped, key_rows, value_rows, visible):
    run_max, run_sum, run_acc = run_state
    scores = (
        jnp.einsum("tkgd,skd->kgts", grouped, key_rows, preferred_element_type=jnp.float32)
        * ATTN_SCALE
    )
    scores = jnp.where(visible, scores, -jnp.inf)
    new_max = jnp.maximum(run_max, jnp.max(scores, axis=-1))
    factor = jnp.exp(run_max - new_max)
    weights = jnp.exp(scores - new_max[..., None])
    run_sum = run_sum * factor + jnp.sum(weights, axis=-1)
    gathered_values = jnp.einsum(
        "kgts,skd->kgtd",
        weights.astype(jnp.bfloat16),
        value_rows,
        preferred_element_type=jnp.float32,
    )
    run_acc = run_acc * factor[..., None] + gathered_values
    return (new_max, run_sum, run_acc)


def slot_numbers(ids):
    chosen = ids.reshape(-1)
    hit_table = (chosen[:, None] == jnp.arange(EXPERTS, dtype=jnp.int32)[None, :]).astype(jnp.int32)
    before = jnp.cumsum(hit_table, axis=0) - hit_table
    ranked = jnp.sum(before * hit_table, axis=1)
    return (chosen, ranked)


def local_general(
    tokens,
    attn_gain,
    w_query,
    w_key,
    w_value,
    w_out,
    prefix_keys,
    prefix_values,
    lengths,
    assignment,
    moe_gain,
    expert_ids,
    route_weights,
    w_gate,
    w_up,
    w_down,
):
    tok_count = tokens.shape[1]
    model_width = tokens.shape[2]
    peer_count = lax.axis_size("req")
    prefix_len = prefix_keys.shape[1] * peer_count
    own_rows = tokens[0]
    normed = normalize(own_rows, attn_gain)
    my_index = lax.axis_index("req")
    request_ids = jnp.arange(lengths.shape[1], dtype=jnp.int32)
    request = jnp.sum(jnp.where(request_ids == my_index, assignment[0], 0))
    suffix_len = jnp.sum(jnp.where(request_ids == request, lengths[0], 0))
    positions = (prefix_len + jnp.arange(tok_count, dtype=jnp.int32)).astype(jnp.float32)
    queries = jnp.dot(normed, w_query, preferred_element_type=jnp.float32).reshape(tok_count, H, HD)
    queries = rotate(queries, positions).astype(jnp.bfloat16)
    suffix_keys = jnp.dot(normed, w_key, preferred_element_type=jnp.float32).reshape(
        tok_count, KV, HD
    )
    suffix_keys = rotate(suffix_keys, positions).astype(jnp.bfloat16)
    suffix_values = (
        jnp.dot(normed, w_value, preferred_element_type=jnp.float32)
        .astype(jnp.bfloat16)
        .reshape(tok_count, KV, HD)
    )
    grouped = queries.reshape(tok_count, KV, H // KV, HD)
    slot_row = jnp.arange(tok_count, dtype=jnp.int32)
    suffix_visible = (slot_row[None, :] <= slot_row[:, None]) & (slot_row[None, :] < suffix_len)
    suffix_state = absorb(
        fresh_state(tok_count), grouped, suffix_keys, suffix_values, suffix_visible[None, None]
    )
    run_state = suffix_state
    key_piece = lax.all_gather(prefix_keys, "req", axis=1, tiled=True)
    value_piece = lax.all_gather(prefix_values, "req", axis=1, tiled=True)
    piece_len = key_piece.shape[1]
    key_block = math.gcd(piece_len, 512)
    key_blocks = key_piece[0].reshape(piece_len // key_block, key_block, KV, HD)
    value_blocks = value_piece[0].reshape(piece_len // key_block, key_block, KV, HD)

    def absorb_step(carry, pair_set):
        return (absorb(carry, grouped, pair_set[0], pair_set[1], True), None)

    run_state, unused = lax.scan(absorb_step, run_state, (key_blocks, value_blocks))
    run_max, run_sum, run_acc = run_state
    context = (
        (run_acc / run_sum[..., None])
        .transpose(2, 0, 1, 3)
        .reshape(tok_count, H * HD)
        .astype(jnp.bfloat16)
    )
    projected = jnp.dot(context, w_out, preferred_element_type=jnp.float32)
    hidden = (own_rows.astype(jnp.float32) + RESIDUAL_SCALE * projected).astype(jnp.bfloat16)
    moe_in = normalize(hidden, moe_gain)
    chosen, ranked = slot_numbers(expert_ids[0])
    slot_index = chosen * CAP + ranked
    sources = jnp.repeat(moe_in, TOP, axis=0)
    outgoing = jnp.zeros((EXPERTS * CAP, model_width), jnp.bfloat16).at[slot_index].set(sources)
    outgoing = outgoing.reshape(peer_count, EXPERTS // peer_count, CAP, model_width)
    arrived = lax.all_to_all(outgoing, "req", split_axis=0, concat_axis=0, tiled=True)
    slot_span = arrived.shape[2]
    results = []
    for expert_local in range(arrived.shape[1]):
        expert_rows = arrived[:, expert_local].reshape(-1, model_width)
        gate_act = jnp.dot(expert_rows, w_gate[expert_local], preferred_element_type=jnp.float32)
        up_act = jnp.dot(expert_rows, w_up[expert_local], preferred_element_type=jnp.float32)
        product = (jax.nn.silu(gate_act) * up_act).astype(jnp.bfloat16)
        expert_out = jnp.dot(
            product, w_down[expert_local], preferred_element_type=jnp.float32
        ).astype(jnp.bfloat16)
        results.append(expert_out.reshape(arrived.shape[0], slot_span, model_width))
    produced = jnp.stack(results, axis=1)
    returned = lax.all_to_all(produced, "req", split_axis=0, concat_axis=0, tiled=True).reshape(
        EXPERTS * CAP, model_width
    )
    picked = returned[slot_index].astype(jnp.float32).reshape(tok_count, TOP, model_width)
    expert_mix = jnp.sum(picked * route_weights[0][..., None], axis=1).astype(jnp.bfloat16)
    return (context[None], hidden[None], expert_mix[None])


F32 = jnp.float32
BF16 = jnp.bfloat16
MIB = 1 << 20
LANES = 128
VMEM_ATTEND = 54
VMEM_LAST = 57
VMEM_NEAR = 54
NOTE_ROWS = 16
VMEM_EXPERTS = 17


def dot(lhs, rhs):
    return jnp.dot(lhs, rhs, preferred_element_type=F32)


def dot_nt(lhs, rhs):
    return lax.dot_general(lhs, rhs, (((1,), (1,)), ((), ())), preferred_element_type=F32)


def dot_tn(lhs, rhs):
    return lax.dot_general(lhs, rhs, (((0,), (0,)), ((), ())), preferred_element_type=F32)


def held_in_hbm(arrays):
    return [pltpu.with_memory_space_constraint(array, pltpu.HBM) for array in arrays]


def held_in_vmem(arrays):
    return [pltpu.with_memory_space_constraint(array, pltpu.VMEM) for array in arrays]


def lane_index(shape):
    return lax.broadcasted_iota(jnp.int32, shape, len(shape) - 1)


def rope_tables(prefix_len, tok_count):
    frequency = ROPE_BASE ** (-(np.arange(HD // 2, dtype=np.float64) * 2.0 / HD))
    angles = (prefix_len + np.arange(tok_count, dtype=np.float64))[:, None] * frequency[None, :]
    cosine, sine = np.cos(angles), np.sin(angles)
    cosine = np.concatenate([cosine, cosine, cosine, cosine], axis=1)
    sine = np.concatenate([-sine, sine, -sine, sine], axis=1)
    return jnp.asarray(cosine, F32), jnp.asarray(sine, F32)


def rotate_tile(tile, cosine, sine):
    first = lane_index(tile.shape) % HD < HD // 2
    other = jnp.where(
        first, pltpu.roll(tile, LANES - HD // 2, 1), pltpu.roll(tile, HD // 2, 1)
    )
    return tile * cosine + other * sine


SUM_ROWS = 16


def attend_heads(queries, key_tiles, value_tiles, suffix_len, states):
    heads = len(queries)
    tok_count = queries[0].shape[0] // 2
    turned = [[tile.astype(F32).T.astype(BF16) for tile in tiles] for tiles in value_tiles]
    ones = jnp.ones((SUM_ROWS, turned[0][0].shape[1]), BF16)

    def scores_of(head):
        scores = [dot_nt(tile, queries[head]) for tile in key_tiles[head // 2]]
        if suffix_len is not None:
            shape = scores[0].shape
            slot = lax.broadcasted_iota(jnp.int32, shape, 0)
            row = lane_index(shape) % tok_count
            visible = (slot <= row) & (slot < suffix_len)
            scores[0] = jnp.where(visible, scores[0], -1e30)
        return scores

    results = []
    ahead = scores_of(0)
    for head in range(heads):
        scores, ahead = ahead, scores_of(head + 1) if head + 1 < heads else None
        new_max = jnp.max(functools.reduce(jnp.maximum, scores), axis=0, keepdims=True)
        total = None
        if states is not None:
            old_max, old_total = states[head]
            new_max = jnp.maximum(new_max, old_max)
            total = old_total * jnp.exp(old_max - new_max)
        first_row = head % 2 * HD
        for score, tile in zip(scores, turned[head // 2]):
            weights = jnp.exp(score - new_max).astype(BF16)
            part = dot(jnp.concatenate([tile[first_row : first_row + HD], ones], axis=0), weights)
            total = part if total is None else total + part
        results.append((new_max, total))
    return results


def pair_tiles(refs):
    pairs = refs[0].shape[1] // LANES
    return [[ref[:, pair * LANES : (pair + 1) * LANES] for ref in refs] for pair in range(pairs)]


def near_kernel(*refs):
    tok_ref, gain_ref, *held = refs[:5]
    cos_ref, sin_ref, lengths_ref, order_ref, keys_ref, values_ref, mate_keys_ref, mate_values_ref = refs[5:13]
    q_ref, max_ref, acc_ref = refs[13:]
    suffix_len = lengths_ref[0, order_ref[0, lax.axis_index("req")]]
    rows = tok_ref[...].astype(F32)
    mean_square = jnp.mean(rows * rows, axis=-1, keepdims=True)
    normed = (rows * lax.rsqrt(mean_square + NORM_EPS) * gain_ref[...]).astype(BF16)
    cosine, sine = cos_ref[...], sin_ref[...]
    low = lane_index(cosine.shape) < HD
    queries, key_tiles, value_tiles = [], [], []
    for pair in range(KV // 2):
        lanes = slice(pair * LANES, (pair + 1) * LANES)
        suffix_keys = rotate_tile(dot(normed, held[1][:, lanes]), cosine, sine).astype(BF16)
        suffix_values = dot(normed, held[2][:, lanes]).astype(BF16)
        key_tiles.append([suffix_keys, keys_ref[:, lanes], mate_keys_ref[:, lanes]])
        value_tiles.append([suffix_values, values_ref[:, lanes], mate_values_ref[:, lanes]])
        projected = dot(normed, held[0][:, 2 * pair * LANES : 2 * (pair + 1) * LANES])
        for half in range(2):
            tile = rotate_tile(projected[:, half * LANES : (half + 1) * LANES], cosine, sine) * ATTN_SCALE
            turned = pltpu.roll(tile, HD, 1)
            if half == 0:
                first, second = jnp.where(low, tile, 0.0), jnp.where(low, turned, 0.0)
            else:
                first, second = jnp.where(low, 0.0, turned), jnp.where(low, 0.0, tile)
            queries.append(jnp.concatenate([first, second], axis=0).astype(BF16))
            q_ref[2 * pair + half] = queries[-1]
    results = attend_heads(queries, key_tiles, value_tiles, suffix_len, None)
    for head, (new_max, total) in enumerate(results):
        max_ref[head] = new_max
        acc_ref[head] = total


def whole_spec(*shape):
    return pl.BlockSpec(shape, lambda i: (0,) * len(shape))


def cached_specs(cached):
    specs = []
    for kind in range(2):
        for array in cached:
            stacked = not isinstance(array, tuple)
            length = array.shape[0] // 2 if stacked else array[0].shape[0]
            place = kind if stacked else 0
            specs.append(pl.BlockSpec((length, KV * HD), lambda i, place=place: (place, 0)))
    return specs


def cached_args(cached):
    return [array[kind] if isinstance(array, tuple) else array for kind in range(2) for array in cached]


def attend_near(own_rows, attn_gain, w_query, w_key, w_value, prefix_len, lengths, assignment, keys, values, mate):
    tok_count, width = own_rows.shape
    rows, block = 2 * tok_count, keys.shape[0]
    cosine, sine = rope_tables(prefix_len, tok_count)
    smem = pl.BlockSpec(memory_space=pltpu.SMEM)
    queries, *state = pl.pallas_call(
        near_kernel,
        grid=(1,),
        in_specs=[whole_spec(tok_count, width), whole_spec(1, width)]
        + [whole_spec(*array.shape) for array in (w_query, w_key, w_value)]
        + [whole_spec(tok_count, LANES)] * 2
        + [smem, smem]
        + [whole_spec(block, KV * HD)] * 4,
        out_specs=[whole_spec(KV, rows, LANES), whole_spec(KV, 1, rows), whole_spec(KV, HD + SUM_ROWS, rows)],
        out_shape=[
            pltpu.VMEM((KV, rows, LANES), BF16),
            pltpu.VMEM((KV, 1, rows), F32),
            pltpu.VMEM((KV, HD + SUM_ROWS, rows), F32),
        ],
        compiler_params=pltpu.CompilerParams(vmem_limit_bytes=VMEM_NEAR * MIB),
        cost_estimate=pl.CostEstimate(flops=4000 * MIB, bytes_accessed=6 * MIB, transcendentals=0),
        name="attend_near",
    )(
        *held_in_hbm([own_rows, attn_gain.reshape(1, width), w_query, w_key, w_value, cosine, sine]),
        *held_in_hbm([lengths, assignment, keys, values]),
        *held_in_vmem(mate),
    )
    return queries, state


def far_kernel(blocks, last, *refs):
    q_ref, max_in, acc_in = refs[:3]
    key_refs, value_refs = refs[3 : 3 + blocks], refs[3 + blocks : 3 + 2 * blocks]
    refs = refs[3 + 2 * blocks :]
    heads = q_ref.shape[0]
    states = [(max_in[head], acc_in[head]) for head in range(heads)]
    queries = [q_ref[head] for head in range(heads)]
    results = attend_heads(queries, pair_tiles(key_refs), pair_tiles(value_refs), None, states)
    if not last:
        max_ref, acc_ref = refs
        for half, (new_max, total) in enumerate(results):
            max_ref[half] = new_max
            acc_ref[half] = total
        return
    tok_ref, w_out_ref, gain_ref, ids_ref, route_ref, ctx_ref, hidden_ref, moe_ref = refs
    tok_count = tok_ref.shape[0]
    tiles = []
    for _, total in results:
        mixed = total[:HD] / total[HD : HD + 1]
        tiles.append(jnp.concatenate([mixed[:, :tok_count], mixed[:, tok_count:]], axis=0).T)
    context = jnp.concatenate(tiles, axis=1).astype(BF16)
    ctx_ref[...] = context
    projected = dot(context, w_out_ref[...])
    hidden = (tok_ref[...].astype(F32) + RESIDUAL_SCALE * projected).astype(BF16)
    hidden_ref[...] = hidden
    wide = hidden.astype(F32)
    mean_square = jnp.mean(wide * wide, axis=-1, keepdims=True)
    moe_ref[:tok_count] = (wide * lax.rsqrt(mean_square + NORM_EPS) * gain_ref[...]).astype(BF16)
    moe_ref[tok_count:] = jnp.zeros((NOTE_ROWS, wide.shape[1]), BF16)
    moe_ref[tok_count : tok_count + TOP, :tok_count] = ids_ref[...].astype(F32).astype(BF16)
    moe_ref[tok_count : tok_count + TOP, tok_count : 2 * tok_count] = route_ref[...].astype(BF16)


def attend_far(queries, state, cached, final=None):
    last, blocks, rows = final is not None, len(cached), queries.shape[1]
    tok_count = rows // 2
    args, tiles = [queries, *state], held_in_vmem(cached_args(cached))
    in_specs = [whole_spec(KV, rows, LANES), whole_spec(KV, 1, rows), whole_spec(KV, HD + SUM_ROWS, rows)]
    in_specs += cached_specs(cached)
    if last:
        own_rows, w_out, moe_gain, expert_ids, route_weights = final
        width = own_rows.shape[1]
        own_args = [own_rows, w_out, moe_gain.reshape(1, width), expert_ids.T, route_weights.T]
        whole = whole_spec(tok_count, width)
        in_specs += [whole, whole_spec(*w_out.shape), whole_spec(1, width)]
        in_specs += [whole_spec(TOP, tok_count)] * 2
        out_specs = [whole, whole, whole_spec(tok_count + NOTE_ROWS, width)]
        out_shape = [pltpu.HBM((tok_count, width), BF16)] * 2 + [pltpu.VMEM((tok_count + NOTE_ROWS, width), BF16)]
    else:
        own_args = []
        out_specs = in_specs[1:3]
        out_shape = [pltpu.VMEM(array.shape, F32) for array in state]
    return pl.pallas_call(
        functools.partial(far_kernel, blocks, last),
        grid=(1,),
        in_specs=in_specs,
        out_specs=out_specs,
        out_shape=out_shape,
        compiler_params=pltpu.CompilerParams(vmem_limit_bytes=(VMEM_LAST if last else VMEM_ATTEND) * MIB),
        cost_estimate=pl.CostEstimate(flops=blocks * 1200 * MIB, bytes_accessed=4 * MIB, transcendentals=0),
        name="attend_far",
    )(*held_in_vmem(args), *tiles, *held_in_hbm(own_args))


def experts_kernel(sources, pieces, owners, load, *refs):
    refs = list(refs)
    take = lambda n: [refs.pop(0) for _ in range(n)]
    row_refs = [take(pieces) for _ in range(sources)]
    weight_refs = [take(3) for _ in owners]
    out_refs = take(sources)
    held = [take(3) for _ in owners] if load else weight_refs
    picked_ref, made_ref, combine_ref, *sems = refs
    local_experts = held[0][0].shape[0]
    experts = len(owners) * local_experts
    tok_count, width = out_refs[0].shape
    slots = experts * CAP
    me = lax.axis_index("req")
    firsts = [(me + owner * (1 - 2 * lax.rem(me, 2))) * local_experts for owner in owners]

    def copy(group, kind, e):
        return pltpu.make_async_copy(
            weight_refs[group][kind].at[e], held[group][kind].at[e], sems[0].at[group, kind, e]
        )

    for group in range(len(owners) if load else 0):
        for e in range(local_experts):
            for kind in range(3):
                copy(group, kind, e).start()

    before = lax.broadcasted_iota(jnp.int32, (tok_count, tok_count), 0)
    after = lane_index((tok_count, tok_count))
    earlier = jnp.where(before < after, 1.0, 0.0).astype(BF16)
    slot = lax.broadcasted_iota(jnp.int32, (slots, EXPERTS), 0) // CAP
    held_here = slot + firsts[0]
    if len(owners) > 1:
        held_here = jnp.where(slot < local_experts, held_here, slot + (firsts[1] - local_experts))
    spread = jnp.where(held_here == lane_index((slots, EXPERTS)), 1.0, 0.0).astype(BF16)
    within = (lax.broadcasted_iota(jnp.int32, (slots, tok_count), 0) % CAP).astype(F32)
    expert_row = lax.broadcasted_iota(jnp.int32, (EXPERTS, tok_count), 0).astype(F32)
    for source in range(sources):
        message = jnp.concatenate([ref[...] for ref in row_refs[source]], axis=0)
        rows, note = message[:tok_count], message[tok_count:].astype(F32)
        route = jnp.zeros((EXPERTS, tok_count), F32)
        for k in range(TOP):
            chosen, gain = note[k : k + 1, :tok_count], note[k : k + 1, tok_count : 2 * tok_count]
            route = jnp.where(chosen == expert_row, gain, route)
        hit = route > 0.0
        ranked = dot(jnp.where(hit, 1.0, 0.0).astype(BF16), earlier)
        ranked = jnp.where(hit, ranked, -1.0).astype(BF16)
        match = dot(spread, ranked) == within
        pick = jnp.where(match, 1.0, 0.0).astype(BF16)
        combine_ref[source] = jnp.where(match, dot(spread, route.astype(BF16)), 0.0).astype(BF16)
        picked = dot(pick, rows).astype(BF16)
        for e in range(experts):
            picked_ref[e, source] = picked[e * CAP : (e + 1) * CAP]

    def one_expert(group, e, carry):
        for kind in range(3 if load else 0):
            copy(group, kind, e).wait()
        expert = group * local_experts + e
        rows = picked_ref[expert].reshape(sources * CAP, width)
        gate = dot(rows, held[group][0][e])
        up = dot(rows, held[group][1][e])
        act = (jax.nn.silu(gate) * up).astype(BF16)
        made = dot(act, held[group][2][e]).astype(BF16)
        for source in range(sources):
            made_ref[source, pl.ds(pl.multiple_of(expert * CAP, CAP), CAP), :] = made[
                source * CAP : (source + 1) * CAP
            ]
        return carry

    for group in range(len(owners)):
        lax.fori_loop(0, local_experts, functools.partial(one_expert, group), 0)
    for source, ref in enumerate(out_refs):
        ref[...] = dot_tn(combine_ref[source], made_ref[source]).astype(ref.dtype)


def run_experts(rows, weights, owners=(0, 1), load=False, out_type=BF16):
    sources, pieces = len(rows), len(rows[0])
    tok_count, width = sum(piece.shape[0] for piece in rows[0]) - NOTE_ROWS, rows[0][0].shape[1]
    vmem = pl.BlockSpec(memory_space=pltpu.VMEM)
    weight_args = [array for owned in weights for array in owned]
    local_experts = weight_args[0].shape[0]
    experts = len(owners) * local_experts
    out_shape = [pltpu.VMEM((tok_count, width), out_type)] * sources
    if load:
        out_shape = out_shape + [pltpu.VMEM(array.shape, BF16) for array in weight_args]
        weight_args, weight_specs = held_in_hbm(weight_args), [pl.BlockSpec(memory_space=pl.ANY)] * len(weight_args)
        semaphores = [pltpu.SemaphoreType.DMA((len(owners), 3, local_experts))]
    else:
        weight_args, weight_specs, semaphores = held_in_vmem(weight_args), [vmem] * len(weight_args), []
    return pl.pallas_call(
        functools.partial(experts_kernel, sources, pieces, owners, load),
        in_specs=[vmem] * (pieces * sources) + weight_specs,
        out_specs=[vmem] * len(out_shape),
        out_shape=out_shape,
        scratch_shapes=[
            pltpu.VMEM((experts, sources, CAP, width), BF16),
            pltpu.VMEM((sources, experts * CAP, width), BF16),
            pltpu.VMEM((sources, experts * CAP, tok_count), BF16),
            *semaphores,
        ],
        compiler_params=pltpu.CompilerParams(vmem_limit_bytes=VMEM_EXPERTS * MIB),
        cost_estimate=pl.CostEstimate(flops=12000 * MIB, bytes_accessed=30 * MIB, transcendentals=0),
        name="experts",
    )(*held_in_vmem([piece for source in rows for piece in source]), *weight_args)


CORE, ACROSS_X, ACROSS_Y = 1, 2, 4


def swap(array, mask):
    return lax.ppermute(array, "req", [(i, i ^ mask) for i in range(lax.axis_size("req"))])


def ordered(*arrays):
    return lax.optimization_barrier(arrays)


def local_chips(
    tokens,
    attn_gain,
    w_query,
    w_key,
    w_value,
    w_out,
    prefix_keys,
    prefix_values,
    lengths,
    assignment,
    moe_gain,
    expert_ids,
    route_weights,
    w_gate,
    w_up,
    w_down,
):
    peer_count = lax.axis_size("req")
    own_rows = tokens[0]
    tok_count = own_rows.shape[0]
    prefix_len = prefix_keys.shape[1] * peer_count
    keys, values = prefix_keys[0], prefix_values[0]
    block = keys.shape[0]
    keys_x, values_y = swap(keys, ACROSS_X), swap(values, ACROSS_Y)
    values_x, keys_y = swap(values, ACROSS_X), swap(keys, ACROSS_Y)
    cached_mate = (swap(keys, CORE), swap(values, CORE))

    queries, state = attend_near(
        own_rows, attn_gain, w_query, w_key, w_value, prefix_len, lengths, assignment, keys, values, cached_mate
    )
    keys_x, values_x, keys_y, values_y, *state = ordered(keys_x, values_x, keys_y, values_y, *state)
    far = [swap(keys_x, ACROSS_Y), swap(values_y, ACROSS_X)]
    mates = [swap(array, CORE) for array in (keys_x, values_x, keys_y, values_y)]
    *mates, w_gate = ordered(*mates, w_gate)
    gate = (w_gate, swap(w_gate, CORE))
    near = [(keys_x, values_x), (keys_y, values_y), tuple(mates[:2]), tuple(mates[2:])]
    state = attend_far(queries, state, near)
    *far, gate, s0, s1 = ordered(*far, gate, *state)
    far_mate = [swap(array, CORE) for array in far]
    *far_mate, w_up, w_down = ordered(*far_mate, w_up, w_down)
    up, down = (w_up, swap(w_up, CORE)), (w_down, swap(w_down, CORE))
    context, hidden, moe_in = attend_far(
        queries,
        [s0, s1],
        [tuple(far), tuple(far_mate)],
        final=(own_rows, w_out, moe_gain, expert_ids[0], route_weights[0]),
    )

    owned, mated = zip(gate, up, down)
    half = tok_count // 2
    rows_x, rows_y = swap(moe_in, ACROSS_X), swap(moe_in, ACROSS_Y)
    own, *owned = run_experts([[moe_in]], [owned], (0,), load=True, out_type=F32)
    moe_in, own = ordered(moe_in, own)
    more, *mated = run_experts([[moe_in]], [mated], (1,), load=True, out_type=F32)
    rows_x, rows_y, more = ordered(rows_x, rows_y, more)
    weights = [owned, mated]
    low_xy, high_xy = swap(rows_x[:half], ACROSS_Y), swap(rows_y[half:], ACROSS_X)
    to_x, to_y = run_experts([[rows_x], [rows_y]], weights)
    low_xy, high_xy, to_x, to_y = ordered(low_xy, high_xy, to_x, to_y)
    from_x, from_y = swap(to_x, ACROSS_X), swap(to_y, ACROSS_Y)
    (to_xy,) = run_experts([[low_xy, high_xy]], weights)
    from_xy = swap(to_xy, ACROSS_X | ACROSS_Y)
    partial, from_xy = ordered(own + more + from_x.astype(F32) + from_y.astype(F32), from_xy)
    expert_mix = (partial + from_xy.astype(F32)).astype(BF16)
    return (context[None], hidden[None], expert_mix[None])


def solution(mesh):
    placed = (
        P("grp", "req", None),
        P(),
        P(),
        P(),
        P(),
        P(),
        P("grp", "req", None),
        P("grp", "req", None),
        P("grp", None),
        P("grp", None),
        P(),
        P("grp", "req", None),
        P("grp", "req", None),
        P("req", None, None),
        P("req", None, None),
        P("req", None, None),
    )
    return jax.shard_map(
        local_chips if mesh.shape["req"] == 8 else local_general,
        mesh=mesh,
        in_specs=placed,
        out_specs=(P("grp", "req", None), P("grp", "req", None), P("grp", "req", None)),
        check_vma=False,
    )
```

```python
import functools
import math

import jax
import jax.numpy as jnp
import numpy as np
from jax import lax
from jax.experimental import pallas as pl
from jax.experimental.pallas import tpu as pltpu
from jax.sharding import PartitionSpec as P

H = 16
KV = 8
HD = 64
EXPERTS = 32
TOP = 8
CAP = 96


NORM_EPS = 1e-06
ATTN_SCALE = 0.015625
RESIDUAL_SCALE = 0.22
ROPE_BASE = 10000.0


def normalize(head_rows, gain):
    widened = head_rows.astype(jnp.float32)
    mean_square = jnp.mean(widened * widened, axis=-1, keepdims=True)
    return (widened * lax.rsqrt(mean_square + NORM_EPS) * gain).astype(jnp.bfloat16)


def rotate(head_rows, positions):
    half_dim = head_rows.shape[-1] // 2
    frequency = ROPE_BASE ** (
        -(jnp.arange(half_dim, dtype=jnp.float32) * 2.0 / head_rows.shape[-1])
    )
    angles = positions[:, None] * frequency[None, :]
    cosine = jnp.cos(angles)[:, None, :]
    sine_part = jnp.sin(angles)[:, None, :]
    first_half = head_rows[..., :half_dim]
    second_half = head_rows[..., half_dim:]
    return jnp.concatenate(
        [
            first_half * cosine - second_half * sine_part,
            second_half * cosine + first_half * sine_part,
        ],
        axis=-1,
    )


def fresh_state(tok_count):
    return (
        jnp.full((KV, H // KV, tok_count), -jnp.inf, jnp.float32),
        jnp.zeros((KV, H // KV, tok_count), jnp.float32),
        jnp.zeros((KV, H // KV, tok_count, HD), jnp.float32),
    )


def absorb(run_state, grouped, key_rows, value_rows, visible):
    run_max, run_sum, run_acc = run_state
    scores = (
        jnp.einsum("tkgd,skd->kgts", grouped, key_rows, preferred_element_type=jnp.float32)
        * ATTN_SCALE
    )
    scores = jnp.where(visible, scores, -jnp.inf)
    new_max = jnp.maximum(run_max, jnp.max(scores, axis=-1))
    factor = jnp.exp(run_max - new_max)
    weights = jnp.exp(scores - new_max[..., None])
    run_sum = run_sum * factor + jnp.sum(weights, axis=-1)
    gathered_values = jnp.einsum(
        "kgts,skd->kgtd",
        weights.astype(jnp.bfloat16),
        value_rows,
        preferred_element_type=jnp.float32,
    )
    run_acc = run_acc * factor[..., None] + gathered_values
    return (new_max, run_sum, run_acc)


def slot_numbers(ids):
    chosen = ids.reshape(-1)
    hit_table = (chosen[:, None] == jnp.arange(EXPERTS, dtype=jnp.int32)[None, :]).astype(jnp.int32)
    before = jnp.cumsum(hit_table, axis=0) - hit_table
    ranked = jnp.sum(before * hit_table, axis=1)
    return (chosen, ranked)


def local_general(
    tokens,
    attn_gain,
    w_query,
    w_key,
    w_value,
    w_out,
    prefix_keys,
    prefix_values,
    lengths,
    assignment,
    moe_gain,
    expert_ids,
    route_weights,
    w_gate,
    w_up,
    w_down,
):
    tok_count = tokens.shape[1]
    model_width = tokens.shape[2]
    peer_count = lax.axis_size("req")
    prefix_len = prefix_keys.shape[1] * peer_count
    own_rows = tokens[0]
    normed = normalize(own_rows, attn_gain)
    my_index = lax.axis_index("req")
    request_ids = jnp.arange(lengths.shape[1], dtype=jnp.int32)
    request = jnp.sum(jnp.where(request_ids == my_index, assignment[0], 0))
    suffix_len = jnp.sum(jnp.where(request_ids == request, lengths[0], 0))
    positions = (prefix_len + jnp.arange(tok_count, dtype=jnp.int32)).astype(jnp.float32)
    queries = jnp.dot(normed, w_query, preferred_element_type=jnp.float32).reshape(tok_count, H, HD)
    queries = rotate(queries, positions).astype(jnp.bfloat16)
    suffix_keys = jnp.dot(normed, w_key, preferred_element_type=jnp.float32).reshape(
        tok_count, KV, HD
    )
    suffix_keys = rotate(suffix_keys, positions).astype(jnp.bfloat16)
    suffix_values = (
        jnp.dot(normed, w_value, preferred_element_type=jnp.float32)
        .astype(jnp.bfloat16)
        .reshape(tok_count, KV, HD)
    )
    grouped = queries.reshape(tok_count, KV, H // KV, HD)
    slot_row = jnp.arange(tok_count, dtype=jnp.int32)
    suffix_visible = (slot_row[None, :] <= slot_row[:, None]) & (slot_row[None, :] < suffix_len)
    suffix_state = absorb(
        fresh_state(tok_count), grouped, suffix_keys, suffix_values, suffix_visible[None, None]
    )
    run_state = suffix_state
    key_piece = lax.all_gather(prefix_keys, "req", axis=1, tiled=True)
    value_piece = lax.all_gather(prefix_values, "req", axis=1, tiled=True)
    piece_len = key_piece.shape[1]
    key_block = math.gcd(piece_len, 512)
    key_blocks = key_piece[0].reshape(piece_len // key_block, key_block, KV, HD)
    value_blocks = value_piece[0].reshape(piece_len // key_block, key_block, KV, HD)

    def absorb_step(carry, pair_set):
        return (absorb(carry, grouped, pair_set[0], pair_set[1], True), None)

    run_state, unused = lax.scan(absorb_step, run_state, (key_blocks, value_blocks))
    run_max, run_sum, run_acc = run_state
    context = (
        (run_acc / run_sum[..., None])
        .transpose(2, 0, 1, 3)
        .reshape(tok_count, H * HD)
        .astype(jnp.bfloat16)
    )
    projected = jnp.dot(context, w_out, preferred_element_type=jnp.float32)
    hidden = (own_rows.astype(jnp.float32) + RESIDUAL_SCALE * projected).astype(jnp.bfloat16)
    moe_in = normalize(hidden, moe_gain)
    chosen, ranked = slot_numbers(expert_ids[0])
    slot_index = chosen * CAP + ranked
    sources = jnp.repeat(moe_in, TOP, axis=0)
    outgoing = jnp.zeros((EXPERTS * CAP, model_width), jnp.bfloat16).at[slot_index].set(sources)
    outgoing = outgoing.reshape(peer_count, EXPERTS // peer_count, CAP, model_width)
    arrived = lax.all_to_all(outgoing, "req", split_axis=0, concat_axis=0, tiled=True)
    slot_span = arrived.shape[2]
    results = []
    for expert_local in range(arrived.shape[1]):
        expert_rows = arrived[:, expert_local].reshape(-1, model_width)
        gate_act = jnp.dot(expert_rows, w_gate[expert_local], preferred_element_type=jnp.float32)
        up_act = jnp.dot(expert_rows, w_up[expert_local], preferred_element_type=jnp.float32)
        product = (jax.nn.silu(gate_act) * up_act).astype(jnp.bfloat16)
        expert_out = jnp.dot(
            product, w_down[expert_local], preferred_element_type=jnp.float32
        ).astype(jnp.bfloat16)
        results.append(expert_out.reshape(arrived.shape[0], slot_span, model_width))
    produced = jnp.stack(results, axis=1)
    returned = lax.all_to_all(produced, "req", split_axis=0, concat_axis=0, tiled=True).reshape(
        EXPERTS * CAP, model_width
    )
    picked = returned[slot_index].astype(jnp.float32).reshape(tok_count, TOP, model_width)
    expert_mix = jnp.sum(picked * route_weights[0][..., None], axis=1).astype(jnp.bfloat16)
    return (context[None], hidden[None], expert_mix[None])


F32 = jnp.float32
BF16 = jnp.bfloat16
MIB = 1 << 20
LANES = 128
VMEM_ATTEND = 30
VMEM_LAST = 26
VMEM_NEAR = 30
NOTE_ROWS = 16
VMEM_EXPERTS = 17


def dot(lhs, rhs):
    return jnp.dot(lhs, rhs, preferred_element_type=F32)


def dot_nt(lhs, rhs):
    return lax.dot_general(lhs, rhs, (((1,), (1,)), ((), ())), preferred_element_type=F32)


def dot_tn(lhs, rhs):
    return lax.dot_general(lhs, rhs, (((0,), (0,)), ((), ())), preferred_element_type=F32)


def held_in_hbm(arrays):
    return [pltpu.with_memory_space_constraint(array, pltpu.HBM) for array in arrays]


def held_in_vmem(arrays):
    return [pltpu.with_memory_space_constraint(array, pltpu.VMEM) for array in arrays]


def lane_index(shape):
    return lax.broadcasted_iota(jnp.int32, shape, len(shape) - 1)


def rope_tables(prefix_len, tok_count):
    frequency = ROPE_BASE ** (-(np.arange(HD // 2, dtype=np.float64) * 2.0 / HD))
    angles = (prefix_len + np.arange(tok_count, dtype=np.float64))[:, None] * frequency[None, :]
    cosine, sine = np.cos(angles), np.sin(angles)
    cosine = np.concatenate([cosine, cosine, cosine, cosine], axis=1)
    sine = np.concatenate([-sine, sine, -sine, sine], axis=1)
    return jnp.asarray(cosine, F32), jnp.asarray(sine, F32)


def rotate_tile(tile, cosine, sine):
    first = lane_index(tile.shape) % HD < HD // 2
    other = jnp.where(
        first, pltpu.roll(tile, LANES - HD // 2, 1), pltpu.roll(tile, HD // 2, 1)
    )
    return tile * cosine + other * sine


SUM_ROWS = 16


def attend_heads(queries, key_tiles, value_tiles, suffix_len, states):
    heads = len(queries)
    tok_count = queries[0].shape[0] // 2
    turned = [[tile.astype(F32).T.astype(BF16) for tile in tiles] for tiles in value_tiles]
    ones = jnp.ones((SUM_ROWS, turned[0][0].shape[1]), BF16)

    def scores_of(head):
        scores = [dot_nt(tile, queries[head]) for tile in key_tiles[head // 2]]
        if suffix_len is not None:
            shape = scores[0].shape
            slot = lax.broadcasted_iota(jnp.int32, shape, 0)
            row = lane_index(shape) % tok_count
            visible = (slot <= row) & (slot < suffix_len)
            scores[0] = jnp.where(visible, scores[0], -1e30)
        return scores

    results = []
    ahead = scores_of(0)
    for head in range(heads):
        scores, ahead = ahead, scores_of(head + 1) if head + 1 < heads else None
        new_max = jnp.max(functools.reduce(jnp.maximum, scores), axis=0, keepdims=True)
        total = None
        if states is not None:
            old_max, old_total = states[head]
            new_max = jnp.maximum(new_max, old_max)
            total = old_total * jnp.exp(old_max - new_max)
        first_row = head % 2 * HD
        for score, tile in zip(scores, turned[head // 2]):
            weights = jnp.exp(score - new_max).astype(BF16)
            part = dot(jnp.concatenate([tile[first_row : first_row + HD], ones], axis=0), weights)
            total = part if total is None else total + part
        results.append((new_max, total))
    return results


def pair_tiles(refs):
    pairs = refs[0].shape[1] // LANES
    return [[ref[:, pair * LANES : (pair + 1) * LANES] for ref in refs] for pair in range(pairs)]


def near_kernel(*refs):
    tok_ref, gain_ref, *held = refs[:5]
    cos_ref, sin_ref, lengths_ref, order_ref, keys_ref, values_ref, mate_keys_ref, mate_values_ref = refs[5:13]
    q_ref, max_ref, acc_ref = refs[13:]
    suffix_len = lengths_ref[0, order_ref[0, lax.axis_index("req")]]
    rows = tok_ref[...].astype(F32)
    mean_square = jnp.mean(rows * rows, axis=-1, keepdims=True)
    normed = (rows * lax.rsqrt(mean_square + NORM_EPS) * gain_ref[...]).astype(BF16)
    cosine, sine = cos_ref[...], sin_ref[...]
    low = lane_index(cosine.shape) < HD
    queries, key_tiles, value_tiles = [], [], []
    for pair in range(KV // 2):
        lanes = slice(pair * LANES, (pair + 1) * LANES)
        suffix_keys = rotate_tile(dot(normed, held[1][:, lanes]), cosine, sine).astype(BF16)
        suffix_values = dot(normed, held[2][:, lanes]).astype(BF16)
        key_tiles.append([suffix_keys, keys_ref[:, lanes], mate_keys_ref[:, lanes]])
        value_tiles.append([suffix_values, values_ref[:, lanes], mate_values_ref[:, lanes]])
        projected = dot(normed, held[0][:, 2 * pair * LANES : 2 * (pair + 1) * LANES])
        for half in range(2):
            tile = rotate_tile(projected[:, half * LANES : (half + 1) * LANES], cosine, sine) * ATTN_SCALE
            turned = pltpu.roll(tile, HD, 1)
            if half == 0:
                first, second = jnp.where(low, tile, 0.0), jnp.where(low, turned, 0.0)
            else:
                first, second = jnp.where(low, 0.0, turned), jnp.where(low, 0.0, tile)
            queries.append(jnp.concatenate([first, second], axis=0).astype(BF16))
            q_ref[2 * pair + half] = queries[-1]
    results = attend_heads(queries, key_tiles, value_tiles, suffix_len, None)
    for head, (new_max, total) in enumerate(results):
        max_ref[head] = new_max
        acc_ref[head] = total


def whole_spec(*shape):
    return pl.BlockSpec(shape, lambda i: (0,) * len(shape))


def cached_specs(cached):
    specs = []
    for kind in range(2):
        for array in cached:
            stacked = not isinstance(array, tuple)
            length = array.shape[0] // 2 if stacked else array[0].shape[0]
            place = kind if stacked else 0
            specs.append(pl.BlockSpec((length, KV * HD), lambda i, place=place: (place, 0)))
    return specs


def cached_args(cached):
    return [array[kind] if isinstance(array, tuple) else array for kind in range(2) for array in cached]


def attend_near(own_rows, attn_gain, w_query, w_key, w_value, prefix_len, lengths, assignment, keys, values, mate):
    tok_count, width = own_rows.shape
    rows, block = 2 * tok_count, keys.shape[0]
    cosine, sine = rope_tables(prefix_len, tok_count)
    smem = pl.BlockSpec(memory_space=pltpu.SMEM)
    queries, *state = pl.pallas_call(
        near_kernel,
        grid=(1,),
        in_specs=[whole_spec(tok_count, width), whole_spec(1, width)]
        + [whole_spec(*array.shape) for array in (w_query, w_key, w_value)]
        + [whole_spec(tok_count, LANES)] * 2
        + [smem, smem]
        + [whole_spec(block, KV * HD)] * 4,
        out_specs=[whole_spec(KV, rows, LANES), whole_spec(KV, 1, rows), whole_spec(KV, HD + SUM_ROWS, rows)],
        out_shape=[
            pltpu.VMEM((KV, rows, LANES), BF16),
            pltpu.VMEM((KV, 1, rows), F32),
            pltpu.VMEM((KV, HD + SUM_ROWS, rows), F32),
        ],
        compiler_params=pltpu.CompilerParams(vmem_limit_bytes=VMEM_NEAR * MIB),
        cost_estimate=pl.CostEstimate(flops=4000 * MIB, bytes_accessed=6 * MIB, transcendentals=0),
        name="attend_near",
    )(
        *held_in_hbm([own_rows, attn_gain.reshape(1, width), w_query, w_key, w_value, cosine, sine]),
        *held_in_hbm([lengths, assignment, keys, values]),
        *held_in_vmem(mate),
    )
    return queries, state


def far_kernel(blocks, last, *refs):
    q_ref, max_in, acc_in = refs[:3]
    key_refs, value_refs = refs[3 : 3 + blocks], refs[3 + blocks : 3 + 2 * blocks]
    refs = refs[3 + 2 * blocks :]
    heads = q_ref.shape[0]
    states = [(max_in[head], acc_in[head]) for head in range(heads)]
    queries = [q_ref[head] for head in range(heads)]
    results = attend_heads(queries, pair_tiles(key_refs), pair_tiles(value_refs), None, states)
    if not last:
        max_ref, acc_ref = refs
        for half, (new_max, total) in enumerate(results):
            max_ref[half] = new_max
            acc_ref[half] = total
        return
    tok_ref, w_out_ref, gain_ref, ids_ref, route_ref, ctx_ref, hidden_ref, moe_ref = refs
    tok_count = tok_ref.shape[0]
    tiles = []
    for _, total in results:
        mixed = total[:HD] / total[HD : HD + 1]
        tiles.append(jnp.concatenate([mixed[:, :tok_count], mixed[:, tok_count:]], axis=0).T)
    context = jnp.concatenate(tiles, axis=1).astype(BF16)
    ctx_ref[...] = context
    projected = dot(context, w_out_ref[...])
    hidden = (tok_ref[...].astype(F32) + RESIDUAL_SCALE * projected).astype(BF16)
    hidden_ref[...] = hidden
    wide = hidden.astype(F32)
    mean_square = jnp.mean(wide * wide, axis=-1, keepdims=True)
    moe_ref[:tok_count] = (wide * lax.rsqrt(mean_square + NORM_EPS) * gain_ref[...]).astype(BF16)
    moe_ref[tok_count:] = jnp.zeros((NOTE_ROWS, wide.shape[1]), BF16)
    moe_ref[tok_count : tok_count + TOP, :tok_count] = ids_ref[...].astype(F32).astype(BF16)
    moe_ref[tok_count : tok_count + TOP, tok_count : 2 * tok_count] = route_ref[...].astype(BF16)


def attend_far(queries, state, cached, final=None):
    last, blocks, rows = final is not None, len(cached), queries.shape[1]
    tok_count = rows // 2
    args, tiles = [queries, *state], held_in_vmem(cached_args(cached))
    in_specs = [whole_spec(KV, rows, LANES), whole_spec(KV, 1, rows), whole_spec(KV, HD + SUM_ROWS, rows)]
    in_specs += cached_specs(cached)
    if last:
        own_rows, w_out, moe_gain, expert_ids, route_weights = final
        width = own_rows.shape[1]
        own_args = [own_rows, w_out, moe_gain.reshape(1, width), expert_ids.T, route_weights.T]
        whole = whole_spec(tok_count, width)
        in_specs += [whole, whole_spec(*w_out.shape), whole_spec(1, width)]
        in_specs += [whole_spec(TOP, tok_count)] * 2
        out_specs = [whole, whole, whole_spec(tok_count + NOTE_ROWS, width)]
        out_shape = [pltpu.HBM((tok_count, width), BF16)] * 2 + [pltpu.VMEM((tok_count + NOTE_ROWS, width), BF16)]
    else:
        own_args = []
        out_specs = in_specs[1:3]
        out_shape = [pltpu.VMEM(array.shape, F32) for array in state]
    return pl.pallas_call(
        functools.partial(far_kernel, blocks, last),
        grid=(1,),
        in_specs=in_specs,
        out_specs=out_specs,
        out_shape=out_shape,
        compiler_params=pltpu.CompilerParams(vmem_limit_bytes=(VMEM_LAST if last else VMEM_ATTEND) * MIB),
        cost_estimate=pl.CostEstimate(flops=blocks * 1200 * MIB, bytes_accessed=4 * MIB, transcendentals=0),
        name="attend_far",
    )(*held_in_vmem(args), *tiles, *held_in_hbm(own_args))


def experts_kernel(sources, pieces, owners, load, *refs):
    refs = list(refs)
    take = lambda n: [refs.pop(0) for _ in range(n)]
    row_refs = [take(pieces) for _ in range(sources)]
    weight_refs = [take(3) for _ in owners]
    out_refs = take(sources)
    held = [take(3) for _ in owners] if load else weight_refs
    picked_ref, made_ref, combine_ref, *sems = refs
    local_experts = held[0][0].shape[0]
    experts = len(owners) * local_experts
    tok_count, width = out_refs[0].shape
    slots = experts * CAP
    me = lax.axis_index("req")
    firsts = [(me + owner * (1 - 2 * lax.rem(me, 2))) * local_experts for owner in owners]

    def copy(group, kind, e):
        return pltpu.make_async_copy(
            weight_refs[group][kind].at[e], held[group][kind].at[e], sems[0].at[group, kind, e]
        )

    for group in range(len(owners) if load else 0):
        for e in range(local_experts):
            for kind in range(3):
                copy(group, kind, e).start()

    before = lax.broadcasted_iota(jnp.int32, (tok_count, tok_count), 0)
    after = lane_index((tok_count, tok_count))
    earlier = jnp.where(before < after, 1.0, 0.0).astype(BF16)
    slot = lax.broadcasted_iota(jnp.int32, (slots, EXPERTS), 0) // CAP
    held_here = slot + firsts[0]
    if len(owners) > 1:
        held_here = jnp.where(slot < local_experts, held_here, slot + (firsts[1] - local_experts))
    spread = jnp.where(held_here == lane_index((slots, EXPERTS)), 1.0, 0.0).astype(BF16)
    within = (lax.broadcasted_iota(jnp.int32, (slots, tok_count), 0) % CAP).astype(F32)
    expert_row = lax.broadcasted_iota(jnp.int32, (EXPERTS, tok_count), 0).astype(F32)
    for source in range(sources):
        message = jnp.concatenate([ref[...] for ref in row_refs[source]], axis=0)
        rows, note = message[:tok_count], message[tok_count:].astype(F32)
        route = jnp.zeros((EXPERTS, tok_count), F32)
        for k in range(TOP):
            chosen, gain = note[k : k + 1, :tok_count], note[k : k + 1, tok_count : 2 * tok_count]
            route = jnp.where(chosen == expert_row, gain, route)
        hit = route > 0.0
        ranked = dot(jnp.where(hit, 1.0, 0.0).astype(BF16), earlier)
        ranked = jnp.where(hit, ranked, -1.0).astype(BF16)
        match = dot(spread, ranked) == within
        pick = jnp.where(match, 1.0, 0.0).astype(BF16)
        combine_ref[source] = jnp.where(match, dot(spread, route.astype(BF16)), 0.0).astype(BF16)
        picked = dot(pick, rows).astype(BF16)
        for e in range(experts):
            picked_ref[e, source] = picked[e * CAP : (e + 1) * CAP]

    def one_expert(group, e, carry):
        for kind in range(3 if load else 0):
            copy(group, kind, e).wait()
        expert = group * local_experts + e
        rows = picked_ref[expert].reshape(sources * CAP, width)
        gate = dot(rows, held[group][0][e])
        up = dot(rows, held[group][1][e])
        act = (jax.nn.silu(gate) * up).astype(BF16)
        made = dot(act, held[group][2][e]).astype(BF16)
        for source in range(sources):
            made_ref[source, pl.ds(pl.multiple_of(expert * CAP, CAP), CAP), :] = made[
                source * CAP : (source + 1) * CAP
            ]
        return carry

    for group in range(len(owners)):
        lax.fori_loop(0, local_experts, functools.partial(one_expert, group), 0)
    for source, ref in enumerate(out_refs):
        ref[...] = dot_tn(combine_ref[source], made_ref[source]).astype(ref.dtype)


def run_experts(rows, weights, owners=(0, 1), load=False, out_type=BF16):
    sources, pieces = len(rows), len(rows[0])
    tok_count, width = sum(piece.shape[0] for piece in rows[0]) - NOTE_ROWS, rows[0][0].shape[1]
    vmem = pl.BlockSpec(memory_space=pltpu.VMEM)
    weight_args = [array for owned in weights for array in owned]
    local_experts = weight_args[0].shape[0]
    experts = len(owners) * local_experts
    out_shape = [pltpu.VMEM((tok_count, width), out_type)] * sources
    if load:
        out_shape = out_shape + [pltpu.VMEM(array.shape, BF16) for array in weight_args]
        weight_args, weight_specs = held_in_hbm(weight_args), [pl.BlockSpec(memory_space=pl.ANY)] * len(weight_args)
        semaphores = [pltpu.SemaphoreType.DMA((len(owners), 3, local_experts))]
    else:
        weight_args, weight_specs, semaphores = held_in_vmem(weight_args), [vmem] * len(weight_args), []
    return pl.pallas_call(
        functools.partial(experts_kernel, sources, pieces, owners, load),
        in_specs=[vmem] * (pieces * sources) + weight_specs,
        out_specs=[vmem] * len(out_shape),
        out_shape=out_shape,
        scratch_shapes=[
            pltpu.VMEM((experts, sources, CAP, width), BF16),
            pltpu.VMEM((sources, experts * CAP, width), BF16),
            pltpu.VMEM((sources, experts * CAP, tok_count), BF16),
            *semaphores,
        ],
        compiler_params=pltpu.CompilerParams(vmem_limit_bytes=VMEM_EXPERTS * MIB),
        cost_estimate=pl.CostEstimate(flops=12000 * MIB, bytes_accessed=30 * MIB, transcendentals=0),
        name="experts",
    )(*held_in_vmem([piece for source in rows for piece in source]), *weight_args)


CORE, ACROSS_X, ACROSS_Y = 1, 2, 4


def swap(array, mask):
    return lax.ppermute(array, "req", [(i, i ^ mask) for i in range(lax.axis_size("req"))])


def ordered(*arrays):
    return lax.optimization_barrier(arrays)


def local_chips(
    tokens,
    attn_gain,
    w_query,
    w_key,
    w_value,
    w_out,
    prefix_keys,
    prefix_values,
    lengths,
    assignment,
    moe_gain,
    expert_ids,
    route_weights,
    w_gate,
    w_up,
    w_down,
):
    peer_count = lax.axis_size("req")
    own_rows = tokens[0]
    tok_count = own_rows.shape[0]
    prefix_len = prefix_keys.shape[1] * peer_count
    keys, values = prefix_keys[0], prefix_values[0]
    block = keys.shape[0]
    keys_x, values_y = swap(keys, ACROSS_X), swap(values, ACROSS_Y)
    values_x, keys_y = swap(values, ACROSS_X), swap(keys, ACROSS_Y)
    cached_mate = (swap(keys, CORE), swap(values, CORE))

    queries, state = attend_near(
        own_rows, attn_gain, w_query, w_key, w_value, prefix_len, lengths, assignment, keys, values, cached_mate
    )
    keys_x, values_x, keys_y, values_y, *state = ordered(keys_x, values_x, keys_y, values_y, *state)
    far = [swap(keys_x, ACROSS_Y), swap(values_y, ACROSS_X)]
    mates = [swap(array, CORE) for array in (keys_x, values_x, keys_y, values_y)]
    *mates, w_gate = ordered(*mates, w_gate)
    gate = (w_gate, swap(w_gate, CORE))
    near = [(keys_x, values_x), (keys_y, values_y), tuple(mates[:2]), tuple(mates[2:])]
    state = attend_far(queries, state, near)
    *far, gate, s0, s1 = ordered(*far, gate, *state)
    far_mate = [swap(array, CORE) for array in far]
    *far_mate, w_up, w_down = ordered(*far_mate, w_up, w_down)
    up, down = (w_up, swap(w_up, CORE)), (w_down, swap(w_down, CORE))
    context, hidden, moe_in = attend_far(
        queries,
        [s0, s1],
        [tuple(far), tuple(far_mate)],
        final=(own_rows, w_out, moe_gain, expert_ids[0], route_weights[0]),
    )

    owned, mated = zip(gate, up, down)
    half = tok_count // 2
    rows_x, rows_y = swap(moe_in, ACROSS_X), swap(moe_in, ACROSS_Y)
    weights = [list(owned), list(mated)]
    (own,) = run_experts([[moe_in]], weights, out_type=F32)
    rows_x, rows_y, own = ordered(rows_x, rows_y, own)
    low_xy, high_xy = swap(rows_x[:half], ACROSS_Y), swap(rows_y[half:], ACROSS_X)
    to_x, to_y = run_experts([[rows_x], [rows_y]], weights)
    low_xy, high_xy, to_x, to_y = ordered(low_xy, high_xy, to_x, to_y)
    from_x, from_y = swap(to_x, ACROSS_X), swap(to_y, ACROSS_Y)
    (to_xy,) = run_experts([[low_xy, high_xy]], weights)
    from_xy = swap(to_xy, ACROSS_X | ACROSS_Y)
    partial, from_xy = ordered(own + from_x.astype(F32) + from_y.astype(F32), from_xy)
    expert_mix = (partial + from_xy.astype(F32)).astype(BF16)
    return (context[None], hidden[None], expert_mix[None])


def solution(mesh):
    placed = (
        P("grp", "req", None),
        P(),
        P(),
        P(),
        P(),
        P(),
        P("grp", "req", None),
        P("grp", "req", None),
        P("grp", None),
        P("grp", None),
        P(),
        P("grp", "req", None),
        P("grp", "req", None),
        P("req", None, None),
        P("req", None, None),
        P("req", None, None),
    )
    return jax.shard_map(
        local_chips if mesh.shape["req"] == 8 else local_general,
        mesh=mesh,
        in_specs=placed,
        out_specs=(P("grp", "req", None), P("grp", "req", None), P("grp", "req", None)),
        check_vma=False,
    )
```

```python
import functools
import math

import jax
import jax.numpy as jnp
import numpy as np
from jax import lax
from jax.experimental import pallas as pl
from jax.experimental.pallas import tpu as pltpu
from jax.sharding import PartitionSpec as P

H = 16
KV = 8
HD = 64
EXPERTS = 32
TOP = 8
CAP = 96


NORM_EPS = 1e-06
ATTN_SCALE = 0.015625
RESIDUAL_SCALE = 0.22
ROPE_BASE = 10000.0


def normalize(head_rows, gain):
    widened = head_rows.astype(jnp.float32)
    mean_square = jnp.mean(widened * widened, axis=-1, keepdims=True)
    return (widened * lax.rsqrt(mean_square + NORM_EPS) * gain).astype(jnp.bfloat16)


def rotate(head_rows, positions):
    half_dim = head_rows.shape[-1] // 2
    frequency = ROPE_BASE ** (
        -(jnp.arange(half_dim, dtype=jnp.float32) * 2.0 / head_rows.shape[-1])
    )
    angles = positions[:, None] * frequency[None, :]
    cosine = jnp.cos(angles)[:, None, :]
    sine_part = jnp.sin(angles)[:, None, :]
    first_half = head_rows[..., :half_dim]
    second_half = head_rows[..., half_dim:]
    return jnp.concatenate(
        [
            first_half * cosine - second_half * sine_part,
            second_half * cosine + first_half * sine_part,
        ],
        axis=-1,
    )


def fresh_state(tok_count):
    return (
        jnp.full((KV, H // KV, tok_count), -jnp.inf, jnp.float32),
        jnp.zeros((KV, H // KV, tok_count), jnp.float32),
        jnp.zeros((KV, H // KV, tok_count, HD), jnp.float32),
    )


def absorb(run_state, grouped, key_rows, value_rows, visible):
    run_max, run_sum, run_acc = run_state
    scores = (
        jnp.einsum("tkgd,skd->kgts", grouped, key_rows, preferred_element_type=jnp.float32)
        * ATTN_SCALE
    )
    scores = jnp.where(visible, scores, -jnp.inf)
    new_max = jnp.maximum(run_max, jnp.max(scores, axis=-1))
    factor = jnp.exp(run_max - new_max)
    weights = jnp.exp(scores - new_max[..., None])
    run_sum = run_sum * factor + jnp.sum(weights, axis=-1)
    gathered_values = jnp.einsum(
        "kgts,skd->kgtd",
        weights.astype(jnp.bfloat16),
        value_rows,
        preferred_element_type=jnp.float32,
    )
    run_acc = run_acc * factor[..., None] + gathered_values
    return (new_max, run_sum, run_acc)


def slot_numbers(ids):
    chosen = ids.reshape(-1)
    hit_table = (chosen[:, None] == jnp.arange(EXPERTS, dtype=jnp.int32)[None, :]).astype(jnp.int32)
    before = jnp.cumsum(hit_table, axis=0) - hit_table
    ranked = jnp.sum(before * hit_table, axis=1)
    return (chosen, ranked)


def local_general(
    tokens,
    attn_gain,
    w_query,
    w_key,
    w_value,
    w_out,
    prefix_keys,
    prefix_values,
    lengths,
    assignment,
    moe_gain,
    expert_ids,
    route_weights,
    w_gate,
    w_up,
    w_down,
):
    tok_count = tokens.shape[1]
    model_width = tokens.shape[2]
    peer_count = lax.axis_size("req")
    prefix_len = prefix_keys.shape[1] * peer_count
    own_rows = tokens[0]
    normed = normalize(own_rows, attn_gain)
    my_index = lax.axis_index("req")
    request_ids = jnp.arange(lengths.shape[1], dtype=jnp.int32)
    request = jnp.sum(jnp.where(request_ids == my_index, assignment[0], 0))
    suffix_len = jnp.sum(jnp.where(request_ids == request, lengths[0], 0))
    positions = (prefix_len + jnp.arange(tok_count, dtype=jnp.int32)).astype(jnp.float32)
    queries = jnp.dot(normed, w_query, preferred_element_type=jnp.float32).reshape(tok_count, H, HD)
    queries = rotate(queries, positions).astype(jnp.bfloat16)
    suffix_keys = jnp.dot(normed, w_key, preferred_element_type=jnp.float32).reshape(
        tok_count, KV, HD
    )
    suffix_keys = rotate(suffix_keys, positions).astype(jnp.bfloat16)
    suffix_values = (
        jnp.dot(normed, w_value, preferred_element_type=jnp.float32)
        .astype(jnp.bfloat16)
        .reshape(tok_count, KV, HD)
    )
    grouped = queries.reshape(tok_count, KV, H // KV, HD)
    slot_row = jnp.arange(tok_count, dtype=jnp.int32)
    suffix_visible = (slot_row[None, :] <= slot_row[:, None]) & (slot_row[None, :] < suffix_len)
    suffix_state = absorb(
        fresh_state(tok_count), grouped, suffix_keys, suffix_values, suffix_visible[None, None]
    )
    run_state = suffix_state
    key_piece = lax.all_gather(prefix_keys, "req", axis=1, tiled=True)
    value_piece = lax.all_gather(prefix_values, "req", axis=1, tiled=True)
    piece_len = key_piece.shape[1]
    key_block = math.gcd(piece_len, 512)
    key_blocks = key_piece[0].reshape(piece_len // key_block, key_block, KV, HD)
    value_blocks = value_piece[0].reshape(piece_len // key_block, key_block, KV, HD)

    def absorb_step(carry, pair_set):
        return (absorb(carry, grouped, pair_set[0], pair_set[1], True), None)

    run_state, unused = lax.scan(absorb_step, run_state, (key_blocks, value_blocks))
    run_max, run_sum, run_acc = run_state
    context = (
        (run_acc / run_sum[..., None])
        .transpose(2, 0, 1, 3)
        .reshape(tok_count, H * HD)
        .astype(jnp.bfloat16)
    )
    projected = jnp.dot(context, w_out, preferred_element_type=jnp.float32)
    hidden = (own_rows.astype(jnp.float32) + RESIDUAL_SCALE * projected).astype(jnp.bfloat16)
    moe_in = normalize(hidden, moe_gain)
    chosen, ranked = slot_numbers(expert_ids[0])
    slot_index = chosen * CAP + ranked
    sources = jnp.repeat(moe_in, TOP, axis=0)
    outgoing = jnp.zeros((EXPERTS * CAP, model_width), jnp.bfloat16).at[slot_index].set(sources)
    outgoing = outgoing.reshape(peer_count, EXPERTS // peer_count, CAP, model_width)
    arrived = lax.all_to_all(outgoing, "req", split_axis=0, concat_axis=0, tiled=True)
    slot_span = arrived.shape[2]
    results = []
    for expert_local in range(arrived.shape[1]):
        expert_rows = arrived[:, expert_local].reshape(-1, model_width)
        gate_act = jnp.dot(expert_rows, w_gate[expert_local], preferred_element_type=jnp.float32)
        up_act = jnp.dot(expert_rows, w_up[expert_local], preferred_element_type=jnp.float32)
        product = (jax.nn.silu(gate_act) * up_act).astype(jnp.bfloat16)
        expert_out = jnp.dot(
            product, w_down[expert_local], preferred_element_type=jnp.float32
        ).astype(jnp.bfloat16)
        results.append(expert_out.reshape(arrived.shape[0], slot_span, model_width))
    produced = jnp.stack(results, axis=1)
    returned = lax.all_to_all(produced, "req", split_axis=0, concat_axis=0, tiled=True).reshape(
        EXPERTS * CAP, model_width
    )
    picked = returned[slot_index].astype(jnp.float32).reshape(tok_count, TOP, model_width)
    expert_mix = jnp.sum(picked * route_weights[0][..., None], axis=1).astype(jnp.bfloat16)
    return (context[None], hidden[None], expert_mix[None])


F32 = jnp.float32
BF16 = jnp.bfloat16
MIB = 1 << 20
LANES = 128
VMEM_ATTEND = 30
VMEM_LAST = 26
VMEM_NEAR = 30
NOTE_ROWS = 16
VMEM_EXPERTS = 17


def dot(lhs, rhs):
    return jnp.dot(lhs, rhs, preferred_element_type=F32)


def dot_nt(lhs, rhs):
    return lax.dot_general(lhs, rhs, (((1,), (1,)), ((), ())), preferred_element_type=F32)


def dot_tn(lhs, rhs):
    return lax.dot_general(lhs, rhs, (((0,), (0,)), ((), ())), preferred_element_type=F32)


def held_in_hbm(arrays):
    return [pltpu.with_memory_space_constraint(array, pltpu.HBM) for array in arrays]


def held_in_vmem(arrays):
    return [pltpu.with_memory_space_constraint(array, pltpu.VMEM) for array in arrays]


def lane_index(shape):
    return lax.broadcasted_iota(jnp.int32, shape, len(shape) - 1)


def rope_tables(prefix_len, tok_count):
    frequency = ROPE_BASE ** (-(np.arange(HD // 2, dtype=np.float64) * 2.0 / HD))
    angles = (prefix_len + np.arange(tok_count, dtype=np.float64))[:, None] * frequency[None, :]
    cosine, sine = np.cos(angles), np.sin(angles)
    cosine = np.concatenate([cosine, cosine, cosine, cosine], axis=1)
    sine = np.concatenate([-sine, sine, -sine, sine], axis=1)
    return jnp.asarray(cosine, F32), jnp.asarray(sine, F32)


def rotate_tile(tile, cosine, sine):
    first = lane_index(tile.shape) % HD < HD // 2
    other = jnp.where(
        first, pltpu.roll(tile, LANES - HD // 2, 1), pltpu.roll(tile, HD // 2, 1)
    )
    return tile * cosine + other * sine


SUM_ROWS = 16


def attend_heads(queries, key_tiles, value_tiles, suffix_len, states):
    heads = len(queries)
    tok_count = queries[0].shape[0] // 2
    turned = [[tile.astype(F32).T.astype(BF16) for tile in tiles] for tiles in value_tiles]
    ones = jnp.ones((SUM_ROWS, turned[0][0].shape[1]), BF16)

    def scores_of(head):
        scores = [dot_nt(tile, queries[head]) for tile in key_tiles[head // 2]]
        if suffix_len is not None:
            shape = scores[0].shape
            slot = lax.broadcasted_iota(jnp.int32, shape, 0)
            row = lane_index(shape) % tok_count
            visible = (slot <= row) & (slot < suffix_len)
            scores[0] = jnp.where(visible, scores[0], -1e30)
        return scores

    results = []
    ahead = scores_of(0)
    for head in range(heads):
        scores, ahead = ahead, scores_of(head + 1) if head + 1 < heads else None
        new_max = jnp.max(functools.reduce(jnp.maximum, scores), axis=0, keepdims=True)
        total = None
        if states is not None:
            old_max, old_total = states[head]
            new_max = jnp.maximum(new_max, old_max)
            total = old_total * jnp.exp(old_max - new_max)
        first_row = head % 2 * HD
        for score, tile in zip(scores, turned[head // 2]):
            weights = jnp.exp(score - new_max).astype(BF16)
            part = dot(jnp.concatenate([tile[first_row : first_row + HD], ones], axis=0), weights)
            total = part if total is None else total + part
        results.append((new_max, total))
    return results


def pair_tiles(refs):
    pairs = refs[0].shape[1] // LANES
    return [[ref[:, pair * LANES : (pair + 1) * LANES] for ref in refs] for pair in range(pairs)]


def near_kernel(*refs):
    tok_ref, gain_ref, *held = refs[:5]
    cos_ref, sin_ref, lengths_ref, order_ref, keys_ref, values_ref, mate_keys_ref, mate_values_ref = refs[5:13]
    q_ref, max_ref, acc_ref = refs[13:]
    suffix_len = lengths_ref[0, order_ref[0, lax.axis_index("req")]]
    rows = tok_ref[...].astype(F32)
    mean_square = jnp.mean(rows * rows, axis=-1, keepdims=True)
    normed = (rows * lax.rsqrt(mean_square + NORM_EPS) * gain_ref[...]).astype(BF16)
    cosine, sine = cos_ref[...], sin_ref[...]
    low = lane_index(cosine.shape) < HD
    queries, key_tiles, value_tiles = [], [], []
    for pair in range(KV // 2):
        lanes = slice(pair * LANES, (pair + 1) * LANES)
        suffix_keys = rotate_tile(dot(normed, held[1][:, lanes]), cosine, sine).astype(BF16)
        suffix_values = dot(normed, held[2][:, lanes]).astype(BF16)
        key_tiles.append([suffix_keys, keys_ref[:, lanes], mate_keys_ref[:, lanes]])
        value_tiles.append([suffix_values, values_ref[:, lanes], mate_values_ref[:, lanes]])
        projected = dot(normed, held[0][:, 2 * pair * LANES : 2 * (pair + 1) * LANES])
        for half in range(2):
            tile = rotate_tile(projected[:, half * LANES : (half + 1) * LANES], cosine, sine) * ATTN_SCALE
            turned = pltpu.roll(tile, HD, 1)
            if half == 0:
                first, second = jnp.where(low, tile, 0.0), jnp.where(low, turned, 0.0)
            else:
                first, second = jnp.where(low, 0.0, turned), jnp.where(low, 0.0, tile)
            queries.append(jnp.concatenate([first, second], axis=0).astype(BF16))
            q_ref[2 * pair + half] = queries[-1]
    results = attend_heads(queries, key_tiles, value_tiles, suffix_len, None)
    for head, (new_max, total) in enumerate(results):
        max_ref[head] = new_max
        acc_ref[head] = total


def whole_spec(*shape):
    return pl.BlockSpec(shape, lambda i: (0,) * len(shape))


def cached_specs(cached):
    specs = []
    for kind in range(2):
        for array in cached:
            stacked = not isinstance(array, tuple)
            length = array.shape[0] // 2 if stacked else array[0].shape[0]
            place = kind if stacked else 0
            specs.append(pl.BlockSpec((length, KV * HD), lambda i, place=place: (place, 0)))
    return specs


def cached_args(cached):
    return [array[kind] if isinstance(array, tuple) else array for kind in range(2) for array in cached]


def attend_near(own_rows, attn_gain, w_query, w_key, w_value, prefix_len, lengths, assignment, keys, values, mate):
    tok_count, width = own_rows.shape
    rows, block = 2 * tok_count, keys.shape[0]
    cosine, sine = rope_tables(prefix_len, tok_count)
    smem = pl.BlockSpec(memory_space=pltpu.SMEM)
    queries, *state = pl.pallas_call(
        near_kernel,
        grid=(1,),
        in_specs=[whole_spec(tok_count, width), whole_spec(1, width)]
        + [whole_spec(*array.shape) for array in (w_query, w_key, w_value)]
        + [whole_spec(tok_count, LANES)] * 2
        + [smem, smem]
        + [whole_spec(block, KV * HD)] * 4,
        out_specs=[whole_spec(KV, rows, LANES), whole_spec(KV, 1, rows), whole_spec(KV, HD + SUM_ROWS, rows)],
        out_shape=[
            pltpu.VMEM((KV, rows, LANES), BF16),
            pltpu.VMEM((KV, 1, rows), F32),
            pltpu.VMEM((KV, HD + SUM_ROWS, rows), F32),
        ],
        compiler_params=pltpu.CompilerParams(vmem_limit_bytes=VMEM_NEAR * MIB),
        cost_estimate=pl.CostEstimate(flops=4000 * MIB, bytes_accessed=6 * MIB, transcendentals=0),
        name="attend_near",
    )(
        *held_in_hbm([own_rows, attn_gain.reshape(1, width), w_query, w_key, w_value, cosine, sine]),
        *held_in_hbm([lengths, assignment, keys, values]),
        *held_in_vmem(mate),
    )
    return queries, state


def far_kernel(blocks, last, *refs):
    q_ref, max_in, acc_in = refs[:3]
    key_refs, value_refs = refs[3 : 3 + blocks], refs[3 + blocks : 3 + 2 * blocks]
    refs = refs[3 + 2 * blocks :]
    heads = q_ref.shape[0]
    states = [(max_in[head], acc_in[head]) for head in range(heads)]
    queries = [q_ref[head] for head in range(heads)]
    results = attend_heads(queries, pair_tiles(key_refs), pair_tiles(value_refs), None, states)
    if not last:
        max_ref, acc_ref = refs
        for half, (new_max, total) in enumerate(results):
            max_ref[half] = new_max
            acc_ref[half] = total
        return
    tok_ref, w_out_ref, gain_ref, ids_ref, route_ref, ctx_ref, hidden_ref, moe_ref = refs
    tok_count = tok_ref.shape[0]
    tiles = []
    for _, total in results:
        mixed = total[:HD] / total[HD : HD + 1]
        tiles.append(jnp.concatenate([mixed[:, :tok_count], mixed[:, tok_count:]], axis=0).T)
    context = jnp.concatenate(tiles, axis=1).astype(BF16)
    ctx_ref[...] = context
    projected = dot(context, w_out_ref[...])
    hidden = (tok_ref[...].astype(F32) + RESIDUAL_SCALE * projected).astype(BF16)
    hidden_ref[...] = hidden
    wide = hidden.astype(F32)
    mean_square = jnp.mean(wide * wide, axis=-1, keepdims=True)
    moe_ref[:tok_count] = (wide * lax.rsqrt(mean_square + NORM_EPS) * gain_ref[...]).astype(BF16)
    moe_ref[tok_count:] = jnp.zeros((NOTE_ROWS, wide.shape[1]), BF16)
    moe_ref[tok_count : tok_count + TOP, :tok_count] = ids_ref[...].astype(F32).astype(BF16)
    moe_ref[tok_count : tok_count + TOP, tok_count : 2 * tok_count] = route_ref[...].astype(BF16)


def attend_far(queries, state, cached, final=None):
    last, blocks, rows = final is not None, len(cached), queries.shape[1]
    tok_count = rows // 2
    args, tiles = [queries, *state], held_in_vmem(cached_args(cached))
    in_specs = [whole_spec(KV, rows, LANES), whole_spec(KV, 1, rows), whole_spec(KV, HD + SUM_ROWS, rows)]
    in_specs += cached_specs(cached)
    if last:
        own_rows, w_out, moe_gain, expert_ids, route_weights = final
        width = own_rows.shape[1]
        own_args = [own_rows, w_out, moe_gain.reshape(1, width), expert_ids.T, route_weights.T]
        whole = whole_spec(tok_count, width)
        in_specs += [whole, whole_spec(*w_out.shape), whole_spec(1, width)]
        in_specs += [whole_spec(TOP, tok_count)] * 2
        out_specs = [whole, whole, whole_spec(tok_count + NOTE_ROWS, width)]
        out_shape = [pltpu.HBM((tok_count, width), BF16)] * 2 + [pltpu.VMEM((tok_count + NOTE_ROWS, width), BF16)]
    else:
        own_args = []
        out_specs = in_specs[1:3]
        out_shape = [pltpu.VMEM(array.shape, F32) for array in state]
    return pl.pallas_call(
        functools.partial(far_kernel, blocks, last),
        grid=(1,),
        in_specs=in_specs,
        out_specs=out_specs,
        out_shape=out_shape,
        compiler_params=pltpu.CompilerParams(vmem_limit_bytes=(VMEM_LAST if last else VMEM_ATTEND) * MIB),
        cost_estimate=pl.CostEstimate(flops=blocks * 1200 * MIB, bytes_accessed=4 * MIB, transcendentals=0),
        name="attend_far",
    )(*held_in_vmem(args), *tiles, *held_in_hbm(own_args))


def experts_kernel(sources, pieces, owners, load, *refs):
    refs = list(refs)
    take = lambda n: [refs.pop(0) for _ in range(n)]
    row_refs = [take(pieces) for _ in range(sources)]
    weight_refs = [take(3) for _ in owners]
    out_refs = take(sources)
    held = [take(3) for _ in owners] if load else weight_refs
    picked_ref, made_ref, combine_ref, *sems = refs
    local_experts = held[0][0].shape[0]
    experts = len(owners) * local_experts
    tok_count, width = out_refs[0].shape
    slots = experts * CAP
    me = lax.axis_index("req")
    firsts = [(me + owner * (1 - 2 * lax.rem(me, 2))) * local_experts for owner in owners]

    def copy(group, kind, e):
        return pltpu.make_async_copy(
            weight_refs[group][kind].at[e], held[group][kind].at[e], sems[0].at[group, kind, e]
        )

    for group in range(len(owners) if load else 0):
        for e in range(local_experts):
            for kind in range(3):
                copy(group, kind, e).start()

    before = lax.broadcasted_iota(jnp.int32, (tok_count, tok_count), 0)
    after = lane_index((tok_count, tok_count))
    earlier = jnp.where(before < after, 1.0, 0.0).astype(BF16)
    slot = lax.broadcasted_iota(jnp.int32, (slots, EXPERTS), 0) // CAP
    held_here = slot + firsts[0]
    if len(owners) > 1:
        held_here = jnp.where(slot < local_experts, held_here, slot + (firsts[1] - local_experts))
    spread = jnp.where(held_here == lane_index((slots, EXPERTS)), 1.0, 0.0).astype(BF16)
    within = (lax.broadcasted_iota(jnp.int32, (slots, tok_count), 0) % CAP).astype(F32)
    expert_row = lax.broadcasted_iota(jnp.int32, (EXPERTS, tok_count), 0).astype(F32)
    for source in range(sources):
        message = jnp.concatenate([ref[...] for ref in row_refs[source]], axis=0)
        rows, note = message[:tok_count], message[tok_count:].astype(F32)
        route = jnp.zeros((EXPERTS, tok_count), F32)
        for k in range(TOP):
            chosen, gain = note[k : k + 1, :tok_count], note[k : k + 1, tok_count : 2 * tok_count]
            route = jnp.where(chosen == expert_row, gain, route)
        hit = route > 0.0
        ranked = dot(jnp.where(hit, 1.0, 0.0).astype(BF16), earlier)
        ranked = jnp.where(hit, ranked, -1.0).astype(BF16)
        match = dot(spread, ranked) == within
        pick = jnp.where(match, 1.0, 0.0).astype(BF16)
        combine_ref[source] = jnp.where(match, dot(spread, route.astype(BF16)), 0.0).astype(BF16)
        picked = dot(pick, rows).astype(BF16)
        for e in range(experts):
            picked_ref[e, source] = picked[e * CAP : (e + 1) * CAP]

    def one_expert(group, e, carry):
        for kind in range(3 if load else 0):
            copy(group, kind, e).wait()
        expert = group * local_experts + e
        rows = picked_ref[expert].reshape(sources * CAP, width)
        gate = dot(rows, held[group][0][e])
        up = dot(rows, held[group][1][e])
        act = (jax.nn.silu(gate) * up).astype(BF16)
        made = dot(act, held[group][2][e]).astype(BF16)
        for source in range(sources):
            made_ref[source, pl.ds(pl.multiple_of(expert * CAP, CAP), CAP), :] = made[
                source * CAP : (source + 1) * CAP
            ]
        return carry

    for group in range(len(owners)):
        lax.fori_loop(0, local_experts, functools.partial(one_expert, group), 0, unroll=4)
    for source, ref in enumerate(out_refs):
        ref[...] = dot_tn(combine_ref[source], made_ref[source]).astype(ref.dtype)


def run_experts(rows, weights, owners=(0, 1), load=False, out_type=BF16):
    sources, pieces = len(rows), len(rows[0])
    tok_count, width = sum(piece.shape[0] for piece in rows[0]) - NOTE_ROWS, rows[0][0].shape[1]
    vmem = pl.BlockSpec(memory_space=pltpu.VMEM)
    weight_args = [array for owned in weights for array in owned]
    local_experts = weight_args[0].shape[0]
    experts = len(owners) * local_experts
    out_shape = [pltpu.VMEM((tok_count, width), out_type)] * sources
    if load:
        out_shape = out_shape + [pltpu.VMEM(array.shape, BF16) for array in weight_args]
        weight_args, weight_specs = held_in_hbm(weight_args), [pl.BlockSpec(memory_space=pl.ANY)] * len(weight_args)
        semaphores = [pltpu.SemaphoreType.DMA((len(owners), 3, local_experts))]
    else:
        weight_args, weight_specs, semaphores = held_in_vmem(weight_args), [vmem] * len(weight_args), []
    return pl.pallas_call(
        functools.partial(experts_kernel, sources, pieces, owners, load),
        in_specs=[vmem] * (pieces * sources) + weight_specs,
        out_specs=[vmem] * len(out_shape),
        out_shape=out_shape,
        scratch_shapes=[
            pltpu.VMEM((experts, sources, CAP, width), BF16),
            pltpu.VMEM((sources, experts * CAP, width), BF16),
            pltpu.VMEM((sources, experts * CAP, tok_count), BF16),
            *semaphores,
        ],
        compiler_params=pltpu.CompilerParams(vmem_limit_bytes=VMEM_EXPERTS * MIB),
        cost_estimate=pl.CostEstimate(flops=12000 * MIB, bytes_accessed=30 * MIB, transcendentals=0),
        name="experts",
    )(*held_in_vmem([piece for source in rows for piece in source]), *weight_args)


CORE, ACROSS_X, ACROSS_Y = 1, 2, 4


def swap(array, mask):
    return lax.ppermute(array, "req", [(i, i ^ mask) for i in range(lax.axis_size("req"))])


def ordered(*arrays):
    return lax.optimization_barrier(arrays)


def local_chips(
    tokens,
    attn_gain,
    w_query,
    w_key,
    w_value,
    w_out,
    prefix_keys,
    prefix_values,
    lengths,
    assignment,
    moe_gain,
    expert_ids,
    route_weights,
    w_gate,
    w_up,
    w_down,
):
    peer_count = lax.axis_size("req")
    own_rows = tokens[0]
    tok_count = own_rows.shape[0]
    prefix_len = prefix_keys.shape[1] * peer_count
    keys, values = prefix_keys[0], prefix_values[0]
    block = keys.shape[0]
    keys_x, values_y = swap(keys, ACROSS_X), swap(values, ACROSS_Y)
    values_x, keys_y = swap(values, ACROSS_X), swap(keys, ACROSS_Y)
    cached_mate = (swap(keys, CORE), swap(values, CORE))

    queries, state = attend_near(
        own_rows, attn_gain, w_query, w_key, w_value, prefix_len, lengths, assignment, keys, values, cached_mate
    )
    keys_x, values_x, keys_y, values_y, *state = ordered(keys_x, values_x, keys_y, values_y, *state)
    far = [swap(keys_x, ACROSS_Y), swap(values_y, ACROSS_X)]
    mates = [swap(array, CORE) for array in (keys_x, values_x, keys_y, values_y)]
    *mates, w_gate = ordered(*mates, w_gate)
    gate = (w_gate, swap(w_gate, CORE))
    near = [(keys_x, values_x), (keys_y, values_y), tuple(mates[:2]), tuple(mates[2:])]
    state = attend_far(queries, state, near)
    *far, gate, s0, s1 = ordered(*far, gate, *state)
    far_mate = [swap(array, CORE) for array in far]
    *far_mate, w_up, w_down = ordered(*far_mate, w_up, w_down)
    up, down = (w_up, swap(w_up, CORE)), (w_down, swap(w_down, CORE))
    context, hidden, moe_in = attend_far(
        queries,
        [s0, s1],
        [tuple(far), tuple(far_mate)],
        final=(own_rows, w_out, moe_gain, expert_ids[0], route_weights[0]),
    )

    owned, mated = zip(gate, up, down)
    half = tok_count // 2
    rows_x, rows_y = swap(moe_in, ACROSS_X), swap(moe_in, ACROSS_Y)
    weights = [list(owned), list(mated)]
    (own,) = run_experts([[moe_in]], weights, out_type=F32)
    rows_x, rows_y, own = ordered(rows_x, rows_y, own)
    low_xy, high_xy = swap(rows_x[:half], ACROSS_Y), swap(rows_y[half:], ACROSS_X)
    to_x, to_y = run_experts([[rows_x], [rows_y]], weights)
    low_xy, high_xy, to_x, to_y = ordered(low_xy, high_xy, to_x, to_y)
    from_x, from_y = swap(to_x, ACROSS_X), swap(to_y, ACROSS_Y)
    (to_xy,) = run_experts([[low_xy, high_xy]], weights)
    from_xy = swap(to_xy, ACROSS_X | ACROSS_Y)
    partial, from_xy = ordered(own + from_x.astype(F32) + from_y.astype(F32), from_xy)
    expert_mix = (partial + from_xy.astype(F32)).astype(BF16)
    return (context[None], hidden[None], expert_mix[None])


def solution(mesh):
    placed = (
        P("grp", "req", None),
        P(),
        P(),
        P(),
        P(),
        P(),
        P("grp", "req", None),
        P("grp", "req", None),
        P("grp", None),
        P("grp", None),
        P(),
        P("grp", "req", None),
        P("grp", "req", None),
        P("req", None, None),
        P("req", None, None),
        P("req", None, None),
    )
    return jax.shard_map(
        local_chips if mesh.shape["req"] == 8 else local_general,
        mesh=mesh,
        in_specs=placed,
        out_specs=(P("grp", "req", None), P("grp", "req", None), P("grp", "req", None)),
        check_vma=False,
    )
```

```python
import functools
import math

import jax
import jax.numpy as jnp
import numpy as np
from jax import lax
from jax.experimental import pallas as pl
from jax.experimental.pallas import tpu as pltpu
from jax.sharding import PartitionSpec as P

H = 16
KV = 8
HD = 64
EXPERTS = 32
TOP = 8
CAP = 96


NORM_EPS = 1e-06
ATTN_SCALE = 0.015625
RESIDUAL_SCALE = 0.22
ROPE_BASE = 10000.0


def normalize(head_rows, gain):
    widened = head_rows.astype(jnp.float32)
    mean_square = jnp.mean(widened * widened, axis=-1, keepdims=True)
    return (widened * lax.rsqrt(mean_square + NORM_EPS) * gain).astype(jnp.bfloat16)


def rotate(head_rows, positions):
    half_dim = head_rows.shape[-1] // 2
    frequency = ROPE_BASE ** (
        -(jnp.arange(half_dim, dtype=jnp.float32) * 2.0 / head_rows.shape[-1])
    )
    angles = positions[:, None] * frequency[None, :]
    cosine = jnp.cos(angles)[:, None, :]
    sine_part = jnp.sin(angles)[:, None, :]
    first_half = head_rows[..., :half_dim]
    second_half = head_rows[..., half_dim:]
    return jnp.concatenate(
        [
            first_half * cosine - second_half * sine_part,
            second_half * cosine + first_half * sine_part,
        ],
        axis=-1,
    )


def fresh_state(tok_count):
    return (
        jnp.full((KV, H // KV, tok_count), -jnp.inf, jnp.float32),
        jnp.zeros((KV, H // KV, tok_count), jnp.float32),
        jnp.zeros((KV, H // KV, tok_count, HD), jnp.float32),
    )


def absorb(run_state, grouped, key_rows, value_rows, visible):
    run_max, run_sum, run_acc = run_state
    scores = (
        jnp.einsum("tkgd,skd->kgts", grouped, key_rows, preferred_element_type=jnp.float32)
        * ATTN_SCALE
    )
    scores = jnp.where(visible, scores, -jnp.inf)
    new_max = jnp.maximum(run_max, jnp.max(scores, axis=-1))
    factor = jnp.exp(run_max - new_max)
    weights = jnp.exp(scores - new_max[..., None])
    run_sum = run_sum * factor + jnp.sum(weights, axis=-1)
    gathered_values = jnp.einsum(
        "kgts,skd->kgtd",
        weights.astype(jnp.bfloat16),
        value_rows,
        preferred_element_type=jnp.float32,
    )
    run_acc = run_acc * factor[..., None] + gathered_values
    return (new_max, run_sum, run_acc)


def slot_numbers(ids):
    chosen = ids.reshape(-1)
    hit_table = (chosen[:, None] == jnp.arange(EXPERTS, dtype=jnp.int32)[None, :]).astype(jnp.int32)
    before = jnp.cumsum(hit_table, axis=0) - hit_table
    ranked = jnp.sum(before * hit_table, axis=1)
    return (chosen, ranked)


def local_general(
    tokens,
    attn_gain,
    w_query,
    w_key,
    w_value,
    w_out,
    prefix_keys,
    prefix_values,
    lengths,
    assignment,
    moe_gain,
    expert_ids,
    route_weights,
    w_gate,
    w_up,
    w_down,
):
    tok_count = tokens.shape[1]
    model_width = tokens.shape[2]
    peer_count = lax.axis_size("req")
    prefix_len = prefix_keys.shape[1] * peer_count
    own_rows = tokens[0]
    normed = normalize(own_rows, attn_gain)
    my_index = lax.axis_index("req")
    request_ids = jnp.arange(lengths.shape[1], dtype=jnp.int32)
    request = jnp.sum(jnp.where(request_ids == my_index, assignment[0], 0))
    suffix_len = jnp.sum(jnp.where(request_ids == request, lengths[0], 0))
    positions = (prefix_len + jnp.arange(tok_count, dtype=jnp.int32)).astype(jnp.float32)
    queries = jnp.dot(normed, w_query, preferred_element_type=jnp.float32).reshape(tok_count, H, HD)
    queries = rotate(queries, positions).astype(jnp.bfloat16)
    suffix_keys = jnp.dot(normed, w_key, preferred_element_type=jnp.float32).reshape(
        tok_count, KV, HD
    )
    suffix_keys = rotate(suffix_keys, positions).astype(jnp.bfloat16)
    suffix_values = (
        jnp.dot(normed, w_value, preferred_element_type=jnp.float32)
        .astype(jnp.bfloat16)
        .reshape(tok_count, KV, HD)
    )
    grouped = queries.reshape(tok_count, KV, H // KV, HD)
    slot_row = jnp.arange(tok_count, dtype=jnp.int32)
    suffix_visible = (slot_row[None, :] <= slot_row[:, None]) & (slot_row[None, :] < suffix_len)
    suffix_state = absorb(
        fresh_state(tok_count), grouped, suffix_keys, suffix_values, suffix_visible[None, None]
    )
    run_state = suffix_state
    key_piece = lax.all_gather(prefix_keys, "req", axis=1, tiled=True)
    value_piece = lax.all_gather(prefix_values, "req", axis=1, tiled=True)
    piece_len = key_piece.shape[1]
    key_block = math.gcd(piece_len, 512)
    key_blocks = key_piece[0].reshape(piece_len // key_block, key_block, KV, HD)
    value_blocks = value_piece[0].reshape(piece_len // key_block, key_block, KV, HD)

    def absorb_step(carry, pair_set):
        return (absorb(carry, grouped, pair_set[0], pair_set[1], True), None)

    run_state, unused = lax.scan(absorb_step, run_state, (key_blocks, value_blocks))
    run_max, run_sum, run_acc = run_state
    context = (
        (run_acc / run_sum[..., None])
        .transpose(2, 0, 1, 3)
        .reshape(tok_count, H * HD)
        .astype(jnp.bfloat16)
    )
    projected = jnp.dot(context, w_out, preferred_element_type=jnp.float32)
    hidden = (own_rows.astype(jnp.float32) + RESIDUAL_SCALE * projected).astype(jnp.bfloat16)
    moe_in = normalize(hidden, moe_gain)
    chosen, ranked = slot_numbers(expert_ids[0])
    slot_index = chosen * CAP + ranked
    sources = jnp.repeat(moe_in, TOP, axis=0)
    outgoing = jnp.zeros((EXPERTS * CAP, model_width), jnp.bfloat16).at[slot_index].set(sources)
    outgoing = outgoing.reshape(peer_count, EXPERTS // peer_count, CAP, model_width)
    arrived = lax.all_to_all(outgoing, "req", split_axis=0, concat_axis=0, tiled=True)
    slot_span = arrived.shape[2]
    results = []
    for expert_local in range(arrived.shape[1]):
        expert_rows = arrived[:, expert_local].reshape(-1, model_width)
        gate_act = jnp.dot(expert_rows, w_gate[expert_local], preferred_element_type=jnp.float32)
        up_act = jnp.dot(expert_rows, w_up[expert_local], preferred_element_type=jnp.float32)
        product = (jax.nn.silu(gate_act) * up_act).astype(jnp.bfloat16)
        expert_out = jnp.dot(
            product, w_down[expert_local], preferred_element_type=jnp.float32
        ).astype(jnp.bfloat16)
        results.append(expert_out.reshape(arrived.shape[0], slot_span, model_width))
    produced = jnp.stack(results, axis=1)
    returned = lax.all_to_all(produced, "req", split_axis=0, concat_axis=0, tiled=True).reshape(
        EXPERTS * CAP, model_width
    )
    picked = returned[slot_index].astype(jnp.float32).reshape(tok_count, TOP, model_width)
    expert_mix = jnp.sum(picked * route_weights[0][..., None], axis=1).astype(jnp.bfloat16)
    return (context[None], hidden[None], expert_mix[None])


F32 = jnp.float32
BF16 = jnp.bfloat16
MIB = 1 << 20
LANES = 128
VMEM_ATTEND = 30
VMEM_LAST = 26
VMEM_NEAR = 30
NOTE_ROWS = 16
VMEM_EXPERTS = 17


def dot(lhs, rhs):
    return jnp.dot(lhs, rhs, preferred_element_type=F32)


def dot_nt(lhs, rhs):
    return lax.dot_general(lhs, rhs, (((1,), (1,)), ((), ())), preferred_element_type=F32)


def dot_tn(lhs, rhs):
    return lax.dot_general(lhs, rhs, (((0,), (0,)), ((), ())), preferred_element_type=F32)


def held_in_hbm(arrays):
    return [pltpu.with_memory_space_constraint(array, pltpu.HBM) for array in arrays]


def held_in_vmem(arrays):
    return [pltpu.with_memory_space_constraint(array, pltpu.VMEM) for array in arrays]


def lane_index(shape):
    return lax.broadcasted_iota(jnp.int32, shape, len(shape) - 1)


def rope_tables(prefix_len, tok_count):
    frequency = ROPE_BASE ** (-(np.arange(HD // 2, dtype=np.float64) * 2.0 / HD))
    angles = (prefix_len + np.arange(tok_count, dtype=np.float64))[:, None] * frequency[None, :]
    cosine, sine = np.cos(angles), np.sin(angles)
    cosine = np.concatenate([cosine, cosine, cosine, cosine], axis=1)
    sine = np.concatenate([-sine, sine, -sine, sine], axis=1)
    return jnp.asarray(cosine, F32), jnp.asarray(sine, F32)


def rotate_tile(tile, cosine, sine):
    first = lane_index(tile.shape) % HD < HD // 2
    other = jnp.where(
        first, pltpu.roll(tile, LANES - HD // 2, 1), pltpu.roll(tile, HD // 2, 1)
    )
    return tile * cosine + other * sine


SUM_ROWS = 16


def attend_heads(queries, key_tiles, value_tiles, suffix_len, states):
    heads = len(queries)
    tok_count = queries[0].shape[0] // 2
    turned = [[tile.astype(F32).T.astype(BF16) for tile in tiles] for tiles in value_tiles]
    ones = jnp.ones((SUM_ROWS, turned[0][0].shape[1]), BF16)

    def scores_of(head):
        scores = [dot_nt(tile, queries[head]) for tile in key_tiles[head // 2]]
        if suffix_len is not None:
            shape = scores[0].shape
            slot = lax.broadcasted_iota(jnp.int32, shape, 0)
            row = lane_index(shape) % tok_count
            visible = (slot <= row) & (slot < suffix_len)
            scores[0] = jnp.where(visible, scores[0], -1e30)
        return scores

    results = []
    ahead = scores_of(0)
    for head in range(heads):
        scores, ahead = ahead, scores_of(head + 1) if head + 1 < heads else None
        new_max = jnp.max(functools.reduce(jnp.maximum, scores), axis=0, keepdims=True)
        total = None
        if states is not None:
            old_max, old_total = states[head]
            new_max = jnp.maximum(new_max, old_max)
            total = old_total * jnp.exp(old_max - new_max)
        first_row = head % 2 * HD
        for score, tile in zip(scores, turned[head // 2]):
            weights = jnp.exp(score - new_max).astype(BF16)
            part = dot(jnp.concatenate([tile[first_row : first_row + HD], ones], axis=0), weights)
            total = part if total is None else total + part
        results.append((new_max, total))
    return results


def pair_tiles(refs):
    pairs = refs[0].shape[1] // LANES
    return [[ref[:, pair * LANES : (pair + 1) * LANES] for ref in refs] for pair in range(pairs)]


def near_kernel(*refs):
    tok_ref, gain_ref, *held = refs[:5]
    cos_ref, sin_ref, lengths_ref, order_ref, keys_ref, values_ref, mate_keys_ref, mate_values_ref = refs[5:13]
    q_ref, max_ref, acc_ref = refs[13:]
    suffix_len = lengths_ref[0, order_ref[0, lax.axis_index("req")]]
    rows = tok_ref[...].astype(F32)
    mean_square = jnp.mean(rows * rows, axis=-1, keepdims=True)
    normed = (rows * lax.rsqrt(mean_square + NORM_EPS) * gain_ref[...]).astype(BF16)
    cosine, sine = cos_ref[...], sin_ref[...]
    low = lane_index(cosine.shape) < HD
    queries, key_tiles, value_tiles = [], [], []
    for pair in range(KV // 2):
        lanes = slice(pair * LANES, (pair + 1) * LANES)
        suffix_keys = rotate_tile(dot(normed, held[1][:, lanes]), cosine, sine).astype(BF16)
        suffix_values = dot(normed, held[2][:, lanes]).astype(BF16)
        key_tiles.append([suffix_keys, keys_ref[:, lanes], mate_keys_ref[:, lanes]])
        value_tiles.append([suffix_values, values_ref[:, lanes], mate_values_ref[:, lanes]])
        projected = dot(normed, held[0][:, 2 * pair * LANES : 2 * (pair + 1) * LANES])
        for half in range(2):
            tile = rotate_tile(projected[:, half * LANES : (half + 1) * LANES], cosine, sine) * ATTN_SCALE
            turned = pltpu.roll(tile, HD, 1)
            if half == 0:
                first, second = jnp.where(low, tile, 0.0), jnp.where(low, turned, 0.0)
            else:
                first, second = jnp.where(low, 0.0, turned), jnp.where(low, 0.0, tile)
            queries.append(jnp.concatenate([first, second], axis=0).astype(BF16))
            q_ref[2 * pair + half] = queries[-1]
    results = attend_heads(queries, key_tiles, value_tiles, suffix_len, None)
    for head, (new_max, total) in enumerate(results):
        max_ref[head] = new_max
        acc_ref[head] = total


def whole_spec(*shape):
    return pl.BlockSpec(shape, lambda i: (0,) * len(shape))


def cached_specs(cached):
    specs = []
    for kind in range(2):
        for array in cached:
            stacked = not isinstance(array, tuple)
            length = array.shape[0] // 2 if stacked else array[0].shape[0]
            place = kind if stacked else 0
            specs.append(pl.BlockSpec((length, KV * HD), lambda i, place=place: (place, 0)))
    return specs


def cached_args(cached):
    return [array[kind] if isinstance(array, tuple) else array for kind in range(2) for array in cached]


def attend_near(own_rows, attn_gain, w_query, w_key, w_value, prefix_len, lengths, assignment, keys, values, mate):
    tok_count, width = own_rows.shape
    rows, block = 2 * tok_count, keys.shape[0]
    cosine, sine = rope_tables(prefix_len, tok_count)
    smem = pl.BlockSpec(memory_space=pltpu.SMEM)
    queries, *state = pl.pallas_call(
        near_kernel,
        grid=(1,),
        in_specs=[whole_spec(tok_count, width), whole_spec(1, width)]
        + [whole_spec(*array.shape) for array in (w_query, w_key, w_value)]
        + [whole_spec(tok_count, LANES)] * 2
        + [smem, smem]
        + [whole_spec(block, KV * HD)] * 4,
        out_specs=[whole_spec(KV, rows, LANES), whole_spec(KV, 1, rows), whole_spec(KV, HD + SUM_ROWS, rows)],
        out_shape=[
            pltpu.VMEM((KV, rows, LANES), BF16),
            pltpu.VMEM((KV, 1, rows), F32),
            pltpu.VMEM((KV, HD + SUM_ROWS, rows), F32),
        ],
        compiler_params=pltpu.CompilerParams(vmem_limit_bytes=VMEM_NEAR * MIB),
        cost_estimate=pl.CostEstimate(flops=4000 * MIB, bytes_accessed=6 * MIB, transcendentals=0),
        name="attend_near",
    )(
        *held_in_hbm([own_rows, attn_gain.reshape(1, width), w_query, w_key, w_value, cosine, sine]),
        *held_in_hbm([lengths, assignment, keys, values]),
        *held_in_vmem(mate),
    )
    return queries, state


def far_kernel(blocks, last, *refs):
    q_ref, max_in, acc_in = refs[:3]
    key_refs, value_refs = refs[3 : 3 + blocks], refs[3 + blocks : 3 + 2 * blocks]
    refs = refs[3 + 2 * blocks :]
    heads = q_ref.shape[0]
    states = [(max_in[head], acc_in[head]) for head in range(heads)]
    queries = [q_ref[head] for head in range(heads)]
    results = attend_heads(queries, pair_tiles(key_refs), pair_tiles(value_refs), None, states)
    if not last:
        max_ref, acc_ref = refs
        for half, (new_max, total) in enumerate(results):
            max_ref[half] = new_max
            acc_ref[half] = total
        return
    tok_ref, w_out_ref, gain_ref, ids_ref, route_ref, ctx_ref, hidden_ref, moe_ref = refs
    tok_count = tok_ref.shape[0]
    tiles = []
    for _, total in results:
        mixed = total[:HD] / total[HD : HD + 1]
        tiles.append(jnp.concatenate([mixed[:, :tok_count], mixed[:, tok_count:]], axis=0).T)
    context = jnp.concatenate(tiles, axis=1).astype(BF16)
    ctx_ref[...] = context
    projected = dot(context, w_out_ref[...])
    hidden = (tok_ref[...].astype(F32) + RESIDUAL_SCALE * projected).astype(BF16)
    hidden_ref[...] = hidden
    wide = hidden.astype(F32)
    mean_square = jnp.mean(wide * wide, axis=-1, keepdims=True)
    moe_ref[:tok_count] = (wide * lax.rsqrt(mean_square + NORM_EPS) * gain_ref[...]).astype(BF16)
    moe_ref[tok_count:] = jnp.zeros((NOTE_ROWS, wide.shape[1]), BF16)
    moe_ref[tok_count : tok_count + TOP, :tok_count] = ids_ref[...].astype(F32).astype(BF16)
    moe_ref[tok_count : tok_count + TOP, tok_count : 2 * tok_count] = route_ref[...].astype(BF16)


def attend_far(queries, state, cached, final=None):
    last, blocks, rows = final is not None, len(cached), queries.shape[1]
    tok_count = rows // 2
    args, tiles = [queries, *state], held_in_vmem(cached_args(cached))
    in_specs = [whole_spec(KV, rows, LANES), whole_spec(KV, 1, rows), whole_spec(KV, HD + SUM_ROWS, rows)]
    in_specs += cached_specs(cached)
    if last:
        own_rows, w_out, moe_gain, expert_ids, route_weights = final
        width = own_rows.shape[1]
        own_args = [own_rows, w_out, moe_gain.reshape(1, width), expert_ids.T, route_weights.T]
        whole = whole_spec(tok_count, width)
        in_specs += [whole, whole_spec(*w_out.shape), whole_spec(1, width)]
        in_specs += [whole_spec(TOP, tok_count)] * 2
        out_specs = [whole, whole, whole_spec(tok_count + NOTE_ROWS, width)]
        out_shape = [pltpu.HBM((tok_count, width), BF16)] * 2 + [pltpu.VMEM((tok_count + NOTE_ROWS, width), BF16)]
    else:
        own_args = []
        out_specs = in_specs[1:3]
        out_shape = [pltpu.VMEM(array.shape, F32) for array in state]
    return pl.pallas_call(
        functools.partial(far_kernel, blocks, last),
        grid=(1,),
        in_specs=in_specs,
        out_specs=out_specs,
        out_shape=out_shape,
        compiler_params=pltpu.CompilerParams(vmem_limit_bytes=(VMEM_LAST if last else VMEM_ATTEND) * MIB),
        cost_estimate=pl.CostEstimate(flops=blocks * 1200 * MIB, bytes_accessed=4 * MIB, transcendentals=0),
        name="attend_far",
    )(*held_in_vmem(args), *tiles, *held_in_hbm(own_args))


def experts_kernel(sources, pieces, owners, load, *refs):
    refs = list(refs)
    take = lambda n: [refs.pop(0) for _ in range(n)]
    row_refs = [take(pieces) for _ in range(sources)]
    weight_refs = [take(3) for _ in owners]
    out_refs = take(sources)
    held = [take(3) for _ in owners] if load else weight_refs
    picked_ref, made_ref, combine_ref, *sems = refs
    local_experts = held[0][0].shape[0]
    experts = len(owners) * local_experts
    tok_count, width = out_refs[0].shape
    slots = experts * CAP
    me = lax.axis_index("req")
    firsts = [(me + owner * (1 - 2 * lax.rem(me, 2))) * local_experts for owner in owners]

    def copy(group, kind, e):
        return pltpu.make_async_copy(
            weight_refs[group][kind].at[e], held[group][kind].at[e], sems[0].at[group, kind, e]
        )

    for group in range(len(owners) if load else 0):
        for e in range(local_experts):
            for kind in range(3):
                copy(group, kind, e).start()

    before = lax.broadcasted_iota(jnp.int32, (tok_count, tok_count), 0)
    after = lane_index((tok_count, tok_count))
    earlier = jnp.where(before < after, 1.0, 0.0).astype(BF16)
    slot = lax.broadcasted_iota(jnp.int32, (slots, EXPERTS), 0) // CAP
    held_here = slot + firsts[0]
    if len(owners) > 1:
        held_here = jnp.where(slot < local_experts, held_here, slot + (firsts[1] - local_experts))
    spread = jnp.where(held_here == lane_index((slots, EXPERTS)), 1.0, 0.0).astype(BF16)
    within = (lax.broadcasted_iota(jnp.int32, (slots, tok_count), 0) % CAP).astype(F32)
    expert_row = lax.broadcasted_iota(jnp.int32, (EXPERTS, tok_count), 0).astype(F32)
    for source in range(sources):
        message = jnp.concatenate([ref[...] for ref in row_refs[source]], axis=0)
        rows, note = message[:tok_count], message[tok_count:].astype(F32)
        route = jnp.zeros((EXPERTS, tok_count), F32)
        for k in range(TOP):
            chosen, gain = note[k : k + 1, :tok_count], note[k : k + 1, tok_count : 2 * tok_count]
            route = jnp.where(chosen == expert_row, gain, route)
        hit = route > 0.0
        ranked = dot(jnp.where(hit, 1.0, 0.0).astype(BF16), earlier)
        ranked = jnp.where(hit, ranked, -1.0).astype(BF16)
        match = dot(spread, ranked) == within
        pick = jnp.where(match, 1.0, 0.0).astype(BF16)
        combine_ref[source] = jnp.where(match, dot(spread, route.astype(BF16)), 0.0).astype(BF16)
        picked = dot(pick, rows).astype(BF16)
        for e in range(experts):
            picked_ref[e, source] = picked[e * CAP : (e + 1) * CAP]

    def one_expert(group, e, carry):
        for kind in range(3 if load else 0):
            copy(group, kind, e).wait()
        expert = group * local_experts + e
        rows = picked_ref[expert].reshape(sources * CAP, width)
        gate = dot(rows, held[group][0][e])
        up = dot(rows, held[group][1][e])
        act = (jax.nn.silu(gate) * up).astype(BF16)
        made = dot(act, held[group][2][e]).astype(BF16)
        for source in range(sources):
            made_ref[source, pl.ds(pl.multiple_of(expert * CAP, CAP), CAP), :] = made[
                source * CAP : (source + 1) * CAP
            ]
        return carry

    for group in range(len(owners)):
        lax.fori_loop(0, local_experts, functools.partial(one_expert, group), 0, unroll=4)
    for source, ref in enumerate(out_refs):
        ref[...] = dot_tn(combine_ref[source], made_ref[source]).astype(ref.dtype)


def run_experts(rows, weights, owners=(0, 1), load=False, out_type=BF16):
    sources, pieces = len(rows), len(rows[0])
    tok_count, width = sum(piece.shape[0] for piece in rows[0]) - NOTE_ROWS, rows[0][0].shape[1]
    vmem = pl.BlockSpec(memory_space=pltpu.VMEM)
    weight_args = [array for owned in weights for array in owned]
    local_experts = weight_args[0].shape[0]
    experts = len(owners) * local_experts
    out_shape = [pltpu.VMEM((tok_count, width), out_type)] * sources
    if load:
        out_shape = out_shape + [pltpu.VMEM(array.shape, BF16) for array in weight_args]
        weight_args, weight_specs = held_in_hbm(weight_args), [pl.BlockSpec(memory_space=pl.ANY)] * len(weight_args)
        semaphores = [pltpu.SemaphoreType.DMA((len(owners), 3, local_experts))]
    else:
        weight_args, weight_specs, semaphores = held_in_vmem(weight_args), [vmem] * len(weight_args), []
    return pl.pallas_call(
        functools.partial(experts_kernel, sources, pieces, owners, load),
        in_specs=[vmem] * (pieces * sources) + weight_specs,
        out_specs=[vmem] * len(out_shape),
        out_shape=out_shape,
        scratch_shapes=[
            pltpu.VMEM((experts, sources, CAP, width), BF16),
            pltpu.VMEM((sources, experts * CAP, width), BF16),
            pltpu.VMEM((sources, experts * CAP, tok_count), BF16),
            *semaphores,
        ],
        compiler_params=pltpu.CompilerParams(vmem_limit_bytes=VMEM_EXPERTS * MIB),
        cost_estimate=pl.CostEstimate(flops=12000 * MIB, bytes_accessed=30 * MIB, transcendentals=0),
        name="experts",
    )(*held_in_vmem([piece for source in rows for piece in source]), *weight_args)


CORE, ACROSS_X, ACROSS_Y = 1, 2, 4


def swap(array, mask):
    return lax.ppermute(array, "req", [(i, i ^ mask) for i in range(lax.axis_size("req"))])


def ordered(*arrays):
    return lax.optimization_barrier(arrays)


def local_chips(
    tokens,
    attn_gain,
    w_query,
    w_key,
    w_value,
    w_out,
    prefix_keys,
    prefix_values,
    lengths,
    assignment,
    moe_gain,
    expert_ids,
    route_weights,
    w_gate,
    w_up,
    w_down,
):
    peer_count = lax.axis_size("req")
    own_rows = tokens[0]
    tok_count = own_rows.shape[0]
    prefix_len = prefix_keys.shape[1] * peer_count
    keys, values = prefix_keys[0], prefix_values[0]
    block = keys.shape[0]
    keys_x, values_y = swap(keys, ACROSS_X), swap(values, ACROSS_Y)
    values_x, keys_y = swap(values, ACROSS_X), swap(keys, ACROSS_Y)
    cached_mate = (swap(keys, CORE), swap(values, CORE))

    queries, state = attend_near(
        own_rows, attn_gain, w_query, w_key, w_value, prefix_len, lengths, assignment, keys, values, cached_mate
    )
    keys_x, values_x, keys_y, values_y, *state = ordered(keys_x, values_x, keys_y, values_y, *state)
    far = [swap(keys_x, ACROSS_Y), swap(values_y, ACROSS_X)]
    mates = [swap(array, CORE) for array in (keys_x, values_x, keys_y, values_y)]
    *mates, w_gate = ordered(*mates, w_gate)
    gate = (w_gate, swap(w_gate, CORE))
    near = [(keys_x, values_x), (keys_y, values_y), tuple(mates[:2]), tuple(mates[2:])]
    state = attend_far(queries, state, near)
    *far, gate, s0, s1 = ordered(*far, gate, *state)
    far_mate = [swap(array, CORE) for array in far]
    *far_mate, w_up, w_down = ordered(*far_mate, w_up, w_down)
    up, down = (w_up, swap(w_up, CORE)), (w_down, swap(w_down, CORE))
    context, hidden, moe_in = attend_far(
        queries,
        [s0, s1],
        [tuple(far), tuple(far_mate)],
        final=(own_rows, w_out, moe_gain, expert_ids[0], route_weights[0]),
    )

    owned, mated = zip(gate, up, down)
    half = tok_count // 2
    rows_x, rows_y = swap(moe_in, ACROSS_X), swap(moe_in, ACROSS_Y)
    weights = [list(owned), list(mated)]
    (own,) = run_experts([[moe_in]], weights, out_type=F32)
    rows_y, own = ordered(rows_y, own)
    high_xy = swap(rows_y[half:], ACROSS_X)
    rows_x, rows_y, own = ordered(rows_x, rows_y, own)
    low_xy = swap(rows_x[:half], ACROSS_Y)
    to_x, to_y = run_experts([[rows_x], [rows_y]], weights)
    low_xy, high_xy, to_x, to_y = ordered(low_xy, high_xy, to_x, to_y)
    from_x, from_y = swap(to_x, ACROSS_X), swap(to_y, ACROSS_Y)
    (to_xy,) = run_experts([[low_xy, high_xy]], weights)
    from_xy = swap(to_xy, ACROSS_X | ACROSS_Y)
    partial, from_xy = ordered(own + from_x.astype(F32) + from_y.astype(F32), from_xy)
    expert_mix = (partial + from_xy.astype(F32)).astype(BF16)
    return (context[None], hidden[None], expert_mix[None])


def solution(mesh):
    placed = (
        P("grp", "req", None),
        P(),
        P(),
        P(),
        P(),
        P(),
        P("grp", "req", None),
        P("grp", "req", None),
        P("grp", None),
        P("grp", None),
        P(),
        P("grp", "req", None),
        P("grp", "req", None),
        P("req", None, None),
        P("req", None, None),
        P("req", None, None),
    )
    return jax.shard_map(
        local_chips if mesh.shape["req"] == 8 else local_general,
        mesh=mesh,
        in_specs=placed,
        out_specs=(P("grp", "req", None), P("grp", "req", None), P("grp", "req", None)),
        check_vma=False,
    )
```
